32 devices in a mesh: gx: 4 (over z), gy: 2 (over y), gz: 4 (over x, core).
Axes of the slice: x: 2, y: 2, z: 4, core: 2. Of those that a mesh axis runs over, the one named last changes fastest.
Arguments:
- right_side: float32 [3, 16, 16, 512], P(None, 'gz', 'gy', 'gx'), may hold values from -5 to 5
- stiff_scale: float32 [16, 16, 512], P('gz', 'gy', 'gx'), may hold values from 0.5 to 2
- nodal_mass: float32 [16, 16, 512], P('gz', 'gy', 'gx'), may hold values from 0.01 to 0.1
- stencil_blocks: float32 [27, 3, 3], replicated, may hold values from -0.5 to 6, as said below
Outputs:
- correction: float32 [3, 16, 16, 512], P(None, 'gz', 'gy', 'gx')
The draws below stay inside these ranges and needn't reach their ends.
Inputs may be any that keep to these rules, and one draw needn't show every extreme that they name: `stencil_blocks`: every block is symmetric and the block of the opposite offset equals it; the centre block is S plus 0.01 times the diagonal of S, where S is minus the sum of the other 26 blocks.
All inputs are finite; a program needn't handle non-finite values.
Results may differ from the reference program's by a relative error of at most 0.0003.
Values sent between devices are 32-bit elements; how exact they have to be, the bound alone decides.
No kernel may reach another device: no remote copies, remote signals or barrier semaphores. Data moves between devices by JAX's collectives and lax.ppermute only.
A program may use at most 128 MiB of HBM per device.

```python
import math
import jax
import jax.numpy as jnp
import numpy as np
from jax import lax

SMOOTH_DEGREE = 2
COARSE_ITERS = 8
NX = 512
NY = 16
NZ = 16


def draw_right_side(key, part):
    key = jax.random.fold_in(key, 11)
    grid_z = (jnp.arange(NZ, dtype=jnp.float32)[:, None, None] + 0.5) / NZ
    grid_y = (jnp.arange(NY, dtype=jnp.float32)[None, :, None] + 0.5) / NY
    grid_x = (jnp.arange(NX, dtype=jnp.float32)[None, None, :] + 0.5) / NX
    smooth = jnp.sin(math.pi * grid_x) * jnp.sin(math.pi * grid_y) * (0.6 + 0.4 * jnp.sin(math.pi * grid_z))
    weights = jnp.array([1.0, -0.6, 0.8], dtype=jnp.float32)[:, None, None, None]
    shape_all = (3, NZ, NY, NX)
    noise = jax.random.truncated_normal(key, -4.0, 4.0, shape_all, jnp.float32)
    return noise + 0.5 * weights * smooth[None]


def draw_stencil_blocks(key, part):
    key = jax.random.fold_in(key, 23)
    key_diag, key_off = jax.random.split(key)
    reach = np.array([abs(step_z) + abs(step_y) + abs(step_x) for step_z in (-1, 0, 1) for step_y in (-1, 0, 1) for step_x in (-1, 0, 1)][:13], dtype=np.float32)
    weight = jnp.asarray(0.5 ** (reach - 1.0), dtype=jnp.float32)[:, None]
    diag_raw = 0.15 * jnp.exp(0.5 * jax.random.truncated_normal(key_diag, -2.0, 2.0, (13, 3), jnp.float32))
    off_raw = 0.2 * jax.random.truncated_normal(key_off, -2.2, 2.2, (13, 3), jnp.float32)
    diag_vals = diag_raw * weight
    first = diag_vals[:, 0]
    second = diag_vals[:, 1]
    third = diag_vals[:, 2]
    off_ab = off_raw[:, 0] * jnp.minimum(first, second)
    off_ac = off_raw[:, 1] * jnp.minimum(first, third)
    off_bc = off_raw[:, 2] * jnp.minimum(second, third)
    row_a = jnp.stack([first, off_ab, off_ac], -1)
    row_b = jnp.stack([off_ab, second, off_bc], -1)
    row_c = jnp.stack([off_ac, off_bc, third], -1)
    positive = jnp.stack([row_a, row_b, row_c], 1)
    half_blocks = -positive
    total = 2.0 * jnp.sum(positive, axis=0)
    centre = total + 0.01 * jnp.diag(jnp.diagonal(total))
    return jnp.concatenate([half_blocks, centre[None], half_blocks[::-1]], axis=0)


def block_levels(key, dims, pieces, low, high):
    loudness = 1.0
    for position, parts in pieces:
        steps = jax.random.uniform(jax.random.fold_in(jax.random.fold_in(key, 6), position), (parts,), jnp.float32, low / len(pieces), high / len(pieces))
        loudness = loudness * jnp.repeat(jnp.exp(steps), dims[position] // parts).reshape((-1,) + (1,) * (len(dims) - 1 - position))
    return loudness


def setup_inputs(seed: int = 0) -> dict:
    arg_keys = jax.random.split(jax.random.key(seed), 5)
    right_side = draw_right_side(jax.random.fold_in(arg_keys[4], 71), 0)
    stiff_scale = jnp.clip(jnp.exp(math.log(2.0) - 1.3862944 * jax.random.uniform(arg_keys[1], (NZ, NY, NX), jnp.float32) ** block_levels(arg_keys[1], (NZ, NY, NX), ((0, 4), (1, 2), (2, 4)), -0.2, 0.2)), 0.5, 2.0)
    nodal_mass = jnp.clip(jnp.exp(math.log(0.1) - 2.3025851 * jax.random.uniform(arg_keys[2], (NZ, NY, NX), jnp.float32) ** block_levels(arg_keys[2], (NZ, NY, NX), ((0, 4), (1, 2), (2, 4)), -0.2, 0.2)), 0.01, 0.1)
    stencil_blocks = draw_stencil_blocks(jax.random.fold_in(arg_keys[4], 71), 0)
    return {"right_side": right_side, "stiff_scale": stiff_scale, "nodal_mass": nodal_mass, "stencil_blocks": stencil_blocks}


smooth_ratio = 20.0
coarse_ratio = 200.0


def offset_list():
    return [(step_z, step_y, step_x) for step_z in (-1, 0, 1) for step_y in (-1, 0, 1) for step_x in (-1, 0, 1)]


def stencil(padded, kernel):
    extent_z = padded.shape[1] - 2
    extent_y = padded.shape[2] - 2
    extent_x = padded.shape[3] - 2
    summed = None
    for offset_id, (step_z, step_y, step_x) in enumerate(offset_list()):
        portion = padded[:, 1 + step_z:1 + step_z + extent_z, 1 + step_y:1 + step_y + extent_y, 1 + step_x:1 + step_x + extent_x]
        addend = jnp.einsum("ab,bzyx->azyx", kernel[offset_id], portion, precision=lax.Precision.HIGHEST)
        summed = addend if summed is None else summed + addend
    return summed


def make_operator(scale, mass, kernel, padder):
    def operate(values):
        weighted = scale[None] * values
        return scale[None] * stencil(padder(weighted), kernel) + mass[None] * values
    return operate


def diagonal_of(scale, mass, kernel):
    centre = jnp.diagonal(kernel[13])
    return centre[:, None, None, None] * (scale * scale)[None] + mass[None]


def ratio_max(scale, mass, kernel, padder):
    spread_scale = jnp.broadcast_to(scale[None], (3,) + scale.shape)
    row_sum = scale[None] * stencil(padder(spread_scale), jnp.abs(kernel)) + mass[None]
    return jnp.max(row_sum / diagonal_of(scale, mass, kernel))


def coarsen(values):
    extent = values.shape
    return values.reshape(extent[0], extent[1] // 2, 2, extent[2] // 2, 2, extent[3] // 2, 2).sum(axis=(2, 4, 6))


def refine(values):
    return jnp.repeat(jnp.repeat(jnp.repeat(values, 2, axis=1), 2, axis=2), 2, axis=3)


def chebyshev(iterate, residue, degree, inverse_diag, upper_end, range_ratio, operate, keep_residue):
    lower_end = upper_end / range_ratio
    centre = 0.5 * (upper_end + lower_end)
    spread = 0.5 * (upper_end - lower_end)
    sigma_val = centre / spread
    rho_now = 1.0 / sigma_val
    direction = inverse_diag * residue / centre
    for sweep_id in range(degree):
        iterate = iterate + direction
        if sweep_id < degree - 1 or keep_residue:
            residue = residue - operate(direction)
        if sweep_id < degree - 1:
            rho_next = 1.0 / (2.0 * sigma_val - rho_now)
            direction = rho_next * rho_now * direction + (2.0 * rho_next / spread) * inverse_diag * residue
            rho_now = rho_next
    return iterate, residue


def cycle(tier_id, source, operators, inverses, bounds, coarse_solve):
    if tier_id == 2:
        return coarse_solve(source)
    operate = operators[tier_id]
    inverse_diag = inverses[tier_id]
    start_zero = jnp.zeros_like(source)
    iterate, residue = chebyshev(start_zero, source, SMOOTH_DEGREE, inverse_diag, bounds[tier_id], smooth_ratio, operate, True)
    omega_val = (4.0 / 3.0) / bounds[tier_id]
    smoothed = residue - omega_val * operate(inverse_diag * residue)
    coarse = cycle(tier_id + 1, coarsen(smoothed), operators, inverses, bounds, coarse_solve)
    lifted = refine(coarse)
    iterate = iterate + lifted - omega_val * inverse_diag * operate(lifted)
    residue = source - operate(iterate)
    iterate, residue = chebyshev(iterate, residue, SMOOTH_DEGREE, inverse_diag, bounds[tier_id], smooth_ratio, operate, False)
    return iterate


def pad_zero(values):
    return jnp.pad(values, ((0, 0), (1, 1), (1, 1), (1, 1)))


def reference(right_side, stiff_scale, nodal_mass, stencil_blocks):
    scales = [stiff_scale]
    masses = [nodal_mass]
    for tier_id in range(2):
        scales.append(coarsen(scales[-1][None])[0] / 8.0)
        masses.append(coarsen(masses[-1][None])[0])
    kernels = [stencil_blocks, 2.0 * stencil_blocks, 4.0 * stencil_blocks]
    operators = [make_operator(scales[tier_id], masses[tier_id], kernels[tier_id], pad_zero) for tier_id in range(3)]
    inverses = [1.0 / diagonal_of(scales[tier_id], masses[tier_id], kernels[tier_id]) for tier_id in range(3)]
    bounds = [ratio_max(scales[tier_id], masses[tier_id], kernels[tier_id], pad_zero) for tier_id in range(3)]

    def coarse_solve(source):
        iterate, residue = chebyshev(jnp.zeros_like(source), source, COARSE_ITERS, inverses[2], bounds[2], coarse_ratio, operators[2], False)
        return iterate

    return cycle(0, right_side, operators, inverses, bounds, coarse_solve)
```

```python
import functools

import jax
import jax.numpy as jnp
from jax import lax
from jax.experimental import pallas as pl
from jax.experimental.pallas import tpu as pltpu
from jax.sharding import PartitionSpec as P

AXES = ("gx", "gy", "gz")
COARSE_ITERS = 8
SMOOTH_RATIO = 20.0
COARSE_RATIO = 200.0
F32, BF16 = jnp.float32, jnp.bfloat16
PARAMS = pltpu.CompilerParams(vmem_limit_bytes=40 * 1024 * 1024)
VM = pl.BlockSpec(memory_space=pltpu.VMEM)
SM = pl.BlockSpec(memory_space=pltpu.SMEM)
ROWS, LANES = 16, 256
SLAB = 3 * ROWS
GROUP = 3


def call(kernel, outs, specs=None, scratch=(), flops=1000000, size=100000):
    outs = [jax.ShapeDtypeStruct(shape, dtype) for shape, dtype in outs]

    def run(*args):
        return pl.pallas_call(
            kernel,
            out_shape=outs,
            in_specs=specs or [VM] * len(args),
            out_specs=[VM] * len(outs),
            scratch_shapes=scratch,
            compiler_params=PARAMS,
            cost_estimate=pl.CostEstimate(flops=flops, bytes_accessed=size, transcendentals=0),
        )(*args)

    return run


def iota(shape, dim):
    return lax.broadcasted_iota(jnp.int32, shape, dim)


def ones_where(mask):
    return jnp.where(mask, 1.0, 0.0).astype(F32)


def split(values):
    high = values.astype(BF16)
    return high, (values - high.astype(F32)).astype(BF16)


def dot(left, right):
    return jnp.dot(left, right, preferred_element_type=F32)


def dot_select(left, right):
    return jnp.dot(left, right, preferred_element_type=F32, precision=lax.Precision.HIGHEST)


def banded(matrix_high, matrix_low, values):
    high, low = split(values)
    return dot(matrix_high, high) + dot(matrix_low, high) + dot(matrix_high, low)


def shifted_sum(product, slabs, rows, lanes):
    parts = product.reshape(slabs, 3, rows, lanes)
    below = parts[:, 0].reshape(slabs * rows, lanes)
    above = parts[:, 2].reshape(slabs * rows, lanes)
    here = parts[:, 1].reshape(slabs * rows, lanes)
    return here + pltpu.roll(below, 1, 1) + pltpu.roll(above, lanes - 1, 1)


def fine_stencil(matrix, values):
    planes = values.shape[0] - 2
    flat = values.reshape((planes + 2) * SLAB, LANES)
    outs = []
    at = 0
    while at < planes:
        size = min(GROUP, planes - at)
        if planes - at == 4:
            size = 2
        height, depth = size * 3 * SLAB, (size + 2) * SLAB
        product = banded(
            matrix[0, :height, :depth],
            matrix[1, :height, :depth],
            flat[at * SLAB : at * SLAB + depth],
        )
        outs.append(shifted_sum(product, size, SLAB, LANES))
        at += size
    return jnp.concatenate(outs, axis=0).reshape(planes, 3, ROWS, LANES)


def panels(blocks, rows, circular, width):
    column = iota((8, width), 1)
    which = column // rows
    row_in = column % rows
    result = {}
    for step_x in range(3):
        for comp in range(3):
            coeffs = []
            for step_y in range(3):
                coeff = jnp.zeros((8, width), F32)
                for plane in range(3):
                    for other in range(3):
                        value = blocks[(plane * 9 + step_y * 3 + step_x) * 9 + comp * 3 + other]
                        coeff = jnp.where(which == plane * 3 + other, value, coeff)
                coeffs.append(coeff)
            pieces = []
            for block in range(rows // 8):
                gap = row_in - (iota((8, width), 0) + block * 8)
                if circular:
                    gap = jnp.where(gap == rows - 1, -1, jnp.where(gap == 1 - rows, 1, gap))
                piece = jnp.zeros((8, width), F32)
                for step_y in range(3):
                    piece = jnp.where(gap == step_y - 1, coeffs[step_y], piece)
                pieces.append(piece)
            result[step_x, comp] = jnp.concatenate(pieces, axis=0)
    return result


def put(ref, start, value):
    high, low = split(value)
    size = value.shape[0]
    ref[0, start : start + size, :] = high
    ref[1, start : start + size, :] = low


def matrices_kernel(mid_rows, mid_planes, blocks, fine, fine_abs, mid, local_abs):
    found = panels(blocks, ROWS, True, LANES)
    for plane in range(GROUP):
        for step_x in range(3):
            rows = [
                found[step_x, comp] if plane == 0 else pltpu.roll(found[step_x, comp], plane * SLAB, 1)
                for comp in range(3)
            ]
            value = jnp.concatenate(rows, axis=0)
            start = (plane * 3 + step_x) * SLAB
            put(fine, start, value)
            put(fine_abs, start, jnp.abs(value))
    found = panels(blocks, 8, True, 128)
    for plane in range(2):
        for step_x in range(3):
            rows = [
                found[step_x, comp] if plane == 0 else pltpu.roll(found[step_x, comp], plane * 24, 1)
                for comp in range(3)
            ]
            put(local_abs, (plane * 3 + step_x) * 24, jnp.abs(jnp.concatenate(rows, axis=0)))
    slab = 3 * mid_rows
    width = mid.shape[2]
    found = panels(blocks, mid_rows, False, width)
    column = iota((slab, width), 1)
    for plane in range(mid_planes):
        for step_x in range(3):
            value = jnp.concatenate([found[step_x, comp] for comp in range(3)], axis=0)
            if plane == 0:
                value = jnp.where(column < slab, 0.0, value)
            if plane == mid_planes - 1:
                value = jnp.where(column >= 2 * slab, 0.0, value)
            turn = ((plane - 1) * slab) % width
            if turn:
                value = pltpu.roll(value, turn, 1)
            put(mid, (plane * 3 + step_x) * slab, value)


def even_index(axis):
    return lax.rem(lax.axis_index(axis), 2) == 0


def halves(planes, axis, size, low):
    first, second = planes[:10], pltpu.roll(planes[10:], size // 2, axis)
    return jnp.where(low, second, first), jnp.where(low, first, second)


def unhalve(from_above, from_below, axis, size, low):
    first = jnp.where(low, from_above, from_below)
    second = jnp.where(low, pltpu.roll(from_above, size // 2, axis), pltpu.roll(from_below, size // 2, axis))
    return jnp.concatenate([first, second], axis=0)


def neighbours(even, index, count, first, second):
    above = jnp.where(even, first, second)
    below = jnp.where(even, second, first)
    return jnp.where(index < count - 1, above, 0.0), jnp.where(index > 0, below, 0.0)


def pack_x_kernel(source, scale, mass, main, send_a, send_b):
    planes = jnp.concatenate([source[...].reshape(12, 8, 128), scale[...], mass[...]], axis=0)
    main[...] = planes
    high, low = halves(planes, 2, 128, iota((10, 8, 128), 2) < 64)
    even = even_index("gx")
    send_a[...] = jnp.where(even, high, low)
    send_b[...] = jnp.where(even, low, high)


def pack_y_kernel(count, main, got_a, got_b, wide, *sends):
    even = even_index("gx")
    above, below = neighbours(even, lax.axis_index("gx"), count, got_a[...], got_b[...])
    halo = unhalve(above, below, 2, 128, iota((10, 8, 128), 2) < 64)
    wide[:, :, :128] = main[...]
    wide[:, :, 128:] = halo
    planes = wide[...]
    high, low = halves(planes, 1, 8, iota((10, 8, LANES), 1) < 4)
    even = even_index("gy")
    sends[0][...] = jnp.where(even, high, low)
    if len(sends) > 1:
        sends[1][...] = jnp.where(even, low, high)


def pack_z_kernel(count, wide, *refs):
    *gots, whole, send_a, send_b = refs
    even = even_index("gy")
    above, below = neighbours(even, lax.axis_index("gy"), count, gots[0][...], gots[-1][...])
    halo = unhalve(above, below, 1, 8, iota((10, 8, LANES), 1) < 4)
    whole[:, :8, :] = wide[...]
    whole[:, 8:, :] = halo
    planes = whole[...]
    even = even_index("gz")
    for send, up in ((send_a, even), (send_b, jnp.logical_not(even))):
        for slot, field in enumerate((0, 1, 2, 4)):
            send[slot * 3 : slot * 3 + 3] = jnp.where(
                up, planes[field * 4 + 1 : field * 4 + 4], planes[field * 4 : field * 4 + 3]
            )
        send[12:16] = planes[12:16]


def restrict_lanes(width):
    return ones_where(iota((width, 128), 0) // 2 == iota((width, 128), 1))


def inverse_diagonal(scale, mass, blocks, factor):
    square = scale * scale
    parts = []
    for comp in range(3):
        diag = factor * blocks[13 * 9 + comp * 4] * square + mass
        parts.append(jnp.where(scale > 0.0, 1.0 / diag, 0.0)[:, None])
    return jnp.concatenate(parts, axis=1)


def worst_ratio(scale, mass, total, blocks, factor, rows, lanes):
    inverse = inverse_diagonal(scale, mass, blocks, factor)
    ratio = (factor * scale[:, None] * total + mass[:, None]) * inverse
    shape = ratio.shape
    own = jnp.logical_and(iota(shape, 2) < rows, iota(shape, 3) < lanes)
    return jnp.full((8, 128), jnp.max(jnp.where(own, ratio, -jnp.inf)), F32)


def window_kernel(count, blocks, whole, got_a, got_b, fine_abs, local_abs, scale_w, mass_w, source_w, bounds):
    even = even_index("gz")
    above, below = neighbours(even, lax.axis_index("gz"), count, got_a[...], got_b[...])
    planes = whole[...]
    for comp in range(3):
        source_w[0:3, comp] = below[comp * 3 : comp * 3 + 3]
        source_w[3:7, comp] = planes[comp * 4 : comp * 4 + 4]
        source_w[7:10, comp] = above[comp * 3 : comp * 3 + 3]
    mass_w[0:3] = below[9:12]
    mass_w[3:7] = planes[16:20]
    mass_w[7:10] = above[9:12]
    scale_w[0:4] = below[12:16]
    scale_w[4:8] = planes[12:16]
    scale_w[8:12] = above[12:16]

    scale = scale_w[...]
    mass = mass_w[3:7]
    spread = jnp.broadcast_to(scale[3:9][:, None], (6, 3, ROWS, LANES))
    total = fine_stencil(fine_abs, spread)
    bounds[0] = worst_ratio(scale[4:8], mass, total, blocks, 1.0, 8, 128)

    paired = jnp.concatenate(
        [scale.reshape(6, 2, ROWS, LANES).sum(axis=1), mass.reshape(2, 2, ROWS, LANES).sum(axis=1)], axis=0
    )
    squeezed = dot_select(paired.reshape(8 * ROWS, LANES), restrict_lanes(LANES))
    middle = dot_select(ones_where(iota((64, 128), 0) == iota((64, 128), 1) // 2), squeezed).reshape(8, 8, 128)
    scale_1 = middle[:6] * 0.125
    mass_1 = middle[6:]
    spread = jnp.broadcast_to(scale_1[1:5][:, None], (4, 3, 8, 128)).reshape(96, 128)
    product = banded(local_abs[0, :, :96], local_abs[1, :, :96], spread)
    total = shifted_sum(product, 2, 24, 128).reshape(2, 3, 8, 128)
    bounds[1] = worst_ratio(scale_1[2:4], mass_1, total, blocks, 2.0, 4, 64)

    paired = jnp.concatenate([scale_1.reshape(3, 2, 8, 128).sum(axis=1), mass_1.sum(axis=0)[None]], axis=0)
    fold = ones_where(iota((128, 128), 0) // 2 == iota((128, 128), 1) % 64)
    squeezed = dot_select(paired.reshape(32, 128), fold)
    out_row, in_row = iota((32, 32), 0), iota((32, 32), 1)
    same = jnp.logical_and(out_row // 8 == in_row // 8, out_row % 4 == (in_row % 8) // 2)
    coarse = dot_select(ones_where(same), squeezed).reshape(4, 8, 128)
    scale_2 = coarse[:3] * 0.125
    mass_2 = coarse[3:]
    spread = jnp.broadcast_to(scale_2[:, None], (3, 3, 8, 128)).reshape(72, 128)
    product = banded(local_abs[0, :72, :72], local_abs[1, :72, :72], spread)
    total = shifted_sum(product, 1, 24, 128).reshape(1, 3, 8, 128)
    bounds[2] = worst_ratio(scale_2[1:2], mass_2, total, blocks, 4.0, 2, 32)


def fine_operator(matrix, scale, mass, values):
    total = fine_stencil(matrix, scale[:, None] * values)
    return scale[1:-1][:, None] * total + mass[:, None] * values[1:-1]


def power_kernel(blocks, scale_w, mass_w, source_w, fine, power_1):
    scale, mass = scale_w[1:11], mass_w[...]
    inverse = inverse_diagonal(scale, mass, blocks, 1.0)
    power_1[...] = fine_operator(fine, scale, mass[1:9], inverse * source_w[...])


def restrict_kernel(blocks, scale_w, mass_w, source_w, power_1, fine, bounds, *refs):
    *others, power_2, message = refs
    scale, mass = scale_w[2:10], mass_w[1:9]
    inverse = inverse_diagonal(scale, mass, blocks, 1.0)
    second = fine_operator(fine, scale, mass[1:7], inverse * power_1[...])
    power_2[...] = second
    third = fine_operator(fine, scale[1:7], mass[2:6], inverse[1:7] * second)
    fields = []
    for values in (source_w[3:7], power_1[2:6], second[1:5], third):
        pairs = values[:, :, :8].reshape(2, 2, 3, 8, LANES).sum(axis=1)
        fields += [pairs[:, comp] for comp in range(3)]
    for values in (scale[2:6], mass[2:6]):
        fields.append(values[:, :8].reshape(2, 2, 8, LANES).sum(axis=1))
    stacked = jnp.concatenate(fields, axis=0).reshape(224, LANES)
    squeezed = dot_select(stacked, restrict_lanes(LANES))
    pair = ones_where(iota((112, 224), 0) == iota((112, 224), 1) // 2)
    message[0:14] = dot_select(pair, squeezed).reshape(14, 8, 128)
    worst = bounds[...]
    for other in others:
        worst = jnp.maximum(worst, other[...])
    message[14:17] = worst


def chebyshev_scalars(bound, ratio):
    lower = bound / ratio
    return 0.5 * (bound + lower), 0.5 * (bound - lower)


def scaled(coeff, values):
    lanes = values.shape[-1]
    if lanes != 128:
        coeff = jnp.concatenate([coeff] * (lanes // 128), axis=1)
    flat = values.reshape(-1, 8, lanes)
    return (coeff[None] * flat).reshape(values.shape)


def chebyshev(residue, degree, inverse, bound, ratio, operate, keep):
    centre, spread = chebyshev_scalars(bound, ratio)
    sigma = centre / spread
    rho = 1.0 / sigma
    direction = scaled(1.0 / centre, inverse * residue)
    total = direction
    for step in range(degree):
        if step < degree - 1 or keep:
            residue = residue - operate(direction)
        if step < degree - 1:
            rho_next = 1.0 / (2.0 * sigma - rho)
            direction = scaled(rho_next * rho, direction) + scaled(2.0 * rho_next / spread, inverse * residue)
            total = total + direction
            rho = rho_next
    return total, residue


def final_kernel(
    gzs, gys, ordered, blocks, gathered, scale_w, mass_w, source_w, power_1, power_2, fine, mid, result, held, middle, lifted_w
):
    planes, rows = 2 * gzs, 4 * gys
    slab = 3 * rows
    gz, gy = lax.axis_index("gz"), lax.axis_index("gy")
    bounds = jnp.max(gathered[:, 14:17], axis=0)

    centre, spread = chebyshev_scalars(bounds[0], SMOOTH_RATIO)
    sigma = centre / spread
    rho = 1.0 / sigma
    rho_next = 1.0 / (2.0 * sigma - rho)
    keep, push = rho_next * rho, 2.0 * rho_next / spread
    beta = push / centre
    gamma = 1.0 / centre + keep / centre + push
    omega = (4.0 / 3.0) / bounds[0]

    for block in range(gzs * gys):
        part = gathered[block]
        source = (
            part[0:3]
            - (gamma + omega)[None] * part[3:6]
            + (beta + omega * gamma)[None] * part[6:9]
            - (omega * beta)[None] * part[9:12]
        )
        if ordered:
            place_z, place_y = block // gys, block % gys
        else:
            place_z = lax.bitwise_xor(gz, (block // 4) + 2 * (block % 2))
            place_y = lax.bitwise_xor(gy, (block % 4) // 2)
        held[place_z, place_y, 0:3] = source
        held[place_z, place_y, 3] = part[12] * 0.125
        held[place_z, place_y, 4] = part[13]
    first = iota((5, 8, 128), 1) < 4
    for place_z in range(gzs):
        for pair in range(gys // 2):
            low, high = held[place_z, 2 * pair], held[place_z, 2 * pair + 1]
            middle[2 * place_z, :, pair * 8 : pair * 8 + 8] = jnp.where(first, low, pltpu.roll(high, 4, 1))
            middle[2 * place_z + 1, :, pair * 8 : pair * 8 + 8] = jnp.where(first, pltpu.roll(low, 4, 1), high)

    everything = middle[...]
    source_1 = everything[:, :3].reshape(planes * slab, 128)
    scale_1 = everything[:, 3]
    mass_1 = everything[:, 4]
    inverse_1 = inverse_diagonal(scale_1, mass_1, blocks, 2.0).reshape(planes * slab, 128)
    spread_1 = jnp.broadcast_to(scale_1[:, None], (planes, 3, rows, 128)).reshape(planes * slab, 128)
    weight_1 = jnp.broadcast_to(mass_1[:, None], (planes, 3, rows, 128)).reshape(planes * slab, 128)

    def operate_1(values):
        product = banded(mid[0, :, : planes * slab], mid[1, :, : planes * slab], spread_1 * values)
        return 2.0 * spread_1 * shifted_sum(product, planes, slab, 128) + weight_1 * values

    half = planes // 2
    small = half * slab
    out_row, in_row = iota((small, planes * slab), 0), iota((small, planes * slab), 1)
    gather_rows = ones_where(
        jnp.logical_and(
            jnp.logical_and(out_row // slab == in_row // (2 * slab), (out_row % slab) // rows == (in_row % slab) // rows),
            out_row % rows == (in_row % rows) // 2,
        )
    )
    fold = ones_where(iota((128, 128), 0) // 2 == iota((128, 128), 1) % 64)
    column, lane = iota((128, 128), 0), iota((128, 128), 1)
    unfold = ones_where(column == lane // 2)

    def coarsen(values):
        return dot_select(dot_select(gather_rows, values), fold)

    scale_2 = coarsen(spread_1) * 0.125
    mass_2 = coarsen(weight_1)
    inverse_2 = inverse_diagonal(
        scale_2.reshape(half, 3, rows, 128)[:, 0], mass_2.reshape(half, 3, rows, 128)[:, 0], blocks, 4.0
    ).reshape(small, 128)

    def operate_2(values):
        product = banded(mid[0, : small * 3, :small], mid[1, : small * 3, :small], scale_2 * values)
        return 4.0 * scale_2 * shifted_sum(product, half, slab, 128) + mass_2 * values

    omega_1 = (4.0 / 3.0) / bounds[1]
    iterate, residue = chebyshev(source_1, 2, inverse_1, bounds[1], SMOOTH_RATIO, operate_1, True)
    smoothed = residue - scaled(omega_1, operate_1(inverse_1 * residue))
    source_2 = coarsen(smoothed)
    error_2, _ = chebyshev(source_2, COARSE_ITERS, inverse_2, bounds[2], COARSE_RATIO, operate_2, False)
    spread_rows = ones_where(
        jnp.logical_and(
            jnp.logical_and(
                iota((planes * slab, small), 1) // slab == iota((planes * slab, small), 0) // (2 * slab),
                (iota((planes * slab, small), 1) % slab) // rows == (iota((planes * slab, small), 0) % slab) // rows,
            ),
            iota((planes * slab, small), 1) % rows == (iota((planes * slab, small), 0) % rows) // 2,
        )
    )
    lifted = dot_select(dot_select(spread_rows, error_2), unfold)
    iterate = iterate + lifted - scaled(omega_1, inverse_1 * operate_1(lifted))
    residue = source_1 - operate_1(iterate)
    more, _ = chebyshev(residue, 2, inverse_1, bounds[1], SMOOTH_RATIO, operate_1, False)
    error_1 = iterate + more

    lifted_w[0:2] = jnp.zeros((2, slab, 128), F32)
    lifted_w[planes + 2 : planes + 4] = jnp.zeros((2, slab, 128), F32)
    lifted_w[2 : planes + 2] = error_1.reshape(planes, slab, 128)
    near = lifted_w[pl.ds(2 * gz, 6)]
    out_row, in_row = iota((SLAB, slab), 0), iota((SLAB, slab), 1)
    place = out_row % ROWS
    wanted = 4 * gy + place // 2 - jnp.where(place < 12, 0, 8)
    expand = ones_where(jnp.logical_and(out_row // ROWS == in_row // rows, in_row % rows == wanted))
    side = jnp.concatenate([near[plane] for plane in range(6)], axis=1)
    tall = dot_select(expand, side)
    tall = jnp.concatenate([tall[:, plane * 128 : plane * 128 + 128] for plane in range(6)], axis=0)
    stretch = ones_where(iota((128, LANES), 0) == iota((128, LANES), 1) // 2)
    sparse = dot_select(tall, stretch).reshape(6, 3, ROWS, LANES)
    error = jnp.stack([sparse[(plane + 1) // 2] for plane in range(10)], axis=0)

    scale, mass = scale_w[1:11], mass_w[...]
    inverse = inverse_diagonal(scale[1:9], mass[1:9], blocks, 1.0)
    image = fine_operator(fine, scale, mass[1:9], error)
    source = source_w[1:9]
    iterate = inverse * (scaled(gamma, source) - scaled(beta, power_1[...]) - scaled(omega, image)) + error[1:9]
    residue = source[1:7] - fine_operator(fine, scale[1:9], mass[2:8], iterate)
    direction = scaled(1.0 / centre, inverse[1:7] * residue)
    last = residue[1:5] - fine_operator(fine, scale[2:8], mass[3:7], direction)
    answer = iterate[2:6] + scaled(1.0 + keep, direction[1:5]) + scaled(push, inverse[2:6] * last)
    for comp in range(3):
        result[comp] = answer[:, comp, :8, :128]


def devices(counts):
    return [(x, y, z) for x in range(counts[0]) for y in range(counts[1]) for z in range(counts[2])]


def pairs(counts, target):
    def number(place):
        return (place[0] * counts[1] + place[1]) * counts[2] + place[2]

    return [(number(place), number(target(*place))) for place in devices(counts)]


def odd_partner(index):
    return index - 1 if index % 2 == 0 else index + 1


def on_device(right_side, stiff_scale, nodal_mass, stencil_blocks):
    counts = tuple(lax.axis_size(axis) for axis in AXES)
    gxs, gys, gzs = counts
    blocks = stencil_blocks.reshape(243)

    def send(values, target):
        return lax.ppermute(values, AXES, pairs(counts, target))

    def x_second(x, y, z):
        return (x, y, z ^ 1) if x in (0, gxs - 1) else (odd_partner(x), y, z)

    def z_second(x, y, z):
        return (x, y ^ 1, z) if z in (0, gzs - 1) else (x, y, odd_partner(z))

    planes, rows = 2 * gzs, 4 * gys
    width = -(-planes * 3 * rows // 128) * 128
    fine, fine_abs, mid, local_abs = call(
        functools.partial(matrices_kernel, rows, planes),
        [
            ((2, GROUP * 3 * SLAB, LANES), BF16),
            ((2, GROUP * 3 * SLAB, LANES), BF16),
            ((2, planes * 9 * rows, width), BF16),
            ((2, 144, 128), BF16),
        ],
        specs=[SM],
    )(blocks)

    half = ((10, 8, 128), F32)
    main, send_a, send_b = call(pack_x_kernel, [((20, 8, 128), F32), half, half])(right_side, stiff_scale, nodal_mass)
    got_a = send(send_a, lambda x, y, z: (x ^ 1, y, z))
    got_b = send(send_b, x_second)
    half = ((10, 8, LANES), F32)
    wide, *sends = call(
        functools.partial(pack_y_kernel, gxs), [((20, 8, LANES), F32)] + [half] * (1 if gys == 2 else 2)
    )(main, got_a, got_b)
    gots = [send(sends[0], lambda x, y, z: (x, y ^ 1, z))]
    if gys > 2:
        gots.append(send(sends[1], lambda x, y, z: (x, odd_partner(y) % gys, z)))
    part = ((16, ROWS, LANES), F32)
    whole, send_a, send_b = call(functools.partial(pack_z_kernel, gys), [((20, ROWS, LANES), F32), part, part])(wide, *gots)
    got_a = send(send_a, lambda x, y, z: (x, y, z ^ 1))
    got_b = send(send_b, z_second)

    scale_w, mass_w, source_w, bounds = call(
        functools.partial(window_kernel, gzs),
        [
            ((12, ROWS, LANES), F32),
            ((10, ROWS, LANES), F32),
            ((10, 3, ROWS, LANES), F32),
            ((3, 8, 128), F32),
        ],
        specs=[SM] + [VM] * 5,
    )(blocks, whole, got_a, got_b, fine_abs, local_abs)

    step = 4
    while step < gxs:
        bounds = jnp.maximum(bounds, send(bounds, lambda x, y, z: (x ^ step, y, z)))
        step *= 2
    others = [send(bounds, lambda x, y, z, flip=flip: (x ^ flip, y, z)) for flip in (1, 2, 3)]
    (power_1,) = call(
        power_kernel, [((8, 3, ROWS, LANES), F32)], specs=[SM] + [VM] * 4, flops=500000000, size=1000000
    )(blocks, scale_w, mass_w, source_w, fine)
    power_2, message = call(
        restrict_kernel, [((6, 3, ROWS, LANES), F32), ((17, 8, 128), F32)], specs=[SM] + [VM] * 9
    )(blocks, scale_w, mass_w, source_w, power_1, fine, bounds, *others)

    ordered = not (gys == 2 and gzs == 4)
    if ordered:
        gathered = lax.all_gather(message, ("gz", "gy"), tiled=False)
    else:
        four = jnp.stack(
            [
                message,
                send(message, lambda x, y, z: (x, y, z ^ 2)),
                send(message, lambda x, y, z: (x, y ^ 1, z)),
                send(message, lambda x, y, z: (x, y ^ 1, z ^ 2)),
            ]
        )
        gathered = jnp.concatenate([four, send(four, lambda x, y, z: (x, y, z ^ 1))])

    (result,) = call(
        functools.partial(final_kernel, gzs, gys, ordered),
        [(right_side.shape, F32)],
        specs=[SM] + [VM] * 8,
        scratch=[
            pltpu.VMEM((gzs, gys, 5, 8, 128), F32),
            pltpu.VMEM((planes, 5, rows, 128), F32),
            pltpu.VMEM((planes + 4, 3 * rows, 128), F32),
        ],
    )(blocks, gathered, scale_w, mass_w, source_w, power_1, power_2, fine, mid)
    return result


def solution(mesh):
    placed = (P(None, "gz", "gy", "gx"), P("gz", "gy", "gx"), P("gz", "gy", "gx"), P())
    return jax.shard_map(
        on_device, mesh=mesh, in_specs=placed, out_specs=P(None, "gz", "gy", "gx"), check_vma=False
    )
```

```python
import functools

import jax
import jax.numpy as jnp
from jax import lax
from jax.experimental import pallas as pl
from jax.experimental.pallas import tpu as pltpu
from jax.sharding import PartitionSpec as P

AXES = ("gx", "gy", "gz")
COARSE_ITERS = 8
SMOOTH_RATIO = 20.0
COARSE_RATIO = 200.0
F32, BF16 = jnp.float32, jnp.bfloat16
VM = pl.BlockSpec(memory_space=pltpu.VMEM)
SM = pl.BlockSpec(memory_space=pltpu.SMEM)
HB = pl.BlockSpec(memory_space=pltpu.HBM)
LANES = 256
PAD = 3


def call(kernel, outs, specs=None, scratch=(), flops=1000000, size=100000, grant=None):
    params = pltpu.CompilerParams(vmem_limit_bytes=grant * 1024 * 1024) if grant else None
    outs = [jax.ShapeDtypeStruct(shape, dtype) for shape, dtype in outs]

    def run(*args):
        return pl.pallas_call(
            kernel,
            out_shape=outs,
            in_specs=specs or [VM] * len(args),
            out_specs=[VM] * len(outs),
            scratch_shapes=scratch,
            compiler_params=params,
            cost_estimate=pl.CostEstimate(flops=flops, bytes_accessed=size, transcendentals=0),
        )(*args)

    return run


def iota(shape, dim):
    return lax.broadcasted_iota(jnp.int32, shape, dim)


def ones_where(mask):
    return jnp.where(mask, 1.0, 0.0).astype(BF16)


def split(values):
    high = values.astype(BF16)
    return high, (values - high.astype(F32)).astype(BF16)


def dot(left, right):
    return jnp.dot(left, right, preferred_element_type=F32)


def lanes_apply(values, stacked):
    return dot(jnp.concatenate(split(values), axis=1), stacked)


def rows_apply(selection, values):
    width = values.shape[1]
    product = dot(selection, jnp.concatenate(split(values), axis=1))
    return product[:, :width] + product[:, width:]


def banded(matrix_high, matrix_low, values):
    high, low = split(values)
    return dot(matrix_high, high) + dot(matrix_low, high) + dot(matrix_high, low)


def banded_stacked(matrix, values):
    high, low = split(values)
    return dot(matrix, jnp.concatenate([high, high, low], axis=0))


def shifted_sum(product, slabs, rows, lanes):
    parts = product.reshape(slabs, 3, rows, lanes)
    below = parts[:, 0].reshape(slabs * rows, lanes)
    above = parts[:, 2].reshape(slabs * rows, lanes)
    here = parts[:, 1].reshape(slabs * rows, lanes)
    return here + pltpu.roll(below, 1, 1) + pltpu.roll(above, lanes - 1, 1)


def group_of(slab):
    return max(1, 256 // slab - 2)


def groups(planes, most):
    sizes = []
    while planes:
        size = min(most, planes)
        if most > 2 and planes == most + 1:
            size = 2
        sizes.append(size)
        planes -= size
    return sizes


def fine_stencil(matrix, values):
    planes, rows = values.shape[0] - 2, values.shape[2]
    slab = 3 * rows
    flat = values.reshape((planes + 2) * slab, LANES)
    outs = []
    at = 0
    for size in groups(planes, group_of(slab)):
        height, depth = size * 3 * slab, (size + 2) * slab
        product = banded(
            matrix[0, :height, :depth], matrix[1, :height, :depth], flat[at * slab : at * slab + depth]
        )
        outs.append(shifted_sum(product, size, slab, LANES))
        at += size
    return jnp.concatenate(outs, axis=0).reshape(planes, 3, rows, LANES)


def panels(value_of, others, rows, width):
    column = iota((8, width), 1)
    which = column // rows
    row_in = column % rows
    result = {}
    for step_x in range(3):
        for comp in range(3):
            coeffs = []
            for step_y in range(3):
                coeff = jnp.zeros((8, width), F32)
                for plane in range(3):
                    for other in range(others):
                        value = value_of(plane * 9 + step_y * 3 + step_x, comp, other)
                        coeff = jnp.where(which == plane * others + other, value, coeff)
                coeffs.append(coeff)
            pieces = []
            for block in range(rows // 8):
                gap = row_in - (iota((8, width), 0) + block * 8)
                piece = jnp.zeros((8, width), F32)
                for step_y in range(3):
                    piece = jnp.where(gap == step_y - 1, coeffs[step_y], piece)
                pieces.append(piece)
            result[step_x, comp] = jnp.concatenate(pieces, axis=0)
    return result


def turned(value, turn):
    turn %= value.shape[1]
    return pltpu.roll(value, turn, 1) if turn else value


def parts_of(value):
    high = value.astype(BF16).astype(F32)
    return high, value - high


def stack3(value, size):
    high, low = parts_of(value)
    return (high + turned(low, size) + turned(high, 2 * size)).astype(BF16)


def up128(size):
    return -(-size // 128) * 128


def matrices_kernel(
    rows, planes, blocks, fine, fine_bound, mid, mid_bound, coarse, coarse_bound, coarse_diag,
    gather_rows, spread_rows, expand, fold, unfold, squeeze, stretch,
):
    def direct(offset, comp, other):
        return blocks[offset * 9 + comp * 3 + other]

    def absolute(offset, comp, other):
        at = offset * 9 + comp * 3
        return jnp.abs(blocks[at]) + jnp.abs(blocks[at + 1]) + jnp.abs(blocks[at + 2])

    slab = 3 * rows
    group = group_of(slab)
    found = panels(direct, 3, rows, fine.shape[2])
    bound = panels(absolute, 1, rows, fine_bound.shape[1])
    for plane in range(group):
        for step_x in range(3):
            start = (plane * 3 + step_x) * slab
            value = turned(jnp.concatenate([found[step_x, comp] for comp in range(3)], axis=0), plane * slab)
            high, low = split(value)
            fine[0, start : start + slab, :] = high
            fine[1, start : start + slab, :] = low
            value = turned(jnp.concatenate([bound[step_x, comp] for comp in range(3)], axis=0), plane * rows)
            fine_bound[start : start + slab, :] = stack3(value, (group + 2) * rows)

    rows, planes = rows // 2, planes // 2
    slab = 3 * rows
    width, bound_width = mid.shape[2], mid_bound.shape[1]
    found = panels(direct, 3, rows, width)
    bound = panels(absolute, 1, rows, bound_width)

    def cut(value, plane, size):
        column = iota(value.shape, 1)
        if plane == 0:
            value = jnp.where(column < size, 0.0, value)
        if plane == planes - 1:
            value = jnp.where(column >= 2 * size, 0.0, value)
        return turned(value, (plane - 1) * size)

    for plane in range(planes):
        for step_x in range(3):
            start = (plane * 3 + step_x) * slab
            value = jnp.concatenate([found[step_x, comp] for comp in range(3)], axis=0)
            high, low = split(cut(value, plane, slab))
            mid[0, start : start + slab, :] = high
            mid[1, start : start + slab, :] = low
            value = jnp.concatenate([bound[step_x, comp] for comp in range(3)], axis=0)
            mid_bound[start : start + slab, :] = stack3(cut(value, plane, rows), planes * rows)

    few, half = rows // 2, planes // 2
    tall, wide = half * 9 * few, half * 3 * few
    place = iota((tall, 2 * tall), 0)
    choose = ones_where(iota((tall, 2 * tall), 1) == place // few * rows + place % few)

    def smaller(matrix, count, size):
        place = iota((2 * count, size), 1)
        pick = ones_where(iota((2 * count, size), 0) == place // few * rows + place % few)
        return dot(dot(choose, matrix).astype(BF16), pick)

    high = smaller(mid[0, : 2 * tall, : 2 * wide], wide, coarse.shape[1])
    low = smaller(mid[1, : 2 * tall, : 2 * wide], wide, coarse.shape[1])
    keep = iota(high.shape, 1) < wide
    high, low = jnp.where(keep, high, 0.0), jnp.where(keep, low, 0.0)
    coarse[...] = (high + turned(low, wide) + turned(high, 2 * wide)).astype(BF16)
    count = half * few
    size = planes * rows
    whole = mid_bound[: 2 * tall, :]
    high = smaller(whole[:, : 2 * count], count, coarse_bound.shape[1])
    low = smaller(whole[:, size : size + 2 * count], count, coarse_bound.shape[1])
    keep = iota(high.shape, 1) < count
    high, low = jnp.where(keep, high, 0.0), jnp.where(keep, low, 0.0)
    coarse_bound[...] = (high + turned(low, count) + turned(high, 2 * count)).astype(BF16)
    comp = (iota((wide, 128), 0) // few) % 3
    diag = [blocks[13 * 9 + 4 * at] for at in range(3)]
    coarse_diag[...] = jnp.where(comp == 0, diag[0], jnp.where(comp == 1, diag[1], diag[2]))

    def same_aggregate(out_row, in_row, out_rows, in_rows, ratio_z):
        same_plane = out_row // (3 * out_rows) == in_row // (3 * in_rows * ratio_z)
        same_comp = out_row // out_rows % 3 == in_row // in_rows % 3
        return jnp.logical_and(jnp.logical_and(same_plane, same_comp), out_row % out_rows == in_row % in_rows // 2)

    big = planes * slab
    shape = (wide, big)
    gather_rows[...] = ones_where(same_aggregate(iota(shape, 0), iota(shape, 1), few, rows, 2))
    shape = (big, 2 * wide)
    spread_rows[...] = ones_where(same_aggregate(iota(shape, 1) % wide, iota(shape, 0), few, rows, 2))
    shape = (2 * slab, 2 * slab)
    expand[...] = ones_where(same_aggregate(iota(shape, 1) % slab, iota(shape, 0), rows, 2 * rows, 1))
    shape = (256, 128)
    fold[...] = ones_where(iota(shape, 0) % 128 // 2 == iota(shape, 1) % 64)
    unfold[...] = ones_where(iota(shape, 0) % 128 == iota(shape, 1) // 2)
    shape = (2 * LANES, 128)
    squeeze[...] = ones_where(iota(shape, 0) % LANES // 2 == iota(shape, 1))
    shape = (256, LANES)
    stretch[...] = ones_where(iota(shape, 0) % 128 == iota(shape, 1) // 2)


def halves(planes, low):
    first, second = planes[:10], pltpu.roll(planes[10:], 64, 2)
    return jnp.where(low, second, first), jnp.where(low, first, second)


def pack_kernel(source, scale, mass, main, send_a, send_b, sems):
    copies = [
        pltpu.make_async_copy(source.at[comp], main.at[pl.ds(comp * 4, 4)], sems.at[comp]) for comp in range(3)
    ]
    copies.append(pltpu.make_async_copy(scale, main.at[pl.ds(12, 4)], sems.at[3]))
    copies.append(pltpu.make_async_copy(mass, main.at[pl.ds(16, 4)], sems.at[4]))
    for copy in copies:
        copy.start()
    for copy in copies:
        copy.wait()
    high, low = halves(main[...], iota((10, 8, 128), 2) < 64)
    even = lax.rem(lax.axis_index("gx"), 2) == 0
    send_a[...] = jnp.where(even, high, low)
    send_b[...] = jnp.where(even, low, high)


def widen_kernel(count, main, got_a, got_b, wide):
    index = lax.axis_index("gx")
    even = lax.rem(index, 2) == 0
    first, second = got_a[...], got_b[...]
    above = jnp.where(index < count - 1, jnp.where(even, first, second), 0.0)
    below = jnp.where(index > 0, jnp.where(even, second, first), 0.0)
    low = iota((10, 8, 128), 2) < 64
    wide[:, :, :128] = main[...]
    wide[:10, :, 128:] = jnp.where(low, above, below)
    wide[10:, :, 128:] = jnp.where(low, pltpu.roll(above, 64, 2), pltpu.roll(below, 64, 2))


def inverse_diagonal(scale, mass, blocks, factor):
    square = scale * scale
    parts = []
    for comp in range(3):
        diag = factor * blocks[13 * 9 + comp * 4] * square + mass
        parts.append(jnp.where(scale > 0.0, 1.0 / diag, 0.0)[:, None])
    return jnp.concatenate(parts, axis=1)


def largest(ratio, lanes):
    width = ratio.shape[1]
    flat = jnp.max(ratio.reshape(-1, 8, width), axis=0)
    own = jnp.where(iota((8, width), 1) < lanes, flat, -jnp.inf)
    return jnp.full((8, 128), jnp.max(own), F32)


def paired_planes(values):
    pairs = values.reshape((-1, 2) + values.shape[1:])
    return pairs[:, 0] + pairs[:, 1]


def paired_rows(held, values):
    for half in (0, 1):
        held[half] = values[:, half * 128 : half * 128 + 128]
    count = held.shape[1] // 2
    return jnp.concatenate(
        [held[half, pl.ds(0, count, stride=2)] + held[half, pl.ds(1, count, stride=2)] for half in (0, 1)], axis=1
    )


def window_kernel(
    gys, ordered, blocks, *refs
):
    (*blocks_in, fine_bound, mid_bound, coarse_bound, coarse_diag, gather_rows, fold, squeeze,
     source_w, scale_w, mass_w, inverse_w, spread_1w, weight_1w, inverse_1w, spread_2w, weight_2w, inverse_2w, bounds, held) = refs
    planes, rows = scale_w.shape[0] - 2 * PAD, scale_w.shape[1]
    gz, gy = lax.axis_index("gz"), lax.axis_index("gy")
    for at in (0, planes + PAD):
        source_w[at : at + PAD] = jnp.zeros((PAD, 3, rows, LANES), F32)
        inverse_w[at : at + PAD] = jnp.zeros((PAD, 3, rows, LANES), F32)
        scale_w[at : at + PAD] = jnp.zeros((PAD, rows, LANES), F32)
        mass_w[at : at + PAD] = jnp.zeros((PAD, rows, LANES), F32)
    number = 0
    for ref in blocks_in:
        for block in range(ref.shape[0]):
            if ordered:
                place_z, place_y = number // gys, number % gys
            else:
                place_z = lax.bitwise_xor(gz, number // 4 + 2 * (number % 2))
                place_y = lax.bitwise_xor(gy, number % 4 // 2)
            at_z = pl.ds(PAD + 4 * place_z, 4)
            at_y = pl.ds(pl.multiple_of(8 * place_y, 8), 8)
            for comp in range(3):
                source_w[at_z, comp, at_y, :] = ref[block, comp * 4 : comp * 4 + 4]
            scale_w[at_z, at_y, :] = ref[block, 12:16]
            mass_w[at_z, at_y, :] = ref[block, 16:20]
            number += 1

    scale, mass = scale_w[PAD : PAD + planes], mass_w[PAD : PAD + planes]
    inverse = inverse_diagonal(scale, mass, blocks, 1.0)
    inverse_w[PAD : PAD + planes] = inverse
    slab = 3 * rows
    outs = []
    at = 0
    for size in groups(planes, group_of(slab)):
        near = scale_w[PAD - 1 + at : PAD + 1 + at + size].reshape((size + 2) * rows, LANES)
        if size < group_of(slab):
            near = jnp.concatenate([near, jnp.zeros(((group_of(slab) - size) * rows, LANES), F32)], axis=0)
        depth = 3 * (group_of(slab) + 2) * rows
        outs.append(shifted_sum(banded_stacked(fine_bound[: size * 3 * slab, :depth], near), size, slab, LANES))
        at += size
    total = jnp.concatenate(outs, axis=0).reshape(planes, 3, rows, LANES)
    ratio = (scale[:, None] * total + mass[:, None]) * inverse
    bounds[0] = largest(ratio.reshape(planes * slab, LANES), 128)

    rows, planes = rows // 2, planes // 2
    slab = 3 * rows
    count = planes * rows
    pairs = [
        paired_rows(held.at[at], paired_planes(values).reshape(2 * count, LANES))
        for at, values in enumerate((scale, mass))
    ]
    middle = lanes_apply(jnp.concatenate(pairs, axis=0), squeeze[...])
    scale_1 = (middle[:count] * 0.125).reshape(planes, rows, 128)
    mass_1 = middle[count:].reshape(planes, rows, 128)
    inverse_1 = inverse_diagonal(scale_1, mass_1, blocks, 2.0).reshape(planes * slab, 128)
    spread_1 = jnp.broadcast_to(scale_1[:, None], (planes, 3, rows, 128)).reshape(planes * slab, 128)
    weight_1 = jnp.broadcast_to(mass_1[:, None], (planes, 3, rows, 128)).reshape(planes * slab, 128)
    product = banded_stacked(mid_bound[:, : 3 * count], scale_1.reshape(count, 128))
    total = shifted_sum(product, planes, slab, 128)
    bounds[1] = largest((2.0 * spread_1 * total + weight_1) * inverse_1, 64)
    spread_1w[...], weight_1w[...], inverse_1w[...] = spread_1, weight_1, inverse_1

    both = rows_apply(gather_rows[...], jnp.concatenate([spread_1, weight_1], axis=1))
    spread_2 = lanes_apply(both[:, :128], fold[...]) * 0.125
    weight_2 = lanes_apply(both[:, 128:], fold[...])
    inverse_2 = jnp.where(spread_2 > 0.0, 1.0 / (4.0 * coarse_diag[...] * spread_2 * spread_2 + weight_2), 0.0)
    rows, planes = rows // 2, planes // 2
    single = spread_2.reshape(planes, 3, rows, 128)[:, 0].reshape(planes * rows, 128)
    total = shifted_sum(banded_stacked(coarse_bound[:, : 3 * planes * rows], single), planes, 3 * rows, 128)
    bounds[2] = largest((4.0 * spread_2 * total + weight_2) * inverse_2, 32)
    spread_2w[...], weight_2w[...], inverse_2w[...] = spread_2, weight_2, inverse_2


def fine_operator(matrix, scale, mass, values):
    total = fine_stencil(matrix, scale[:, None] * values)
    return scale[1:-1][:, None] * total + mass[:, None] * values[1:-1]


def inner_power(scale_w, mass_w, inverse_w, matrix, values):
    planes = scale_w.shape[0] - 2 * PAD
    near = slice(PAD - 1, PAD + planes + 1)
    return fine_operator(matrix, scale_w[near], mass_w[PAD : PAD + planes], inverse_w[near] * values[near])


def power_kernel(scale_w, mass_w, inverse_w, source_w, fine, power):
    planes, shape = scale_w.shape[0] - 2 * PAD, power.shape[1:]
    power[:PAD] = jnp.zeros((PAD,) + shape, F32)
    power[PAD + planes :] = jnp.zeros((PAD,) + shape, F32)
    power[PAD : PAD + planes] = inner_power(scale_w, mass_w, inverse_w, fine, source_w)


def restrict_kernel(scale_w, mass_w, inverse_w, source_w, power_1, fine, squeeze, power_2, basis, held):
    planes, rows = scale_w.shape[0] - 2 * PAD, scale_w.shape[1]
    power_kernel(scale_w, mass_w, inverse_w, power_1, fine, power_2)
    third = inner_power(scale_w, mass_w, inverse_w, fine, power_2)
    inner = slice(PAD, PAD + planes)
    size = planes // 2 * 3 * rows
    for at, values in enumerate((source_w[inner], power_1[inner], power_2[inner], third)):
        pairs = paired_rows(held.at[at], paired_planes(values).reshape(size, LANES))
        basis[at] = lanes_apply(pairs, squeeze[...])


def chebyshev_scalars(bound, ratio):
    lower = bound / ratio
    return 0.5 * (bound + lower), 0.5 * (bound - lower)


def scaled(coeff, values):
    lanes = values.shape[-1]
    if lanes != 128:
        coeff = jnp.concatenate([coeff] * (lanes // 128), axis=1)
    flat = values.reshape(-1, 8, lanes)
    return (coeff[None] * flat).reshape(values.shape)


def chebyshev(residue, degree, inverse, bound, ratio, operate, keep):
    centre, spread = chebyshev_scalars(bound, ratio)
    sigma = centre / spread
    rho = 1.0 / sigma
    direction = scaled(1.0 / centre, inverse * residue)
    total = direction
    for step in range(degree):
        if step < degree - 1 or keep:
            residue = residue - operate(direction)
        if step < degree - 1:
            rho_next = 1.0 / (2.0 * sigma - rho)
            direction = scaled(rho_next * rho, direction) + scaled(2.0 * rho_next / spread, inverse * residue)
            total = total + direction
            rho = rho_next
    return total, residue


def final_kernel(
    bounds_a, bounds_b, source_w, scale_w, mass_w, inverse_w, power_1, power_2, basis,
    spread_1w, weight_1w, inverse_1w, spread_2w, weight_2w, inverse_2w,
    fine, mid, coarse, gather_rows, spread_rows, expand, fold, unfold, stretch, result, lifted_w, answer_w,
):
    rows = scale_w.shape[1] // 2
    planes = (scale_w.shape[0] - 2 * PAD) // 2
    slab = 3 * rows
    size = planes * slab
    small = size // 4
    gz, gy = lax.axis_index("gz"), lax.axis_index("gy")
    bounds = jnp.maximum(bounds_a[...], bounds_b[...])

    centre, spread = chebyshev_scalars(bounds[0], SMOOTH_RATIO)
    sigma = centre / spread
    rho = 1.0 / sigma
    rho_next = 1.0 / (2.0 * sigma - rho)
    keep, push = rho_next * rho, 2.0 * rho_next / spread
    beta = push / centre
    gamma = 1.0 / centre + keep / centre + push
    omega = (4.0 / 3.0) / bounds[0]

    source_1 = (
        basis[0]
        - scaled(gamma + omega, basis[1])
        + scaled(beta + omega * gamma, basis[2])
        - scaled(omega * beta, basis[3])
    )
    spread_1, weight_1, inverse_1 = spread_1w[...], weight_1w[...], inverse_1w[...]
    spread_2, weight_2, inverse_2 = spread_2w[...], weight_2w[...], inverse_2w[...]

    def operate_1(values):
        product = banded(mid[0, :, :size], mid[1, :, :size], spread_1 * values)
        return 2.0 * spread_1 * shifted_sum(product, planes, slab, 128) + weight_1 * values

    def operate_2(values):
        product = banded_stacked(coarse[:, : 3 * small], spread_2 * values)
        return 4.0 * spread_2 * shifted_sum(product, planes // 2, slab // 2, 128) + weight_2 * values

    omega_1 = (4.0 / 3.0) / bounds[1]
    iterate, residue = chebyshev(source_1, 2, inverse_1, bounds[1], SMOOTH_RATIO, operate_1, True)
    smoothed = residue - scaled(omega_1, operate_1(inverse_1 * residue))
    source_2 = lanes_apply(rows_apply(gather_rows[...], smoothed), fold[...])
    error_2, _ = chebyshev(source_2, COARSE_ITERS, inverse_2, bounds[2], COARSE_RATIO, operate_2, False)
    lifted = lanes_apply(error_2, unfold[...])
    lifted = dot(spread_rows[...], jnp.concatenate(split(lifted), axis=0))
    iterate = iterate + lifted - scaled(omega_1, inverse_1 * operate_1(lifted))
    residue = source_1 - operate_1(iterate)
    more, _ = chebyshev(residue, 2, inverse_1, bounds[1], SMOOTH_RATIO, operate_1, False)
    error_1 = iterate + more

    lifted_w[0:2] = jnp.zeros((2, slab, 128), F32)
    lifted_w[planes + 2 : planes + 4] = jnp.zeros((2, slab, 128), F32)
    lifted_w[2 : planes + 2] = error_1.reshape(planes, slab, 128)
    near = lifted_w[pl.ds(2 * gz, 6)].reshape(6 * slab, 128)
    wide = lanes_apply(near, stretch[...]).reshape(6, slab, LANES)
    side = jnp.concatenate([wide[plane] for plane in range(6)], axis=1)
    tall = dot(expand[...], jnp.concatenate(split(side), axis=0))
    slabs = [tall[:, plane * LANES : plane * LANES + LANES] for plane in range(6)]
    error = jnp.stack([slabs[(plane + 1) // 2] for plane in range(10)], axis=0).reshape(10, 3, 2 * rows, LANES)

    def near_own(ref, reach):
        return ref[pl.ds(4 * gz + PAD - reach, 4 + 2 * reach)]

    scale, mass, inverse = near_own(scale_w, 3), near_own(mass_w, 2), near_own(inverse_w, 2)
    source = near_own(source_w, 2)
    image = fine_operator(fine, scale, mass, error)
    iterate = inverse * (scaled(gamma, source) - scaled(beta, near_own(power_1, 2)) - scaled(omega, image)) + error[1:9]
    residue = source[1:7] - fine_operator(fine, scale[1:9], mass[1:7], iterate)
    direction = scaled(1.0 / centre, inverse[1:7] * residue)
    last = residue[1:5] - fine_operator(fine, scale[2:8], mass[2:6], direction)
    answer = iterate[2:6] + scaled(1.0 + keep, direction[1:5]) + scaled(push, inverse[2:6] * last)
    answer_w[...] = answer[:, :, :, :128]
    for comp in range(3):
        result[comp] = answer_w[:, comp, pl.ds(pl.multiple_of(8 * gy, 8), 8), :]


def swap_pairs(counts, target):
    def number(place):
        return (place[0] * counts[1] + place[1]) * counts[2] + place[2]

    places = [(x, y, z) for x in range(counts[0]) for y in range(counts[1]) for z in range(counts[2])]
    return [(number(place), number(target(*place))) for place in places]


def odd_partner(index):
    return index - 1 if index % 2 == 0 else index + 1


def on_device(right_side, stiff_scale, nodal_mass, stencil_blocks):
    counts = tuple(lax.axis_size(axis) for axis in AXES)
    gxs, gys, gzs = counts
    blocks = stencil_blocks.reshape(243)

    def send(values, target):
        return lax.ppermute(values, AXES, swap_pairs(counts, target))

    def x_second(x, y, z):
        return (x, y, z ^ 1) if x in (0, gxs - 1) else (odd_partner(x), y, z)

    rows, planes = 8 * gys, 4 * gzs
    grant = 20 if planes * rows <= 256 else 48
    slab = 3 * rows
    group = group_of(slab)
    size_1, count_1 = planes * slab // 4, planes * rows // 4
    size_2, count_2 = size_1 // 4, count_1 // 4
    (
        fine, fine_bound, mid, mid_bound, coarse, coarse_bound, coarse_diag,
        gather_rows, spread_rows, expand, fold, unfold, squeeze, stretch,
    ) = call(
        functools.partial(matrices_kernel, rows, planes),
        [
            ((2, group * 3 * slab, up128((group + 2) * slab)), BF16),
            ((group * 3 * slab, up128(3 * (group + 2) * rows)), BF16),
            ((2, 3 * size_1, up128(size_1)), BF16),
            ((3 * size_1, up128(3 * count_1)), BF16),
            ((3 * size_2, up128(3 * size_2)), BF16),
            ((3 * size_2, up128(3 * count_2)), BF16),
            ((size_2, 128), F32),
            ((size_2, size_1), BF16),
            ((size_1, 2 * size_2), BF16),
            ((slab, slab), BF16),
            ((256, 128), BF16),
            ((256, 128), BF16),
            ((2 * LANES, 128), BF16),
            ((256, LANES), BF16),
        ],
        specs=[SM],
        flops=5000000000,
        size=8000000,
        grant=grant,
    )(blocks)

    half = ((10, 8, 128), F32)
    main, send_a, send_b = call(
        pack_kernel,
        [((20, 8, 128), F32), half, half],
        specs=[HB] * 3,
        scratch=[pltpu.SemaphoreType.DMA((5,))],
        grant=8,
    )(right_side, stiff_scale, nodal_mass)
    got_a = send(send_a, lambda x, y, z: (x ^ 1, y, z))
    got_b = send(send_b, x_second)
    (wide,) = call(functools.partial(widen_kernel, gxs), [((20, 8, LANES), F32)], grant=8)(main, got_a, got_b)
    ordered = not (gys == 2 and gzs == 4)
    if ordered:
        gathered = [lax.all_gather(wide, ("gz", "gy"), tiled=False)]
    else:
        near = [
            wide,
            send(wide, lambda x, y, z: (x, y, z ^ 2)),
            send(wide, lambda x, y, z: (x, y ^ 1, z)),
            send(wide, lambda x, y, z: (x, y ^ 1, z ^ 2)),
        ]
        near[3], fine = lax.optimization_barrier((near[3], fine))
        gathered = [block[None] for block in near + [send(block, lambda x, y, z: (x, y, z ^ 1)) for block in near]]

    field = ((planes + 2 * PAD, 3, rows, LANES), F32)
    single = ((planes + 2 * PAD, rows, LANES), F32)
    source_w, scale_w, mass_w, inverse_w, *levels, bounds = call(
        functools.partial(window_kernel, gys, ordered),
        [field, single, single, field] + [((size_1, 128), F32)] * 3 + [((size_2, 128), F32)] * 3 + [((3, 8, 128), F32)],
        specs=[SM] + [VM] * (len(gathered) + 7),
        scratch=[pltpu.VMEM((2, 2, planes * rows // 2, 128), F32)],
        grant=grant,
    )(blocks, *gathered, fine_bound, mid_bound, coarse_bound, coarse_diag, gather_rows, fold, squeeze)

    step = 4
    while step < gxs:
        bounds = jnp.maximum(bounds, send(bounds, lambda x, y, z: (x ^ step, y, z)))
        step *= 2
    bounds = jnp.maximum(bounds, send(bounds, lambda x, y, z: (x ^ 1, y, z ^ 1)))
    other = send(bounds, lambda x, y, z: (x ^ 2, y, z ^ 1))
    (power_1,) = call(power_kernel, [field], flops=1000000000, size=4000000, grant=grant)(scale_w, mass_w, inverse_w, source_w, fine)
    power_2, basis = call(
        restrict_kernel,
        [field, ((4, size_1, 128), F32)],
        scratch=[pltpu.VMEM((4, 2, 2 * size_1, 128), F32)],
        flops=2000000000,
        size=8000000,
        grant=grant,
    )(scale_w, mass_w, inverse_w, source_w, power_1, fine, squeeze)
    (result,) = call(
        final_kernel,
        [(right_side.shape, F32)],
        scratch=[
            pltpu.VMEM((planes // 2 + 4, slab // 2, 128), F32),
            pltpu.VMEM((4, 3, rows, 128), F32),
        ],
        grant=grant,
    )(
        bounds, other, source_w, scale_w, mass_w, inverse_w, power_1, power_2, basis, *levels,
        fine, mid, coarse, gather_rows, spread_rows, expand, fold, unfold, stretch,
    )
    return result


def solution(mesh):
    placed = (P(None, "gz", "gy", "gx"), P("gz", "gy", "gx"), P("gz", "gy", "gx"), P())
    return jax.shard_map(
        on_device, mesh=mesh, in_specs=placed, out_specs=P(None, "gz", "gy", "gx"), check_vma=False
    )
```

```python
import functools

import jax
import jax.numpy as jnp
from jax import lax
from jax.experimental import pallas as pl
from jax.experimental.pallas import tpu as pltpu
from jax.sharding import PartitionSpec as P

AXES = ("gx", "gy", "gz")
COARSE_ITERS = 8
SMOOTH_RATIO = 20.0
COARSE_RATIO = 200.0
F32, BF16 = jnp.float32, jnp.bfloat16
VM = pl.BlockSpec(memory_space=pltpu.VMEM)
SM = pl.BlockSpec(memory_space=pltpu.SMEM)
LANES = 256
PAD = 3


def call(kernel, outs, specs=None, scratch=(), flops=1000000, size=100000, grant=None):
    params = pltpu.CompilerParams(vmem_limit_bytes=grant * 1024 * 1024) if grant else None
    outs = [jax.ShapeDtypeStruct(shape, dtype) for shape, dtype in outs]

    def run(*args):
        return pl.pallas_call(
            kernel,
            out_shape=outs,
            in_specs=specs or [VM] * len(args),
            out_specs=[VM] * len(outs),
            scratch_shapes=scratch,
            compiler_params=params,
            cost_estimate=pl.CostEstimate(flops=flops, bytes_accessed=size, transcendentals=0),
        )(*args)

    return run


def iota(shape, dim):
    return lax.broadcasted_iota(jnp.int32, shape, dim)


def ones_where(mask):
    return jnp.where(mask, 1.0, 0.0).astype(BF16)


def split(values):
    high = values.astype(BF16)
    return high, (values - high.astype(F32)).astype(BF16)


def dot(left, right):
    return jnp.dot(left, right, preferred_element_type=F32)


def lanes_apply(values, stacked):
    return dot(jnp.concatenate(split(values), axis=1), stacked)


def rows_apply(selection, values):
    width = values.shape[1]
    product = dot(selection, jnp.concatenate(split(values), axis=1))
    return product[:, :width] + product[:, width:]


def banded(matrix_high, matrix_low, values):
    high, low = split(values)
    return dot(matrix_high, high) + dot(matrix_low, high) + dot(matrix_high, low)


def banded_beside(matrix_high, matrix_low, values):
    high, low = split(values)
    width = values.shape[1]
    product = dot(matrix_high, jnp.concatenate([high, low], axis=1))
    return product[:, :width] + product[:, width:] + dot(matrix_low, high)


def banded_stacked(matrix, values):
    high, low = split(values)
    return dot(matrix, jnp.concatenate([high, high, low], axis=0))


def shifted_sum(product, slabs, rows, lanes):
    parts = product.reshape(slabs, 3, rows, lanes)
    below = parts[:, 0].reshape(slabs * rows, lanes)
    above = parts[:, 2].reshape(slabs * rows, lanes)
    here = parts[:, 1].reshape(slabs * rows, lanes)
    return here + pltpu.roll(below, 1, 1) + pltpu.roll(above, lanes - 1, 1)


def group_of(slab):
    return max(1, 256 // slab - 2)


def groups(planes, most):
    sizes = []
    while planes:
        size = min(most, planes)
        if most > 2 and planes == most + 1:
            size = 2
        sizes.append(size)
        planes -= size
    return sizes


def fine_stencil(matrix, values):
    planes, rows = values.shape[0] - 2, values.shape[2]
    slab = 3 * rows
    flat = values.reshape((planes + 2) * slab, LANES)
    outs = []
    at = 0
    for size in groups(planes, group_of(slab)):
        height, depth = size * 3 * slab, (size + 2) * slab
        product = banded(
            matrix[0, :height, :depth], matrix[1, :height, :depth], flat[at * slab : at * slab + depth]
        )
        outs.append(shifted_sum(product, size, slab, LANES))
        at += size
    return jnp.concatenate(outs, axis=0).reshape(planes, 3, rows, LANES)


def panels(value_of, others, rows, width):
    column = iota((8, width), 1)
    which = column // rows
    row_in = column % rows
    result = {}
    for step_x in range(3):
        for comp in range(3):
            coeffs = []
            for step_y in range(3):
                coeff = jnp.zeros((8, width), F32)
                for plane in range(3):
                    for other in range(others):
                        value = value_of(plane * 9 + step_y * 3 + step_x, comp, other)
                        coeff = jnp.where(which == plane * others + other, value, coeff)
                coeffs.append(coeff)
            pieces = []
            for block in range(rows // 8):
                gap = row_in - (iota((8, width), 0) + block * 8)
                piece = jnp.zeros((8, width), F32)
                for step_y in range(3):
                    piece = jnp.where(gap == step_y - 1, coeffs[step_y], piece)
                pieces.append(piece)
            result[step_x, comp] = jnp.concatenate(pieces, axis=0)
    return result


def turned(value, turn):
    turn %= value.shape[1]
    return pltpu.roll(value, turn, 1) if turn else value


def parts_of(value):
    high = value.astype(BF16).astype(F32)
    return high, value - high


def stack3(value, size):
    high, low = parts_of(value)
    return (high + turned(low, size) + turned(high, 2 * size)).astype(BF16)


def up128(size):
    return -(-size // 128) * 128


def matrices_kernel(
    rows, planes, blocks, fine, fine_bound, mid, mid_bound, coarse, coarse_bound, coarse_diag,
    gather_rows, spread_rows, expand, fold, unfold, squeeze, stretch,
):
    def direct(offset, comp, other):
        return blocks[offset * 9 + comp * 3 + other]

    def absolute(offset, comp, other):
        at = offset * 9 + comp * 3
        return jnp.abs(blocks[at]) + jnp.abs(blocks[at + 1]) + jnp.abs(blocks[at + 2])

    slab = 3 * rows
    group = group_of(slab)
    found = panels(direct, 3, rows, fine.shape[2])
    bound = panels(absolute, 1, rows, fine_bound.shape[1])
    for plane in range(group):
        for step_x in range(3):
            start = (plane * 3 + step_x) * slab
            value = turned(jnp.concatenate([found[step_x, comp] for comp in range(3)], axis=0), plane * slab)
            high, low = split(value)
            fine[0, start : start + slab, :] = high
            fine[1, start : start + slab, :] = low
            value = turned(jnp.concatenate([bound[step_x, comp] for comp in range(3)], axis=0), plane * rows)
            fine_bound[start : start + slab, :] = stack3(value, (group + 2) * rows)

    rows, planes = rows // 2, planes // 2
    slab = 3 * rows
    width, bound_width = mid.shape[2], mid_bound.shape[1]
    found = panels(direct, 3, rows, width)
    bound = panels(absolute, 1, rows, bound_width)

    def cut(value, plane, size):
        column = iota(value.shape, 1)
        if plane == 0:
            value = jnp.where(column < size, 0.0, value)
        if plane == planes - 1:
            value = jnp.where(column >= 2 * size, 0.0, value)
        return turned(value, (plane - 1) * size)

    for plane in range(planes):
        for step_x in range(3):
            start = (plane * 3 + step_x) * slab
            value = jnp.concatenate([found[step_x, comp] for comp in range(3)], axis=0)
            high, low = split(cut(value, plane, slab))
            mid[0, start : start + slab, :] = high
            mid[1, start : start + slab, :] = low
            value = jnp.concatenate([bound[step_x, comp] for comp in range(3)], axis=0)
            mid_bound[start : start + slab, :] = stack3(cut(value, plane, rows), planes * rows)

    few, half = rows // 2, planes // 2
    tall, wide = half * 9 * few, half * 3 * few
    place = iota((tall, 2 * tall), 0)
    choose = ones_where(iota((tall, 2 * tall), 1) == place // few * rows + place % few)

    def smaller(matrix, count, size):
        place = iota((2 * count, size), 1)
        pick = ones_where(iota((2 * count, size), 0) == place // few * rows + place % few)
        return dot(dot(choose, matrix).astype(BF16), pick)

    high = smaller(mid[0, : 2 * tall, : 2 * wide], wide, coarse.shape[1])
    low = smaller(mid[1, : 2 * tall, : 2 * wide], wide, coarse.shape[1])
    keep = iota(high.shape, 1) < wide
    high, low = jnp.where(keep, high, 0.0), jnp.where(keep, low, 0.0)
    coarse[...] = (high + turned(low, wide) + turned(high, 2 * wide)).astype(BF16)
    count = half * few
    size = planes * rows
    whole = mid_bound[: 2 * tall, :]
    high = smaller(whole[:, : 2 * count], count, coarse_bound.shape[1])
    low = smaller(whole[:, size : size + 2 * count], count, coarse_bound.shape[1])
    keep = iota(high.shape, 1) < count
    high, low = jnp.where(keep, high, 0.0), jnp.where(keep, low, 0.0)
    coarse_bound[...] = (high + turned(low, count) + turned(high, 2 * count)).astype(BF16)
    comp = (iota((wide, 128), 0) // few) % 3
    diag = [blocks[13 * 9 + 4 * at] for at in range(3)]
    coarse_diag[...] = jnp.where(comp == 0, diag[0], jnp.where(comp == 1, diag[1], diag[2]))

    def same_aggregate(out_row, in_row, out_rows, in_rows, ratio_z):
        same_plane = out_row // (3 * out_rows) == in_row // (3 * in_rows * ratio_z)
        same_comp = out_row // out_rows % 3 == in_row // in_rows % 3
        return jnp.logical_and(jnp.logical_and(same_plane, same_comp), out_row % out_rows == in_row % in_rows // 2)

    big = planes * slab
    shape = (wide, big)
    gather_rows[...] = ones_where(same_aggregate(iota(shape, 0), iota(shape, 1), few, rows, 2))
    shape = (big, 2 * wide)
    spread_rows[...] = ones_where(same_aggregate(iota(shape, 1) % wide, iota(shape, 0), few, rows, 2))
    shape = (2 * slab, 2 * slab)
    expand[...] = ones_where(same_aggregate(iota(shape, 1) % slab, iota(shape, 0), rows, 2 * rows, 1))
    shape = (256, 128)
    fold[...] = ones_where(iota(shape, 0) % 128 // 2 == iota(shape, 1) % 64)
    unfold[...] = ones_where(iota(shape, 0) % 128 == iota(shape, 1) // 2)
    shape = (2 * LANES, 128)
    squeeze[...] = ones_where(iota(shape, 0) % LANES // 2 == iota(shape, 1))
    shape = (256, LANES)
    stretch[...] = ones_where(iota(shape, 0) % 128 == iota(shape, 1) // 2)


def halves(planes, low):
    first, second = planes[:10], pltpu.roll(planes[10:], 64, 2)
    return jnp.where(low, second, first), jnp.where(low, first, second)


def pack_kernel(main, send_a, send_b):
    high, low = halves(main[...], iota((10, 8, 128), 2) < 64)
    even = lax.rem(lax.axis_index("gx"), 2) == 0
    send_a[...] = jnp.where(even, high, low)
    send_b[...] = jnp.where(even, low, high)


def widen_kernel(count, main, got_b, got_a, wide):
    index = lax.axis_index("gx")
    even = lax.rem(index, 2) == 0
    first, second = got_a[...], got_b[...]
    above = jnp.where(index < count - 1, jnp.where(even, first, second), 0.0)
    below = jnp.where(index > 0, jnp.where(even, second, first), 0.0)
    low = iota((10, 8, 128), 2) < 64
    wide[:, :, :128] = main[...]
    wide[:10, :, 128:] = jnp.where(low, above, below)
    wide[10:, :, 128:] = jnp.where(low, pltpu.roll(above, 64, 2), pltpu.roll(below, 64, 2))


def inverse_diagonal(scale, mass, blocks, factor):
    square = scale * scale
    parts = []
    for comp in range(3):
        diag = factor * blocks[13 * 9 + comp * 4] * square + mass
        parts.append(jnp.where(scale > 0.0, 1.0 / diag, 0.0)[:, None])
    return jnp.concatenate(parts, axis=1)


def largest(ratio, lanes):
    width = ratio.shape[1]
    flat = jnp.max(ratio.reshape(-1, 8, width), axis=0)
    own = jnp.where(iota((8, width), 1) < lanes, flat, -jnp.inf)
    return jnp.full((8, 128), jnp.max(own), F32)


def paired_planes(values):
    pairs = values.reshape((-1, 2) + values.shape[1:])
    return pairs[:, 0] + pairs[:, 1]


def paired_rows(held, values):
    for half in (0, 1):
        held[half] = values[:, half * 128 : half * 128 + 128]
    count = held.shape[1] // 2
    return jnp.concatenate(
        [held[half, pl.ds(0, count, stride=2)] + held[half, pl.ds(1, count, stride=2)] for half in (0, 1)], axis=1
    )


def window_kernel(
    gys, ordered, blocks, *refs
):
    (*blocks_in, fine_bound, mid_bound, coarse_bound, coarse_diag, gather_rows, fold, squeeze,
     source_w, scale_w, mass_w, inverse_w, spread_1w, weight_1w, inverse_1w, spread_2w, weight_2w, inverse_2w, bounds, held) = refs
    planes, rows = scale_w.shape[0] - 2 * PAD, scale_w.shape[1]
    gz, gy = lax.axis_index("gz"), lax.axis_index("gy")
    for at in (0, planes + PAD):
        source_w[at : at + PAD] = jnp.zeros((PAD, 3, rows, LANES), F32)
        inverse_w[at : at + PAD] = jnp.zeros((PAD, 3, rows, LANES), F32)
        scale_w[at : at + PAD] = jnp.zeros((PAD, rows, LANES), F32)
        mass_w[at : at + PAD] = jnp.zeros((PAD, rows, LANES), F32)
    number = 0
    for ref in blocks_in:
        for block in range(ref.shape[0]):
            if ordered:
                place_z, place_y = number // gys, number % gys
            else:
                place_z = lax.bitwise_xor(gz, number // 4 + 2 * (number % 2))
                place_y = lax.bitwise_xor(gy, number % 4 // 2)
            at_z = pl.ds(PAD + 4 * place_z, 4)
            at_y = pl.ds(pl.multiple_of(8 * place_y, 8), 8)
            for comp in range(3):
                source_w[at_z, comp, at_y, :] = ref[block, comp * 4 : comp * 4 + 4]
            scale_w[at_z, at_y, :] = ref[block, 12:16]
            mass_w[at_z, at_y, :] = ref[block, 16:20]
            number += 1

    scale, mass = scale_w[PAD : PAD + planes], mass_w[PAD : PAD + planes]
    inverse = inverse_diagonal(scale, mass, blocks, 1.0)
    inverse_w[PAD : PAD + planes] = inverse
    slab = 3 * rows
    outs = []
    at = 0
    for size in groups(planes, group_of(slab)):
        near = scale_w[PAD - 1 + at : PAD + 1 + at + size].reshape((size + 2) * rows, LANES)
        if size < group_of(slab):
            near = jnp.concatenate([near, jnp.zeros(((group_of(slab) - size) * rows, LANES), F32)], axis=0)
        depth = 3 * (group_of(slab) + 2) * rows
        outs.append(shifted_sum(banded_stacked(fine_bound[: size * 3 * slab, :depth], near), size, slab, LANES))
        at += size
    total = jnp.concatenate(outs, axis=0).reshape(planes, 3, rows, LANES)
    ratio = (scale[:, None] * total + mass[:, None]) * inverse
    bounds[0] = largest(ratio.reshape(planes * slab, LANES), 128)

    rows, planes = rows // 2, planes // 2
    slab = 3 * rows
    count = planes * rows
    pairs = [
        paired_rows(held.at[at], paired_planes(values).reshape(2 * count, LANES))
        for at, values in enumerate((scale, mass))
    ]
    middle = lanes_apply(jnp.concatenate(pairs, axis=0), squeeze[...])
    scale_1 = (middle[:count] * 0.125).reshape(planes, rows, 128)
    mass_1 = middle[count:].reshape(planes, rows, 128)
    inverse_1 = inverse_diagonal(scale_1, mass_1, blocks, 2.0).reshape(planes * slab, 128)
    spread_1 = jnp.broadcast_to(scale_1[:, None], (planes, 3, rows, 128)).reshape(planes * slab, 128)
    weight_1 = jnp.broadcast_to(mass_1[:, None], (planes, 3, rows, 128)).reshape(planes * slab, 128)
    product = banded_stacked(mid_bound[:, : 3 * count], scale_1.reshape(count, 128))
    total = shifted_sum(product, planes, slab, 128)
    bounds[1] = largest((2.0 * spread_1 * total + weight_1) * inverse_1, 64)
    spread_1w[...], weight_1w[...], inverse_1w[...] = spread_1, weight_1, inverse_1

    both = rows_apply(gather_rows[...], jnp.concatenate([spread_1, weight_1], axis=1))
    spread_2 = lanes_apply(both[:, :128], fold[...]) * 0.125
    weight_2 = lanes_apply(both[:, 128:], fold[...])
    inverse_2 = jnp.where(spread_2 > 0.0, 1.0 / (4.0 * coarse_diag[...] * spread_2 * spread_2 + weight_2), 0.0)
    rows, planes = rows // 2, planes // 2
    single = spread_2.reshape(planes, 3, rows, 128)[:, 0].reshape(planes * rows, 128)
    total = shifted_sum(banded_stacked(coarse_bound[:, : 3 * planes * rows], single), planes, 3 * rows, 128)
    bounds[2] = largest((4.0 * spread_2 * total + weight_2) * inverse_2, 32)
    spread_2w[...], weight_2w[...], inverse_2w[...] = spread_2, weight_2, inverse_2


def fine_operator(matrix, scale, mass, values):
    total = fine_stencil(matrix, scale[:, None] * values)
    return scale[1:-1][:, None] * total + mass[:, None] * values[1:-1]


def inner_power(scale_w, mass_w, inverse_w, matrix, values):
    planes = scale_w.shape[0] - 2 * PAD
    near = slice(PAD - 1, PAD + planes + 1)
    return fine_operator(matrix, scale_w[near], mass_w[PAD : PAD + planes], inverse_w[near] * values[near])


def power_kernel(scale_w, mass_w, inverse_w, source_w, fine, power):
    planes, shape = scale_w.shape[0] - 2 * PAD, power.shape[1:]
    power[:PAD] = jnp.zeros((PAD,) + shape, F32)
    power[PAD + planes :] = jnp.zeros((PAD,) + shape, F32)
    power[PAD : PAD + planes] = inner_power(scale_w, mass_w, inverse_w, fine, source_w)


def restrict_kernel(scale_w, mass_w, inverse_w, source_w, power_1, fine, squeeze, power_2, basis, held):
    planes, rows = scale_w.shape[0] - 2 * PAD, scale_w.shape[1]
    power_kernel(scale_w, mass_w, inverse_w, power_1, fine, power_2)
    third = inner_power(scale_w, mass_w, inverse_w, fine, power_2)
    inner = slice(PAD, PAD + planes)
    size = planes // 2 * 3 * rows
    for at, values in enumerate((source_w[inner], power_1[inner], power_2[inner], third)):
        pairs = paired_rows(held.at[at], paired_planes(values).reshape(size, LANES))
        basis[at] = lanes_apply(pairs, squeeze[...])


def chebyshev_scalars(bound, ratio):
    lower = bound / ratio
    return 0.5 * (bound + lower), 0.5 * (bound - lower)


def scaled(coeff, values):
    lanes = values.shape[-1]
    if lanes != 128:
        coeff = jnp.concatenate([coeff] * (lanes // 128), axis=1)
    flat = values.reshape(-1, 8, lanes)
    return (coeff[None] * flat).reshape(values.shape)


def chebyshev(residue, degree, inverse, bound, ratio, operate, keep):
    centre, spread = chebyshev_scalars(bound, ratio)
    sigma = centre / spread
    rho = 1.0 / sigma
    direction = scaled(1.0 / centre, inverse * residue)
    total = direction
    for step in range(degree):
        if step < degree - 1 or keep:
            residue = residue - operate(direction)
        if step < degree - 1:
            rho_next = 1.0 / (2.0 * sigma - rho)
            direction = scaled(rho_next * rho, direction) + scaled(2.0 * rho_next / spread, inverse * residue)
            total = total + direction
            rho = rho_next
    return total, residue


def final_kernel(
    bounds_a, bounds_b, source_w, scale_w, mass_w, inverse_w, power_1, power_2, basis,
    spread_1w, weight_1w, inverse_1w, spread_2w, weight_2w, inverse_2w,
    fine, mid, coarse, gather_rows, spread_rows, expand, fold, unfold, stretch, result, lifted_w, answer_w,
):
    rows = scale_w.shape[1] // 2
    planes = (scale_w.shape[0] - 2 * PAD) // 2
    slab = 3 * rows
    size = planes * slab
    small = size // 4
    gz, gy = lax.axis_index("gz"), lax.axis_index("gy")
    bounds = jnp.maximum(bounds_a[...], bounds_b[...])

    centre, spread = chebyshev_scalars(bounds[0], SMOOTH_RATIO)
    sigma = centre / spread
    rho = 1.0 / sigma
    rho_next = 1.0 / (2.0 * sigma - rho)
    keep, push = rho_next * rho, 2.0 * rho_next / spread
    beta = push / centre
    gamma = 1.0 / centre + keep / centre + push
    omega = (4.0 / 3.0) / bounds[0]

    source_1 = (
        basis[0]
        - scaled(gamma + omega, basis[1])
        + scaled(beta + omega * gamma, basis[2])
        - scaled(omega * beta, basis[3])
    )
    spread_1, weight_1, inverse_1 = spread_1w[...], weight_1w[...], inverse_1w[...]
    spread_2, weight_2, inverse_2 = spread_2w[...], weight_2w[...], inverse_2w[...]

    def operate_1(values):
        product = banded_beside(mid[0, :, :size], mid[1, :, :size], spread_1 * values)
        return 2.0 * spread_1 * shifted_sum(product, planes, slab, 128) + weight_1 * values

    def operate_2(values):
        product = banded_stacked(coarse[:, : 3 * small], spread_2 * values)
        return 4.0 * spread_2 * shifted_sum(product, planes // 2, slab // 2, 128) + weight_2 * values

    omega_1 = (4.0 / 3.0) / bounds[1]
    iterate, residue = chebyshev(source_1, 2, inverse_1, bounds[1], SMOOTH_RATIO, operate_1, True)
    smoothed = residue - scaled(omega_1, operate_1(inverse_1 * residue))
    source_2 = lanes_apply(rows_apply(gather_rows[...], smoothed), fold[...])
    error_2, _ = chebyshev(source_2, COARSE_ITERS, inverse_2, bounds[2], COARSE_RATIO, operate_2, False)
    lifted = lanes_apply(error_2, unfold[...])
    lifted = dot(spread_rows[...], jnp.concatenate(split(lifted), axis=0))
    iterate = iterate + lifted - scaled(omega_1, inverse_1 * operate_1(lifted))
    residue = source_1 - operate_1(iterate)
    more, _ = chebyshev(residue, 2, inverse_1, bounds[1], SMOOTH_RATIO, operate_1, False)
    error_1 = iterate + more

    lifted_w[0:2] = jnp.zeros((2, slab, 128), F32)
    lifted_w[planes + 2 : planes + 4] = jnp.zeros((2, slab, 128), F32)
    lifted_w[2 : planes + 2] = error_1.reshape(planes, slab, 128)
    near = lifted_w[pl.ds(2 * gz, 6)].reshape(6 * slab, 128)
    wide = lanes_apply(near, stretch[...]).reshape(6, slab, LANES)
    side = jnp.concatenate([wide[plane] for plane in range(6)], axis=1)
    tall = dot(expand[...], jnp.concatenate(split(side), axis=0))
    slabs = [tall[:, plane * LANES : plane * LANES + LANES] for plane in range(6)]
    error = jnp.stack([slabs[(plane + 1) // 2] for plane in range(10)], axis=0).reshape(10, 3, 2 * rows, LANES)

    def near_own(ref, reach):
        return ref[pl.ds(4 * gz + PAD - reach, 4 + 2 * reach)]

    scale, mass, inverse = near_own(scale_w, 3), near_own(mass_w, 2), near_own(inverse_w, 2)
    source = near_own(source_w, 2)
    image = fine_operator(fine, scale, mass, error)
    iterate = inverse * (scaled(gamma, source) - scaled(beta, near_own(power_1, 2)) - scaled(omega, image)) + error[1:9]
    residue = source[1:7] - fine_operator(fine, scale[1:9], mass[1:7], iterate)
    direction = scaled(1.0 / centre, inverse[1:7] * residue)
    last = residue[1:5] - fine_operator(fine, scale[2:8], mass[2:6], direction)
    answer = iterate[2:6] + scaled(1.0 + keep, direction[1:5]) + scaled(push, inverse[2:6] * last)
    answer_w[...] = answer[:, :, :, :128]
    for comp in range(3):
        result[comp] = answer_w[:, comp, pl.ds(pl.multiple_of(8 * gy, 8), 8), :]


def swap_pairs(counts, target):
    def number(place):
        return (place[0] * counts[1] + place[1]) * counts[2] + place[2]

    places = [(x, y, z) for x in range(counts[0]) for y in range(counts[1]) for z in range(counts[2])]
    return [(number(place), number(target(*place))) for place in places]


def odd_partner(index):
    return index - 1 if index % 2 == 0 else index + 1


def on_device(right_side, stiff_scale, nodal_mass, stencil_blocks):
    counts = tuple(lax.axis_size(axis) for axis in AXES)
    gxs, gys, gzs = counts
    blocks = stencil_blocks.reshape(243)

    def send(values, target):
        return lax.ppermute(values, AXES, swap_pairs(counts, target))

    def x_second(x, y, z):
        return (x, y, z ^ 1) if x in (0, gxs - 1) else (odd_partner(x), y, z)

    rows, planes = 8 * gys, 4 * gzs
    grant = 20 if planes * rows <= 256 else 48
    slab = 3 * rows
    group = group_of(slab)
    size_1, count_1 = planes * slab // 4, planes * rows // 4
    size_2, count_2 = size_1 // 4, count_1 // 4
    (
        fine, fine_bound, mid, mid_bound, coarse, coarse_bound, coarse_diag,
        gather_rows, spread_rows, expand, fold, unfold, squeeze, stretch,
    ) = call(
        functools.partial(matrices_kernel, rows, planes),
        [
            ((2, group * 3 * slab, up128((group + 2) * slab)), BF16),
            ((group * 3 * slab, up128(3 * (group + 2) * rows)), BF16),
            ((2, 3 * size_1, up128(size_1)), BF16),
            ((3 * size_1, up128(3 * count_1)), BF16),
            ((3 * size_2, up128(3 * size_2)), BF16),
            ((3 * size_2, up128(3 * count_2)), BF16),
            ((size_2, 128), F32),
            ((size_2, size_1), BF16),
            ((size_1, 2 * size_2), BF16),
            ((slab, slab), BF16),
            ((256, 128), BF16),
            ((256, 128), BF16),
            ((2 * LANES, 128), BF16),
            ((256, LANES), BF16),
        ],
        specs=[SM],
        flops=5000000000,
        size=8000000,
        grant=grant,
    )(blocks)

    half = ((10, 8, 128), F32)
    main = jnp.concatenate([right_side.reshape(12, 8, 128), stiff_scale, nodal_mass], axis=0)
    send_a, send_b = call(pack_kernel, [half, half], grant=8)(main)
    got_b = send(send_b, x_second)
    got_a = send(send_a, lambda x, y, z: (x ^ 1, y, z))
    (wide,) = call(functools.partial(widen_kernel, gxs), [((20, 8, LANES), F32)], grant=8)(main, got_b, got_a)
    ordered = not (gys == 2 and gzs == 4)
    if ordered:
        gathered = [lax.all_gather(wide, ("gz", "gy"), tiled=False)]
    else:
        near = [
            wide,
            send(wide, lambda x, y, z: (x, y, z ^ 2)),
            send(wide, lambda x, y, z: (x, y ^ 1, z)),
            send(wide, lambda x, y, z: (x, y ^ 1, z ^ 2)),
        ]
        near[3], fine = lax.optimization_barrier((near[3], fine))
        gathered = [block[None] for block in near + [send(block, lambda x, y, z: (x, y, z ^ 1)) for block in near]]

    field = ((planes + 2 * PAD, 3, rows, LANES), F32)
    single = ((planes + 2 * PAD, rows, LANES), F32)
    source_w, scale_w, mass_w, inverse_w, *levels, bounds = call(
        functools.partial(window_kernel, gys, ordered),
        [field, single, single, field] + [((size_1, 128), F32)] * 3 + [((size_2, 128), F32)] * 3 + [((3, 8, 128), F32)],
        specs=[SM] + [VM] * (len(gathered) + 7),
        scratch=[pltpu.VMEM((2, 2, planes * rows // 2, 128), F32)],
        grant=grant,
    )(blocks, *gathered, fine_bound, mid_bound, coarse_bound, coarse_diag, gather_rows, fold, squeeze)

    step = 4
    while step < gxs:
        bounds = jnp.maximum(bounds, send(bounds, lambda x, y, z: (x ^ step, y, z)))
        step *= 2
    bounds = jnp.maximum(bounds, send(bounds, lambda x, y, z: (x ^ 1, y, z ^ 1)))
    other = send(bounds, lambda x, y, z: (x ^ 2, y, z ^ 1))
    (power_1,) = call(power_kernel, [field], flops=1000000000, size=4000000, grant=grant)(scale_w, mass_w, inverse_w, source_w, fine)
    power_2, basis = call(
        restrict_kernel,
        [field, ((4, size_1, 128), F32)],
        scratch=[pltpu.VMEM((4, 2, 2 * size_1, 128), F32)],
        flops=2000000000,
        size=8000000,
        grant=grant,
    )(scale_w, mass_w, inverse_w, source_w, power_1, fine, squeeze)
    (result,) = call(
        final_kernel,
        [(right_side.shape, F32)],
        scratch=[
            pltpu.VMEM((planes // 2 + 4, slab // 2, 128), F32),
            pltpu.VMEM((4, 3, rows, 128), F32),
        ],
        grant=grant,
    )(
        bounds, other, source_w, scale_w, mass_w, inverse_w, power_1, power_2, basis, *levels,
        fine, mid, coarse, gather_rows, spread_rows, expand, fold, unfold, stretch,
    )
    return result


def solution(mesh):
    placed = (P(None, "gz", "gy", "gx"), P("gz", "gy", "gx"), P("gz", "gy", "gx"), P())
    return jax.shard_map(
        on_device, mesh=mesh, in_specs=placed, out_specs=P(None, "gz", "gy", "gx"), check_vma=False
    )
```

```python
import functools

import jax
import jax.numpy as jnp
from jax import lax
from jax.experimental import pallas as pl
from jax.experimental.pallas import tpu as pltpu
from jax.sharding import PartitionSpec as P

AXES = ("gx", "gy", "gz")
COARSE_ITERS = 8
SMOOTH_RATIO = 20.0
COARSE_RATIO = 200.0
F32, BF16 = jnp.float32, jnp.bfloat16
VM = pl.BlockSpec(memory_space=pltpu.VMEM)
SM = pl.BlockSpec(memory_space=pltpu.SMEM)
LANES = 256
PAD = 3


def call(kernel, outs, specs=None, scratch=(), flops=1000000, size=100000, grant=None):
    params = pltpu.CompilerParams(vmem_limit_bytes=grant * 1024 * 1024) if grant else None
    outs = [jax.ShapeDtypeStruct(shape, dtype) for shape, dtype in outs]

    def run(*args):
        return pl.pallas_call(
            kernel,
            out_shape=outs,
            in_specs=specs or [VM] * len(args),
            out_specs=[VM] * len(outs),
            scratch_shapes=scratch,
            compiler_params=params,
            cost_estimate=pl.CostEstimate(flops=flops, bytes_accessed=size, transcendentals=0),
        )(*args)

    return run


def iota(shape, dim):
    return lax.broadcasted_iota(jnp.int32, shape, dim)


def ones_where(mask):
    return jnp.where(mask, 1.0, 0.0).astype(BF16)


def split(values):
    high = values.astype(BF16)
    return high, (values - high.astype(F32)).astype(BF16)


def dot(left, right):
    return jnp.dot(left, right, preferred_element_type=F32)


def lanes_apply(values, stacked):
    return dot(jnp.concatenate(split(values), axis=1), stacked)


def rows_apply(selection, values):
    width = values.shape[1]
    product = dot(selection, jnp.concatenate(split(values), axis=1))
    return product[:, :width] + product[:, width:]


def banded(matrix_high, matrix_low, values):
    high, low = split(values)
    return dot(matrix_high, high) + dot(matrix_low, high) + dot(matrix_high, low)


def banded_stacked(matrix, values):
    high, low = split(values)
    return dot(matrix, jnp.concatenate([high, high, low], axis=0))


def banded_planes(matrix, values, planes, step):
    slab = values.shape[0] // planes
    edge = jnp.zeros((slab, 128), F32)
    padded = jnp.concatenate([edge, values, edge], axis=0)
    beside = jnp.concatenate([padded[at * slab : (at + 3) * slab] for at in range(planes)], axis=1)
    high = beside.astype(BF16).astype(F32)
    stacked = jnp.concatenate([high, high, beside - high], axis=0).astype(BF16)
    product = dot(matrix[:, : 9 * slab], stacked)
    outs = []
    for at in range(planes):
        below, here, above = (
            product[part * slab : part * slab + slab, at * 128 : at * 128 + 128] for part in range(3)
        )
        outs.append(here + pltpu.roll(below, step, 1) + pltpu.roll(above, 128 - step, 1))
    return jnp.concatenate(outs, axis=0)


def paired_lanes(values):
    even = iota(values.shape, 1) % 2 == 0
    return values + jnp.where(even, pltpu.roll(values, 127, 1), pltpu.roll(values, 1, 1))


def shifted_sum(product, slabs, rows, lanes):
    parts = product.reshape(slabs, 3, rows, lanes)
    below = parts[:, 0].reshape(slabs * rows, lanes)
    above = parts[:, 2].reshape(slabs * rows, lanes)
    here = parts[:, 1].reshape(slabs * rows, lanes)
    return here + pltpu.roll(below, 1, 1) + pltpu.roll(above, lanes - 1, 1)


def group_of(slab):
    return max(1, 256 // slab - 2)


def groups(planes, most):
    sizes = []
    while planes:
        size = min(most, planes)
        if most > 2 and planes == most + 1:
            size = 2
        sizes.append(size)
        planes -= size
    return sizes


def fine_stencil(matrix, values):
    planes, rows = values.shape[0] - 2, values.shape[2]
    slab = 3 * rows
    flat = values.reshape((planes + 2) * slab, LANES)
    outs = []
    at = 0
    for size in groups(planes, group_of(slab)):
        height, depth = size * 3 * slab, (size + 2) * slab
        product = banded(
            matrix[0, :height, :depth], matrix[1, :height, :depth], flat[at * slab : at * slab + depth]
        )
        outs.append(shifted_sum(product, size, slab, LANES))
        at += size
    return jnp.concatenate(outs, axis=0).reshape(planes, 3, rows, LANES)


def panels(value_of, others, rows, width):
    column = iota((8, width), 1)
    which = column // rows
    row_in = column % rows
    result = {}
    for step_x in range(3):
        for comp in range(3):
            coeffs = []
            for step_y in range(3):
                coeff = jnp.zeros((8, width), F32)
                for plane in range(3):
                    for other in range(others):
                        value = value_of(plane * 9 + step_y * 3 + step_x, comp, other)
                        coeff = jnp.where(which == plane * others + other, value, coeff)
                coeffs.append(coeff)
            pieces = []
            for block in range(rows // 8):
                gap = row_in - (iota((8, width), 0) + block * 8)
                piece = jnp.zeros((8, width), F32)
                for step_y in range(3):
                    piece = jnp.where(gap == step_y - 1, coeffs[step_y], piece)
                pieces.append(piece)
            result[step_x, comp] = jnp.concatenate(pieces, axis=0)
    return result


def turned(value, turn):
    turn %= value.shape[1]
    return pltpu.roll(value, turn, 1) if turn else value


def parts_of(value):
    high = value.astype(BF16).astype(F32)
    return high, value - high


def stack3(value, size):
    high, low = parts_of(value)
    return (high + turned(low, size) + turned(high, 2 * size)).astype(BF16)


def up128(size):
    return -(-size // 128) * 128


def coarse_slab(few):
    return -(-3 * few // 16) * 16


def matrices_kernel(
    rows, planes, blocks, fine, fine_bound, mid, mid_bound, coarse, coarse_bound, coarse_diag,
    gather_rows, spread_rows, squeeze, stretch,
):
    def direct(offset, comp, other):
        return blocks[offset * 9 + comp * 3 + other]

    def absolute(offset, comp, other):
        at = offset * 9 + comp * 3
        return jnp.abs(blocks[at]) + jnp.abs(blocks[at + 1]) + jnp.abs(blocks[at + 2])

    slab = 3 * rows
    group = group_of(slab)
    found = panels(direct, 3, rows, fine.shape[2])
    bound = panels(absolute, 1, rows, fine_bound.shape[1])
    for plane in range(group):
        for step_x in range(3):
            start = (plane * 3 + step_x) * slab
            value = turned(jnp.concatenate([found[step_x, comp] for comp in range(3)], axis=0), plane * slab)
            high, low = split(value)
            fine[0, start : start + slab, :] = high
            fine[1, start : start + slab, :] = low
            value = turned(jnp.concatenate([bound[step_x, comp] for comp in range(3)], axis=0), plane * rows)
            fine_bound[start : start + slab, :] = stack3(value, (group + 2) * rows)

    rows, planes = rows // 2, planes // 2
    slab = 3 * rows
    found = panels(direct, 3, rows, mid.shape[1])
    whole = jnp.concatenate([found[step_x, comp] for step_x in range(3) for comp in range(3)], axis=0)
    few, half = rows // 2, planes // 2
    size = coarse_slab(few)

    def choose(out, source):
        place = out % size
        wanted = out // size * slab + place // few * rows + place % few
        return ones_where(jnp.logical_and(source == wanted, place < 3 * few))

    shape = (3 * size, 3 * slab)
    choose_rows = choose(iota(shape, 0), iota(shape, 1))
    shape = (mid.shape[1], up128(3 * size))
    choose_columns = jnp.where(iota(shape, 1) < 3 * size, choose(iota(shape, 1), iota(shape, 0)), 0.0).astype(BF16)

    def smaller(matrix):
        return dot(dot(choose_rows, matrix.astype(BF16)).astype(BF16), choose_columns)

    for target, small_target, value in ((mid, coarse, whole), (mid_bound, coarse_bound, jnp.abs(whole))):
        target[...] = stack3(value, 3 * slab)
        high, low = parts_of(value)
        high, low = smaller(high), smaller(low)
        width = small_target.shape[1]
        if width > high.shape[1]:
            more = jnp.zeros((3 * size, width - high.shape[1]), F32)
            high, low = jnp.concatenate([high, more], axis=1), jnp.concatenate([low, more], axis=1)
        small_target[...] = (high + turned(low, 3 * size) + turned(high, 6 * size)).astype(BF16)
    comp = iota((half * size, 128), 0) % size // few
    diag = [blocks[13 * 9 + 4 * at] for at in range(3)]
    coarse_diag[...] = jnp.where(comp == 0, diag[0], jnp.where(comp == 1, diag[1], diag[2]))

    def same_aggregate(small, large):
        place, inner = small % size, large % slab
        same = jnp.logical_and(small // size == large // (2 * slab), place // few == inner // rows)
        return jnp.logical_and(same, place % few == inner % rows // 2)

    shape = (half * size, planes * slab)
    gather_rows[...] = ones_where(same_aggregate(iota(shape, 0), iota(shape, 1)))
    shape = (planes * slab, 2 * half * size)
    spread_rows[...] = ones_where(same_aggregate(iota(shape, 1) % (half * size), iota(shape, 0)))
    shape = (2 * LANES, 128)
    squeeze[...] = ones_where(iota(shape, 0) % LANES // 2 == iota(shape, 1))
    shape = (256, LANES)
    stretch[...] = ones_where(iota(shape, 0) % 128 == iota(shape, 1) // 2)


def halves(planes, low):
    first, second = planes[:10], pltpu.roll(planes[10:], 64, 2)
    return jnp.where(low, second, first), jnp.where(low, first, second)


def pack_kernel(main, send_a, send_b):
    high, low = halves(main[...], iota((10, 8, 128), 2) < 64)
    even = lax.rem(lax.axis_index("gx"), 2) == 0
    send_a[...] = jnp.where(even, high, low)
    send_b[...] = jnp.where(even, low, high)


def widen_kernel(count, main, got_b, got_a, wide):
    index = lax.axis_index("gx")
    even = lax.rem(index, 2) == 0
    first, second = got_a[...], got_b[...]
    above = jnp.where(index < count - 1, jnp.where(even, first, second), 0.0)
    below = jnp.where(index > 0, jnp.where(even, second, first), 0.0)
    low = iota((10, 8, 128), 2) < 64
    wide[:, :, :128] = main[...]
    wide[:10, :, 128:] = jnp.where(low, above, below)
    wide[10:, :, 128:] = jnp.where(low, pltpu.roll(above, 64, 2), pltpu.roll(below, 64, 2))


def inverse_diagonal(scale, mass, blocks, factor):
    square = scale * scale
    parts = []
    for comp in range(3):
        diag = factor * blocks[13 * 9 + comp * 4] * square + mass
        parts.append(jnp.where(scale > 0.0, 1.0 / diag, 0.0)[:, None])
    return jnp.concatenate(parts, axis=1)


def largest(ratio, lanes):
    width = ratio.shape[1]
    flat = jnp.max(ratio.reshape(-1, 8, width), axis=0)
    own = jnp.where(iota((8, width), 1) < lanes, flat, -jnp.inf)
    return functools.reduce(jnp.maximum, [own[:, at : at + 128] for at in range(0, width, 128)])


def paired_planes(values):
    pairs = values.reshape((-1, 2) + values.shape[1:])
    return pairs[:, 0] + pairs[:, 1]


def paired_rows(held, values):
    for half in (0, 1):
        held[half] = values[:, half * 128 : half * 128 + 128]
    count = held.shape[1] // 2
    return jnp.concatenate(
        [held[half, pl.ds(0, count, stride=2)] + held[half, pl.ds(1, count, stride=2)] for half in (0, 1)], axis=1
    )


def window_kernel(
    gys, ordered, blocks, *refs
):
    (*blocks_in, fine_bound, mid_bound, coarse_bound, coarse_diag, gather_rows, squeeze,
     source_w, scale_w, mass_w, inverse_w, spread_1w, weight_1w, inverse_1w, spread_2w, weight_2w, inverse_2w, bounds, held) = refs
    planes, rows = scale_w.shape[0] - 2 * PAD, scale_w.shape[1]
    gz, gy = lax.axis_index("gz"), lax.axis_index("gy")
    for at in (0, planes + PAD):
        source_w[at : at + PAD] = jnp.zeros((PAD, 3, rows, LANES), F32)
        inverse_w[at : at + PAD] = jnp.zeros((PAD, 3, rows, LANES), F32)
        scale_w[at : at + PAD] = jnp.zeros((PAD, rows, LANES), F32)
        mass_w[at : at + PAD] = jnp.zeros((PAD, rows, LANES), F32)
    number = 0
    for ref in blocks_in:
        for block in range(ref.shape[0]):
            if ordered:
                place_z, place_y = number // gys, number % gys
            else:
                place_z = lax.bitwise_xor(gz, number // 4 + 2 * (number % 2))
                place_y = lax.bitwise_xor(gy, number % 4 // 2)
            at_z = pl.ds(PAD + 4 * place_z, 4)
            at_y = pl.ds(pl.multiple_of(8 * place_y, 8), 8)
            for comp in range(3):
                source_w[at_z, comp, at_y, :] = ref[block, comp * 4 : comp * 4 + 4]
            scale_w[at_z, at_y, :] = ref[block, 12:16]
            mass_w[at_z, at_y, :] = ref[block, 16:20]
            number += 1

    scale, mass = scale_w[PAD : PAD + planes], mass_w[PAD : PAD + planes]
    inverse = inverse_diagonal(scale, mass, blocks, 1.0)
    inverse_w[PAD : PAD + planes] = inverse
    slab = 3 * rows
    outs = []
    at = 0
    for size in groups(planes, group_of(slab)):
        near = scale_w[PAD - 1 + at : PAD + 1 + at + size].reshape((size + 2) * rows, LANES)
        if size < group_of(slab):
            near = jnp.concatenate([near, jnp.zeros(((group_of(slab) - size) * rows, LANES), F32)], axis=0)
        depth = 3 * (group_of(slab) + 2) * rows
        outs.append(shifted_sum(banded_stacked(fine_bound[: size * 3 * slab, :depth], near), size, slab, LANES))
        at += size
    total = jnp.concatenate(outs, axis=0).reshape(planes, 3, rows, LANES)
    ratio = (scale[:, None] * total + mass[:, None]) * inverse
    bounds[0] = largest(ratio.reshape(planes * slab, LANES), 128)

    rows, planes = rows // 2, planes // 2
    slab = 3 * rows
    count = planes * rows
    pairs = [
        paired_rows(held.at[at], paired_planes(values).reshape(2 * count, LANES))
        for at, values in enumerate((scale, mass))
    ]
    middle = lanes_apply(jnp.concatenate(pairs, axis=0), squeeze[...])
    scale_1 = (middle[:count] * 0.125).reshape(planes, rows, 128)
    mass_1 = middle[count:].reshape(planes, rows, 128)
    inverse_1 = inverse_diagonal(scale_1, mass_1, blocks, 2.0).reshape(planes * slab, 128)
    spread_1 = jnp.broadcast_to(scale_1[:, None], (planes, 3, rows, 128)).reshape(planes * slab, 128)
    weight_1 = jnp.broadcast_to(mass_1[:, None], (planes, 3, rows, 128)).reshape(planes * slab, 128)
    total = banded_planes(mid_bound, spread_1, planes, 1)
    bounds[1] = largest((2.0 * spread_1 * total + weight_1) * inverse_1, 64)
    spread_1w[...], weight_1w[...], inverse_1w[...] = spread_1, weight_1, inverse_1

    both = rows_apply(gather_rows[...], jnp.concatenate([spread_1, weight_1], axis=1))
    spread_2 = paired_lanes(both[:, :128]) * 0.125
    weight_2 = paired_lanes(both[:, 128:])
    inverse_2 = jnp.where(spread_2 > 0.0, 1.0 / (4.0 * coarse_diag[...] * spread_2 * spread_2 + weight_2), 0.0)
    total = banded_planes(coarse_bound, spread_2, planes // 2, 2)
    bounds[2] = largest((4.0 * spread_2 * total + weight_2) * inverse_2, 64)
    spread_2w[...], weight_2w[...], inverse_2w[...] = spread_2, weight_2, inverse_2


def fine_operator(matrix, scale, mass, values):
    total = fine_stencil(matrix, scale[:, None] * values)
    return scale[1:-1][:, None] * total + mass[:, None] * values[1:-1]


def inner_power(scale_w, mass_w, inverse_w, matrix, values):
    planes = scale_w.shape[0] - 2 * PAD
    near = slice(PAD - 1, PAD + planes + 1)
    return fine_operator(matrix, scale_w[near], mass_w[PAD : PAD + planes], inverse_w[near] * values[near])


def power_kernel(scale_w, mass_w, inverse_w, source_w, fine, power):
    planes, shape = scale_w.shape[0] - 2 * PAD, power.shape[1:]
    power[:PAD] = jnp.zeros((PAD,) + shape, F32)
    power[PAD + planes :] = jnp.zeros((PAD,) + shape, F32)
    power[PAD : PAD + planes] = inner_power(scale_w, mass_w, inverse_w, fine, source_w)


def restrict_kernel(scale_w, mass_w, inverse_w, source_w, power_1, fine, squeeze, basis, power_2, held):
    planes, rows = scale_w.shape[0] - 2 * PAD, scale_w.shape[1]
    power_kernel(scale_w, mass_w, inverse_w, power_1, fine, power_2)
    third = inner_power(scale_w, mass_w, inverse_w, fine, power_2)
    inner = slice(PAD, PAD + planes)
    size = planes // 2 * 3 * rows
    for at, values in enumerate((source_w[inner], power_1[inner], power_2[inner], third)):
        pairs = paired_rows(held.at[at], paired_planes(values).reshape(size, LANES))
        basis[at] = lanes_apply(pairs, squeeze[...])


def chebyshev_constants(ratio, degree):
    sigma = (ratio + 1.0) / (ratio - 1.0)
    rho = 1.0 / sigma
    steps = []
    for _ in range(degree - 1):
        rho_next = 1.0 / (2.0 * sigma - rho)
        steps.append((rho_next * rho, 4.0 * rho_next / (1.0 - 1.0 / ratio)))
        rho = rho_next
    return 2.0 / (1.0 + 1.0 / ratio), steps


def chebyshev(residue, degree, inverse, ratio, operate, keep):
    first, steps = chebyshev_constants(ratio, degree)
    direction = first * (inverse * residue)
    total = direction
    for hold, push in steps:
        residue = residue - operate(direction)
        direction = hold * direction + push * (inverse * residue)
        total = total + direction
    if keep:
        residue = residue - operate(direction)
    return total, residue


def scaled(coeff, values):
    lanes = values.shape[-1]
    if lanes != 128:
        coeff = jnp.concatenate([coeff] * (lanes // 128), axis=1)
    flat = values.reshape(-1, 8, lanes)
    return (coeff[None] * flat).reshape(values.shape)


def final_kernel(
    bounds_a, bounds_b, source_w, scale_w, mass_w, inverse_w, power_1, basis,
    spread_1w, weight_1w, inverse_1w, spread_2w, weight_2w, inverse_2w,
    fine, mid, coarse, gather_rows, spread_rows, stretch, result, lifted_w, doubled_w, answer_w,
):
    rows = scale_w.shape[1] // 2
    planes = (scale_w.shape[0] - 2 * PAD) // 2
    slab = 3 * rows
    gz, gy = lax.axis_index("gz"), lax.axis_index("gy")
    worst = jnp.maximum(bounds_a[...], bounds_b[...])
    inverse_bounds = [1.0 / jnp.full((8, 128), jnp.max(worst[level]), F32) for level in range(3)]
    over_0 = inverse_bounds[0]

    first, ((hold, push),) = chebyshev_constants(SMOOTH_RATIO, 2)
    beta = push * first
    gamma = first * (1.0 + hold) + push
    omega = 4.0 / 3.0
    source_1 = basis[0] - scaled(
        over_0,
        (gamma + omega) * basis[1]
        - scaled(over_0, (beta + omega * gamma) * basis[2] - scaled(over_0, (omega * beta) * basis[3])),
    )

    spread_1, weight_1 = spread_1w[...], weight_1w[...]
    spread_2, weight_2 = spread_2w[...], weight_2w[...]
    inverse_1 = scaled(inverse_bounds[1], inverse_1w[...])
    inverse_2 = scaled(inverse_bounds[2], inverse_2w[...])
    double_1, double_2 = 2.0 * spread_1, 4.0 * spread_2

    def operate_1(values):
        return double_1 * banded_planes(mid, spread_1 * values, planes, 1) + weight_1 * values

    def operate_2(values):
        return double_2 * banded_planes(coarse, spread_2 * values, planes // 2, 2) + weight_2 * values

    iterate, residue = chebyshev(source_1, 2, inverse_1, SMOOTH_RATIO, operate_1, True)
    smoothed = residue - omega * operate_1(inverse_1 * residue)
    source_2 = paired_lanes(rows_apply(gather_rows[...], smoothed))
    error_2, _ = chebyshev(source_2, COARSE_ITERS, inverse_2, COARSE_RATIO, operate_2, False)
    lifted = dot(spread_rows[...], jnp.concatenate(split(error_2), axis=0))
    iterate = iterate + lifted - omega * (inverse_1 * operate_1(lifted))
    residue = source_1 - operate_1(iterate)
    more, _ = chebyshev(residue, 2, inverse_1, SMOOTH_RATIO, operate_1, False)
    error_1 = iterate + more

    lifted_w[0:2] = jnp.zeros((2, slab, 128), F32)
    lifted_w[planes + 2 : planes + 4] = jnp.zeros((2, slab, 128), F32)
    lifted_w[2 : planes + 2] = error_1.reshape(planes, slab, 128)
    near = lifted_w[pl.ds(2 * gz, 6)].reshape(6 * slab, 128)
    wide = lanes_apply(near, stretch[...])
    for half in (0, 1):
        for odd in (0, 1):
            doubled_w[half, pl.ds(odd, 6 * slab, stride=2)] = wide[:, half * 128 : half * 128 + 128]
    slabs = jnp.concatenate([doubled_w[0], doubled_w[1]], axis=1).reshape(6, 3, 2 * rows, LANES)
    error = jnp.stack([slabs[(plane + 1) // 2] for plane in range(10)], axis=0)

    def near_own(ref, reach):
        return ref[pl.ds(4 * gz + PAD - reach, 4 + 2 * reach)]

    scale, mass = near_own(scale_w, 3), near_own(mass_w, 2)
    inverse = scaled(over_0, near_own(inverse_w, 2))
    source = near_own(source_w, 2)
    before = gamma * source - scaled(over_0, beta * near_own(power_1, 2))
    image = fine_operator(fine, scale, mass, error)
    iterate = inverse * (before - omega * image) + error[1:9]
    residue = source[1:7] - fine_operator(fine, scale[1:9], mass[1:7], iterate)
    direction = first * (inverse[1:7] * residue)
    last = residue[1:5] - fine_operator(fine, scale[2:8], mass[2:6], direction)
    answer = iterate[2:6] + (1.0 + hold) * direction[1:5] + push * (inverse[2:6] * last)
    answer_w[...] = answer[:, :, :, :128]
    for comp in range(3):
        result[comp] = answer_w[:, comp, pl.ds(pl.multiple_of(8 * gy, 8), 8), :]


def swap_pairs(counts, target):
    def number(place):
        return (place[0] * counts[1] + place[1]) * counts[2] + place[2]

    places = [(x, y, z) for x in range(counts[0]) for y in range(counts[1]) for z in range(counts[2])]
    return [(number(place), number(target(*place))) for place in places]


def odd_partner(index):
    return index - 1 if index % 2 == 0 else index + 1


def on_device(right_side, stiff_scale, nodal_mass, stencil_blocks):
    counts = tuple(lax.axis_size(axis) for axis in AXES)
    gxs, gys, gzs = counts
    blocks = stencil_blocks.reshape(243)

    def send(values, target):
        return lax.ppermute(values, AXES, swap_pairs(counts, target))

    def x_second(x, y, z):
        return (x, y, z ^ 1) if x in (0, gxs - 1) else (odd_partner(x), y, z)

    rows, planes = 8 * gys, 4 * gzs
    grant = 20 if planes * rows <= 256 else 48
    slab = 3 * rows
    group = group_of(slab)
    size_1 = planes * slab // 4
    size = coarse_slab(rows // 4)
    size_2 = planes // 4 * size
    (
        fine, fine_bound, mid, mid_bound, coarse, coarse_bound, coarse_diag, gather_rows, spread_rows, squeeze, stretch,
    ) = call(
        functools.partial(matrices_kernel, rows, planes),
        [
            ((2, group * 3 * slab, up128((group + 2) * slab)), BF16),
            ((group * 3 * slab, up128(3 * (group + 2) * rows)), BF16),
            ((3 * slab // 2, up128(9 * slab // 2)), BF16),
            ((3 * slab // 2, up128(9 * slab // 2)), BF16),
            ((3 * size, up128(9 * size)), BF16),
            ((3 * size, up128(9 * size)), BF16),
            ((size_2, 128), F32),
            ((size_2, size_1), BF16),
            ((size_1, 2 * size_2), BF16),
            ((2 * LANES, 128), BF16),
            ((256, LANES), BF16),
        ],
        specs=[SM],
        flops=5000000000,
        size=8000000,
        grant=grant,
    )(blocks)

    half = ((10, 8, 128), F32)
    main = jnp.concatenate([right_side.reshape(12, 8, 128), stiff_scale, nodal_mass], axis=0)
    send_a, send_b = call(pack_kernel, [half, half], grant=8)(main)
    got_b = send(send_b, x_second)
    got_a = send(send_a, lambda x, y, z: (x ^ 1, y, z))
    (wide,) = call(functools.partial(widen_kernel, gxs), [((20, 8, LANES), F32)], grant=8)(main, got_b, got_a)
    ordered = not (gys == 2 and gzs == 4)
    if ordered:
        gathered = [lax.all_gather(wide, ("gz", "gy"), tiled=False)]
    else:
        near = [
            wide,
            send(wide, lambda x, y, z: (x, y, z ^ 2)),
            send(wide, lambda x, y, z: (x, y ^ 1, z)),
            send(wide, lambda x, y, z: (x, y ^ 1, z ^ 2)),
        ]
        near[3], fine = lax.optimization_barrier((near[3], fine))
        gathered = [block[None] for block in near + [send(block, lambda x, y, z: (x, y, z ^ 1)) for block in near]]

    field = ((planes + 2 * PAD, 3, rows, LANES), F32)
    single = ((planes + 2 * PAD, rows, LANES), F32)
    source_w, scale_w, mass_w, inverse_w, *levels, bounds = call(
        functools.partial(window_kernel, gys, ordered),
        [field, single, single, field] + [((size_1, 128), F32)] * 3 + [((size_2, 128), F32)] * 3 + [((3, 8, 128), F32)],
        specs=[SM] + [VM] * (len(gathered) + 6),
        scratch=[pltpu.VMEM((2, 2, planes * rows // 2, 128), F32)],
        grant=grant,
    )(blocks, *gathered, fine_bound, mid_bound, coarse_bound, coarse_diag, gather_rows, squeeze)

    step = 4
    while step < gxs:
        bounds = jnp.maximum(bounds, send(bounds, lambda x, y, z: (x ^ step, y, z)))
        step *= 2
    bounds = jnp.maximum(bounds, send(bounds, lambda x, y, z: (x ^ 1, y, z ^ 1)))
    other = send(bounds, lambda x, y, z: (x ^ 2, y, z ^ 1))
    (power_1,) = call(power_kernel, [field], flops=1000000000, size=4000000, grant=grant)(scale_w, mass_w, inverse_w, source_w, fine)
    (basis,) = call(
        restrict_kernel,
        [((4, size_1, 128), F32)],
        scratch=[pltpu.VMEM(*field), pltpu.VMEM((4, 2, 2 * size_1, 128), F32)],
        flops=2000000000,
        size=8000000,
        grant=grant,
    )(scale_w, mass_w, inverse_w, source_w, power_1, fine, squeeze)
    (result,) = call(
        final_kernel,
        [(right_side.shape, F32)],
        scratch=[
            pltpu.VMEM((planes // 2 + 4, slab // 2, 128), F32),
            pltpu.VMEM((2, 6 * slab, 128), F32),
            pltpu.VMEM((4, 3, rows, 128), F32),
        ],
        grant=grant,
    )(
        bounds, other, source_w, scale_w, mass_w, inverse_w, power_1, basis, *levels,
        fine, mid, coarse, gather_rows, spread_rows, stretch,
    )
    return result


def solution(mesh):
    placed = (P(None, "gz", "gy", "gx"), P("gz", "gy", "gx"), P("gz", "gy", "gx"), P())
    return jax.shard_map(
        on_device, mesh=mesh, in_specs=placed, out_specs=P(None, "gz", "gy", "gx"), check_vma=False
    )
```

```python
import functools

import jax
import jax.numpy as jnp
from jax import lax
from jax.experimental import pallas as pl
from jax.experimental.pallas import tpu as pltpu
from jax.sharding import PartitionSpec as P

AXES = ("gx", "gy", "gz")
COARSE_ITERS = 8
SMOOTH_RATIO = 20.0
COARSE_RATIO = 200.0
F32, BF16 = jnp.float32, jnp.bfloat16
VM = pl.BlockSpec(memory_space=pltpu.VMEM)
SM = pl.BlockSpec(memory_space=pltpu.SMEM)
LANES = 256
PAD = 3


def call(kernel, outs, specs=None, scratch=(), flops=1000000, size=100000, grant=None):
    params = pltpu.CompilerParams(vmem_limit_bytes=grant * 1024 * 1024) if grant else None
    outs = [jax.ShapeDtypeStruct(shape, dtype) for shape, dtype in outs]

    def run(*args):
        return pl.pallas_call(
            kernel,
            out_shape=outs,
            in_specs=specs or [VM] * len(args),
            out_specs=[VM] * len(outs),
            scratch_shapes=scratch,
            compiler_params=params,
            cost_estimate=pl.CostEstimate(flops=flops, bytes_accessed=size, transcendentals=0),
        )(*args)

    return run


def iota(shape, dim):
    return lax.broadcasted_iota(jnp.int32, shape, dim)


def ones_where(mask):
    return jnp.where(mask, 1.0, 0.0).astype(BF16)


def split(values):
    high = values.astype(BF16)
    return high, (values - high.astype(F32)).astype(BF16)


def dot(left, right):
    return jnp.dot(left, right, preferred_element_type=F32)


def lanes_apply(values, stacked):
    return dot(jnp.concatenate(split(values), axis=1), stacked)


def rows_apply(selection, values):
    width = values.shape[1]
    product = dot(selection, jnp.concatenate(split(values), axis=1))
    return product[:, :width] + product[:, width:]


def banded_stacked(matrix, values):
    high, low = split(values)
    return dot(matrix, jnp.concatenate([high, high, low], axis=0))


def banded_planes(matrix, values, planes, step):
    slab = values.shape[0] // planes
    edge = jnp.zeros((slab, 128), F32)
    padded = jnp.concatenate([edge, values, edge], axis=0)
    beside = jnp.concatenate([padded[at * slab : (at + 3) * slab] for at in range(planes)], axis=1)
    high = beside.astype(BF16).astype(F32)
    stacked = jnp.concatenate([high, high, beside - high], axis=0).astype(BF16)
    product = dot(matrix[:, : 9 * slab], stacked)
    outs = []
    for at in range(planes):
        below, here, above = (
            product[part * slab : part * slab + slab, at * 128 : at * 128 + 128] for part in range(3)
        )
        outs.append(here + pltpu.roll(below, step, 1) + pltpu.roll(above, 128 - step, 1))
    return jnp.concatenate(outs, axis=0)


def paired_lanes(values):
    even = iota(values.shape, 1) % 2 == 0
    return values + jnp.where(even, pltpu.roll(values, 127, 1), pltpu.roll(values, 1, 1))


def shifted_sum(product, slabs, rows, lanes):
    parts = product.reshape(slabs, 3, rows, lanes)
    below = parts[:, 0].reshape(slabs * rows, lanes)
    above = parts[:, 2].reshape(slabs * rows, lanes)
    here = parts[:, 1].reshape(slabs * rows, lanes)
    return here + pltpu.roll(below, 1, 1) + pltpu.roll(above, lanes - 1, 1)


def group_of(slab):
    return max(1, 256 // slab - 2)


def groups(planes, most):
    sizes = []
    while planes:
        size = min(most, planes)
        if most > 2 and planes == most + 1:
            size = 2
        sizes.append(size)
        planes -= size
    return sizes


def fine_operator(matrix, scale_of, mass_of, weighted_of, value_of, planes, rows, finish):
    slab = 3 * rows
    parts = {}
    for plane in range(planes):
        near = range(plane - 1, plane + 2)
        for i in near:
            if i not in parts:
                parts[i] = split(weighted_of(i).reshape(slab, LANES))
        high = [parts[i][0] for i in near]
        low = [parts[i][1] for i in near]
        product = dot(matrix[:, : 9 * slab], jnp.concatenate(high + high + low, axis=0))
        total = shifted_sum(product, 1, slab, LANES).reshape(3, rows, LANES)
        finish(plane, scale_of(plane)[None] * total + mass_of(plane)[None] * value_of(plane))


def panels(value_of, others, rows, width):
    column = iota((8, width), 1)
    which = column // rows
    row_in = column % rows
    result = {}
    for step_x in range(3):
        for comp in range(3):
            coeffs = []
            for step_y in range(3):
                coeff = jnp.zeros((8, width), F32)
                for plane in range(3):
                    for other in range(others):
                        value = value_of(plane * 9 + step_y * 3 + step_x, comp, other)
                        coeff = jnp.where(which == plane * others + other, value, coeff)
                coeffs.append(coeff)
            pieces = []
            for block in range(rows // 8):
                gap = row_in - (iota((8, width), 0) + block * 8)
                piece = jnp.zeros((8, width), F32)
                for step_y in range(3):
                    piece = jnp.where(gap == step_y - 1, coeffs[step_y], piece)
                pieces.append(piece)
            result[step_x, comp] = jnp.concatenate(pieces, axis=0)
    return result


def turned(value, turn):
    turn %= value.shape[1]
    return pltpu.roll(value, turn, 1) if turn else value


def parts_of(value):
    high = value.astype(BF16).astype(F32)
    return high, value - high


def stack3(value, size):
    high, low = parts_of(value)
    return (high + turned(low, size) + turned(high, 2 * size)).astype(BF16)


def up128(size):
    return -(-size // 128) * 128


def coarse_slab(few):
    return -(-3 * few // 16) * 16


def matrices_kernel(
    rows, planes, blocks, fine, fine_bound, mid, mid_bound, coarse, coarse_bound, coarse_diag,
    gather_rows, spread_rows, squeeze, stretch,
):
    def direct(offset, comp, other):
        return blocks[offset * 9 + comp * 3 + other]

    def absolute(offset, comp, other):
        at = offset * 9 + comp * 3
        return jnp.abs(blocks[at]) + jnp.abs(blocks[at + 1]) + jnp.abs(blocks[at + 2])

    slab = 3 * rows
    group = group_of(slab)
    width = up128(3 * slab)
    found = panels(direct, 3, rows, width)
    value = jnp.concatenate([found[step_x, comp] for step_x in range(3) for comp in range(3)], axis=0)
    if fine.shape[1] > width:
        value = jnp.concatenate([value, jnp.zeros((3 * slab, fine.shape[1] - width), F32)], axis=1)
    fine[...] = stack3(value, 3 * slab)
    bound = panels(absolute, 1, rows, fine_bound.shape[1])
    for plane in range(group):
        for step_x in range(3):
            start = (plane * 3 + step_x) * slab
            value = turned(jnp.concatenate([bound[step_x, comp] for comp in range(3)], axis=0), plane * rows)
            fine_bound[start : start + slab, :] = stack3(value, (group + 2) * rows)

    rows, planes = rows // 2, planes // 2
    slab = 3 * rows
    found = panels(direct, 3, rows, mid.shape[1])
    whole = jnp.concatenate([found[step_x, comp] for step_x in range(3) for comp in range(3)], axis=0)
    few, half = rows // 2, planes // 2
    size = coarse_slab(few)

    def choose(out, source):
        place = out % size
        wanted = out // size * slab + place // few * rows + place % few
        return ones_where(jnp.logical_and(source == wanted, place < 3 * few))

    shape = (3 * size, 3 * slab)
    choose_rows = choose(iota(shape, 0), iota(shape, 1))
    shape = (mid.shape[1], up128(3 * size))
    choose_columns = jnp.where(iota(shape, 1) < 3 * size, choose(iota(shape, 1), iota(shape, 0)), 0.0).astype(BF16)

    def smaller(matrix):
        return dot(dot(choose_rows, matrix.astype(BF16)).astype(BF16), choose_columns)

    for target, small_target, value in ((mid, coarse, whole), (mid_bound, coarse_bound, jnp.abs(whole))):
        target[...] = stack3(value, 3 * slab)
        high, low = parts_of(value)
        high, low = smaller(high), smaller(low)
        width = small_target.shape[1]
        if width > high.shape[1]:
            more = jnp.zeros((3 * size, width - high.shape[1]), F32)
            high, low = jnp.concatenate([high, more], axis=1), jnp.concatenate([low, more], axis=1)
        small_target[...] = (high + turned(low, 3 * size) + turned(high, 6 * size)).astype(BF16)
    comp = iota((half * size, 128), 0) % size // few
    diag = [blocks[13 * 9 + 4 * at] for at in range(3)]
    coarse_diag[...] = jnp.where(comp == 0, diag[0], jnp.where(comp == 1, diag[1], diag[2]))

    def same_aggregate(small, large):
        place, inner = small % size, large % slab
        same = jnp.logical_and(small // size == large // (2 * slab), place // few == inner // rows)
        return jnp.logical_and(same, place % few == inner % rows // 2)

    shape = (half * size, planes * slab)
    gather_rows[...] = ones_where(same_aggregate(iota(shape, 0), iota(shape, 1)))
    shape = (planes * slab, 2 * half * size)
    spread_rows[...] = ones_where(same_aggregate(iota(shape, 1) % (half * size), iota(shape, 0)))
    shape = (2 * LANES, 128)
    squeeze[...] = ones_where(iota(shape, 0) % LANES // 2 == iota(shape, 1))
    shape = (256, LANES)
    stretch[...] = ones_where(iota(shape, 0) % 128 == iota(shape, 1) // 2)


def halves(planes, low):
    first, second = planes[:10], pltpu.roll(planes[10:], 64, 2)
    return jnp.where(low, second, first), jnp.where(low, first, second)


def pack_kernel(main, send_a, send_b):
    high, low = halves(main[...], iota((10, 8, 128), 2) < 64)
    even = lax.rem(lax.axis_index("gx"), 2) == 0
    send_a[...] = jnp.where(even, high, low)
    send_b[...] = jnp.where(even, low, high)


def widen_kernel(count, main, got_b, got_a, wide):
    index = lax.axis_index("gx")
    even = lax.rem(index, 2) == 0
    first, second = got_a[...], got_b[...]
    above = jnp.where(index < count - 1, jnp.where(even, first, second), 0.0)
    below = jnp.where(index > 0, jnp.where(even, second, first), 0.0)
    low = iota((10, 8, 128), 2) < 64
    wide[:, :, :128] = main[...]
    wide[:10, :, 128:] = jnp.where(low, above, below)
    wide[10:, :, 128:] = jnp.where(low, pltpu.roll(above, 64, 2), pltpu.roll(below, 64, 2))


def inverse_diagonal(scale, mass, blocks, factor):
    square = scale * scale
    parts = []
    for comp in range(3):
        diag = factor * blocks[13 * 9 + comp * 4] * square + mass
        parts.append(jnp.where(scale > 0.0, 1.0 / diag, 0.0)[:, None])
    return jnp.concatenate(parts, axis=1)


def largest(ratio, lanes):
    width = ratio.shape[1]
    flat = jnp.max(ratio.reshape(-1, 8, width), axis=0)
    own = jnp.where(iota((8, width), 1) < lanes, flat, -jnp.inf)
    return functools.reduce(jnp.maximum, [own[:, at : at + 128] for at in range(0, width, 128)])


def paired_planes(values):
    pairs = values.reshape((-1, 2) + values.shape[1:])
    return pairs[:, 0] + pairs[:, 1]


def paired_rows(held, values):
    for half in (0, 1):
        held[half] = values[:, half * 128 : half * 128 + 128]
    count = held.shape[1] // 2
    return jnp.concatenate(
        [held[half, pl.ds(0, count, stride=2)] + held[half, pl.ds(1, count, stride=2)] for half in (0, 1)], axis=1
    )


def window_kernel(
    gys, ordered, blocks, *refs
):
    (*blocks_in, fine_bound, mid_bound, coarse_bound, coarse_diag, gather_rows, squeeze,
     source_w, scale_w, mass_w, inverse_w, spread_1w, weight_1w, inverse_1w, spread_2w, weight_2w, inverse_2w, bounds, held) = refs
    planes, rows = scale_w.shape[0] - 2 * PAD, scale_w.shape[1]
    gz, gy = lax.axis_index("gz"), lax.axis_index("gy")
    for at in (0, planes + PAD):
        source_w[at : at + PAD] = jnp.zeros((PAD, 3, rows, LANES), F32)
        inverse_w[at : at + PAD] = jnp.zeros((PAD, 3, rows, LANES), F32)
        scale_w[at : at + PAD] = jnp.zeros((PAD, rows, LANES), F32)
        mass_w[at : at + PAD] = jnp.zeros((PAD, rows, LANES), F32)
    number = 0
    for ref in blocks_in:
        for block in range(ref.shape[0]):
            if ordered:
                place_z, place_y = number // gys, number % gys
            else:
                place_z = lax.bitwise_xor(gz, number // 4 + 2 * (number % 2))
                place_y = lax.bitwise_xor(gy, number % 4 // 2)
            at_z = pl.ds(PAD + 4 * place_z, 4)
            at_y = pl.ds(pl.multiple_of(8 * place_y, 8), 8)
            for comp in range(3):
                source_w[at_z, comp, at_y, :] = ref[block, comp * 4 : comp * 4 + 4]
            scale_w[at_z, at_y, :] = ref[block, 12:16]
            mass_w[at_z, at_y, :] = ref[block, 16:20]
            number += 1

    scale, mass = scale_w[PAD : PAD + planes], mass_w[PAD : PAD + planes]
    inverse = inverse_diagonal(scale, mass, blocks, 1.0)
    inverse_w[PAD : PAD + planes] = inverse
    slab = 3 * rows
    outs = []
    at = 0
    for size in groups(planes, group_of(slab)):
        near = scale_w[PAD - 1 + at : PAD + 1 + at + size].reshape((size + 2) * rows, LANES)
        if size < group_of(slab):
            near = jnp.concatenate([near, jnp.zeros(((group_of(slab) - size) * rows, LANES), F32)], axis=0)
        depth = 3 * (group_of(slab) + 2) * rows
        outs.append(shifted_sum(banded_stacked(fine_bound[: size * 3 * slab, :depth], near), size, slab, LANES))
        at += size
    total = jnp.concatenate(outs, axis=0).reshape(planes, 3, rows, LANES)
    ratio = (scale[:, None] * total + mass[:, None]) * inverse
    bounds[0] = largest(ratio.reshape(planes * slab, LANES), 128)

    rows, planes = rows // 2, planes // 2
    slab = 3 * rows
    count = planes * rows
    pairs = [
        paired_rows(held.at[at], paired_planes(values).reshape(2 * count, LANES))
        for at, values in enumerate((scale, mass))
    ]
    middle = lanes_apply(jnp.concatenate(pairs, axis=0), squeeze[...])
    scale_1 = (middle[:count] * 0.125).reshape(planes, rows, 128)
    mass_1 = middle[count:].reshape(planes, rows, 128)
    inverse_1 = inverse_diagonal(scale_1, mass_1, blocks, 2.0).reshape(planes * slab, 128)
    spread_1 = jnp.broadcast_to(scale_1[:, None], (planes, 3, rows, 128)).reshape(planes * slab, 128)
    weight_1 = jnp.broadcast_to(mass_1[:, None], (planes, 3, rows, 128)).reshape(planes * slab, 128)
    total = banded_planes(mid_bound, spread_1, planes, 1)
    bounds[1] = largest((2.0 * spread_1 * total + weight_1) * inverse_1, 64)
    spread_1w[...], weight_1w[...], inverse_1w[...] = spread_1, weight_1, inverse_1

    both = rows_apply(gather_rows[...], jnp.concatenate([spread_1, weight_1], axis=1))
    spread_2 = paired_lanes(both[:, :128]) * 0.125
    weight_2 = paired_lanes(both[:, 128:])
    inverse_2 = jnp.where(spread_2 > 0.0, 1.0 / (4.0 * coarse_diag[...] * spread_2 * spread_2 + weight_2), 0.0)
    total = banded_planes(coarse_bound, spread_2, planes // 2, 2)
    bounds[2] = largest((4.0 * spread_2 * total + weight_2) * inverse_2, 64)
    spread_2w[...], weight_2w[...], inverse_2w[...] = spread_2, weight_2, inverse_2


def inner_power(scale_w, mass_w, inverse_w, matrix, values, finish):
    planes, rows = scale_w.shape[0] - 2 * PAD, scale_w.shape[1]
    fine_operator(
        matrix,
        lambda i: scale_w[PAD + i],
        lambda i: mass_w[PAD + i],
        lambda i: scale_w[PAD + i][None] * (inverse_w[PAD + i] * values[PAD + i]),
        lambda i: inverse_w[PAD + i] * values[PAD + i],
        planes,
        rows,
        finish,
    )


def power_kernel(scale_w, mass_w, inverse_w, source_w, fine, power):
    planes, shape = scale_w.shape[0] - 2 * PAD, power.shape[1:]
    power[:PAD] = jnp.zeros((PAD,) + shape, F32)
    power[PAD + planes :] = jnp.zeros((PAD,) + shape, F32)

    def finish(at, values):
        power[PAD + at] = values

    inner_power(scale_w, mass_w, inverse_w, fine, source_w, finish)


def restrict_kernel(scale_w, mass_w, inverse_w, source_w, power_1, fine, squeeze, basis, power_2, held):
    planes, rows = scale_w.shape[0] - 2 * PAD, scale_w.shape[1]
    power_kernel(scale_w, mass_w, inverse_w, power_1, fine, power_2)
    third = []
    inner_power(scale_w, mass_w, inverse_w, fine, power_2, lambda at, values: third.append(values))
    third = jnp.stack(third, axis=0)
    inner = slice(PAD, PAD + planes)
    size = planes // 2 * 3 * rows
    for at, values in enumerate((source_w[inner], power_1[inner], power_2[inner], third)):
        pairs = paired_rows(held.at[at], paired_planes(values).reshape(size, LANES))
        basis[at] = lanes_apply(pairs, squeeze[...])


def chebyshev_constants(ratio, degree):
    sigma = (ratio + 1.0) / (ratio - 1.0)
    rho = 1.0 / sigma
    steps = []
    for _ in range(degree - 1):
        rho_next = 1.0 / (2.0 * sigma - rho)
        steps.append((rho_next * rho, 4.0 * rho_next / (1.0 - 1.0 / ratio)))
        rho = rho_next
    return 2.0 / (1.0 + 1.0 / ratio), steps


def chebyshev(residue, degree, inverse, ratio, operate, keep):
    first, steps = chebyshev_constants(ratio, degree)
    direction = first * (inverse * residue)
    total = direction
    for hold, push in steps:
        residue = residue - operate(direction)
        direction = hold * direction + push * (inverse * residue)
        total = total + direction
    if keep:
        residue = residue - operate(direction)
    return total, residue


def scaled(coeff, values):
    lanes = values.shape[-1]
    if lanes != 128:
        coeff = jnp.concatenate([coeff] * (lanes // 128), axis=1)
    flat = values.reshape(-1, 8, lanes)
    return (coeff[None] * flat).reshape(values.shape)


def final_kernel(
    bounds_a, bounds_b, source_w, scale_w, mass_w, inverse_w, power_1, basis,
    spread_1w, weight_1w, inverse_1w, spread_2w, weight_2w, inverse_2w,
    fine, mid, coarse, gather_rows, spread_rows, stretch, result, lifted_w, doubled_w, answer_w,
):
    rows = scale_w.shape[1] // 2
    planes = (scale_w.shape[0] - 2 * PAD) // 2
    slab = 3 * rows
    gz, gy = lax.axis_index("gz"), lax.axis_index("gy")
    worst = jnp.maximum(bounds_a[...], bounds_b[...])
    inverse_bounds = [1.0 / jnp.full((8, 128), jnp.max(worst[level]), F32) for level in range(3)]
    over_0 = inverse_bounds[0]

    first, ((hold, push),) = chebyshev_constants(SMOOTH_RATIO, 2)
    beta = push * first
    gamma = first * (1.0 + hold) + push
    omega = 4.0 / 3.0
    source_1 = basis[0] - scaled(
        over_0,
        (gamma + omega) * basis[1]
        - scaled(over_0, (beta + omega * gamma) * basis[2] - scaled(over_0, (omega * beta) * basis[3])),
    )

    spread_1, weight_1 = spread_1w[...], weight_1w[...]
    spread_2, weight_2 = spread_2w[...], weight_2w[...]
    inverse_1 = scaled(inverse_bounds[1], inverse_1w[...])
    inverse_2 = scaled(inverse_bounds[2], inverse_2w[...])
    double_1, double_2 = 2.0 * spread_1, 4.0 * spread_2

    def operate_1(values):
        return double_1 * banded_planes(mid, spread_1 * values, planes, 1) + weight_1 * values

    def operate_2(values):
        return double_2 * banded_planes(coarse, spread_2 * values, planes // 2, 2) + weight_2 * values

    iterate, residue = chebyshev(source_1, 2, inverse_1, SMOOTH_RATIO, operate_1, True)
    smoothed = residue - omega * operate_1(inverse_1 * residue)
    source_2 = paired_lanes(rows_apply(gather_rows[...], smoothed))
    error_2, _ = chebyshev(source_2, COARSE_ITERS, inverse_2, COARSE_RATIO, operate_2, False)
    lifted = dot(spread_rows[...], jnp.concatenate(split(error_2), axis=0))
    iterate = iterate + lifted - omega * (inverse_1 * operate_1(lifted))
    residue = source_1 - operate_1(iterate)
    more, _ = chebyshev(residue, 2, inverse_1, SMOOTH_RATIO, operate_1, False)
    error_1 = iterate + more

    lifted_w[0:2] = jnp.zeros((2, slab, 128), F32)
    lifted_w[planes + 2 : planes + 4] = jnp.zeros((2, slab, 128), F32)
    lifted_w[2 : planes + 2] = error_1.reshape(planes, slab, 128)
    near = lifted_w[pl.ds(2 * gz, 6)].reshape(6 * slab, 128)
    wide = lanes_apply(near, stretch[...])
    for half in (0, 1):
        for odd in (0, 1):
            doubled_w[half, pl.ds(odd, 6 * slab, stride=2)] = wide[:, half * 128 : half * 128 + 128]
    slabs = jnp.concatenate([doubled_w[0], doubled_w[1]], axis=1).reshape(6, 3, 2 * rows, LANES)
    error = jnp.stack([slabs[(plane + 1) // 2] for plane in range(10)], axis=0)

    def near_own(ref, reach):
        return ref[pl.ds(4 * gz + PAD - reach, 4 + 2 * reach)]

    scale, mass = near_own(scale_w, 3), near_own(mass_w, 2)
    inverse = scaled(over_0, near_own(inverse_w, 2))
    source = near_own(source_w, 2)
    before = gamma * source - scaled(over_0, beta * near_own(power_1, 2))

    def apply(values, edge):
        outs = []
        fine_operator(
            fine,
            lambda i: scale[i + 4 - edge],
            lambda i: mass[i + 3 - edge],
            lambda i: scale[i + 4 - edge][None] * values[i + 1],
            lambda i: values[i + 1],
            2 + 2 * edge,
            2 * rows,
            lambda at, result: outs.append(result),
        )
        return jnp.stack(outs, axis=0)

    image = apply(error, 3)
    iterate = inverse * (before - omega * image) + error[1:9]
    residue = source[1:7] - apply(iterate, 2)
    direction = first * (inverse[1:7] * residue)
    last = residue[1:5] - apply(direction, 1)
    answer = iterate[2:6] + (1.0 + hold) * direction[1:5] + push * (inverse[2:6] * last)
    answer_w[...] = answer[:, :, :, :128]
    for comp in range(3):
        result[comp] = answer_w[:, comp, pl.ds(pl.multiple_of(8 * gy, 8), 8), :]


def swap_pairs(counts, target):
    def number(place):
        return (place[0] * counts[1] + place[1]) * counts[2] + place[2]

    places = [(x, y, z) for x in range(counts[0]) for y in range(counts[1]) for z in range(counts[2])]
    return [(number(place), number(target(*place))) for place in places]


def odd_partner(index):
    return index - 1 if index % 2 == 0 else index + 1


def on_device(right_side, stiff_scale, nodal_mass, stencil_blocks):
    counts = tuple(lax.axis_size(axis) for axis in AXES)
    gxs, gys, gzs = counts
    blocks = stencil_blocks.reshape(243)

    def send(values, target):
        return lax.ppermute(values, AXES, swap_pairs(counts, target))

    def x_second(x, y, z):
        return (x, y, z ^ 1) if x in (0, gxs - 1) else (odd_partner(x), y, z)

    rows, planes = 8 * gys, 4 * gzs
    grant = 20 if planes * rows <= 256 else 48
    slab = 3 * rows
    group = group_of(slab)
    size_1 = planes * slab // 4
    size = coarse_slab(rows // 4)
    size_2 = planes // 4 * size
    (
        fine, fine_bound, mid, mid_bound, coarse, coarse_bound, coarse_diag, gather_rows, spread_rows, squeeze, stretch,
    ) = call(
        functools.partial(matrices_kernel, rows, planes),
        [
            ((3 * slab, up128(9 * slab)), BF16),
            ((group * 3 * slab, up128(3 * (group + 2) * rows)), BF16),
            ((3 * slab // 2, up128(9 * slab // 2)), BF16),
            ((3 * slab // 2, up128(9 * slab // 2)), BF16),
            ((3 * size, up128(9 * size)), BF16),
            ((3 * size, up128(9 * size)), BF16),
            ((size_2, 128), F32),
            ((size_2, size_1), BF16),
            ((size_1, 2 * size_2), BF16),
            ((2 * LANES, 128), BF16),
            ((256, LANES), BF16),
        ],
        specs=[SM],
        flops=5000000000,
        size=8000000,
        grant=grant,
    )(blocks)

    half = ((10, 8, 128), F32)
    main = jnp.concatenate([right_side.reshape(12, 8, 128), stiff_scale, nodal_mass], axis=0)
    send_a, send_b = call(pack_kernel, [half, half], grant=8)(main)
    got_b = send(send_b, x_second)
    got_a = send(send_a, lambda x, y, z: (x ^ 1, y, z))
    (wide,) = call(functools.partial(widen_kernel, gxs), [((20, 8, LANES), F32)], grant=8)(main, got_b, got_a)
    ordered = not (gys == 2 and gzs == 4)
    if ordered:
        gathered = [lax.all_gather(wide, ("gz", "gy"), tiled=False)]
    else:
        near = [
            wide,
            send(wide, lambda x, y, z: (x, y, z ^ 2)),
            send(wide, lambda x, y, z: (x, y ^ 1, z)),
            send(wide, lambda x, y, z: (x, y ^ 1, z ^ 2)),
        ]
        near[3], fine = lax.optimization_barrier((near[3], fine))
        gathered = [block[None] for block in near + [send(block, lambda x, y, z: (x, y, z ^ 1)) for block in near]]

    field = ((planes + 2 * PAD, 3, rows, LANES), F32)
    single = ((planes + 2 * PAD, rows, LANES), F32)
    source_w, scale_w, mass_w, inverse_w, *levels, bounds = call(
        functools.partial(window_kernel, gys, ordered),
        [field, single, single, field] + [((size_1, 128), F32)] * 3 + [((size_2, 128), F32)] * 3 + [((3, 8, 128), F32)],
        specs=[SM] + [VM] * (len(gathered) + 6),
        scratch=[pltpu.VMEM((2, 2, planes * rows // 2, 128), F32)],
        grant=grant,
    )(blocks, *gathered, fine_bound, mid_bound, coarse_bound, coarse_diag, gather_rows, squeeze)

    step = 4
    while step < gxs:
        bounds = jnp.maximum(bounds, send(bounds, lambda x, y, z: (x ^ step, y, z)))
        step *= 2
    bounds = jnp.maximum(bounds, send(bounds, lambda x, y, z: (x ^ 1, y, z ^ 1)))
    other = send(bounds, lambda x, y, z: (x ^ 2, y, z ^ 1))
    (power_1,) = call(power_kernel, [field], flops=1000000000, size=4000000, grant=grant)(scale_w, mass_w, inverse_w, source_w, fine)
    (basis,) = call(
        restrict_kernel,
        [((4, size_1, 128), F32)],
        scratch=[pltpu.VMEM(*field), pltpu.VMEM((4, 2, 2 * size_1, 128), F32)],
        flops=2000000000,
        size=8000000,
        grant=grant,
    )(scale_w, mass_w, inverse_w, source_w, power_1, fine, squeeze)
    (result,) = call(
        final_kernel,
        [(right_side.shape, F32)],
        scratch=[
            pltpu.VMEM((planes // 2 + 4, slab // 2, 128), F32),
            pltpu.VMEM((2, 6 * slab, 128), F32),
            pltpu.VMEM((4, 3, rows, 128), F32),
        ],
        grant=grant,
    )(
        bounds, other, source_w, scale_w, mass_w, inverse_w, power_1, basis, *levels,
        fine, mid, coarse, gather_rows, spread_rows, stretch,
    )
    return result


def solution(mesh):
    placed = (P(None, "gz", "gy", "gx"), P("gz", "gy", "gx"), P("gz", "gy", "gx"), P())
    return jax.shard_map(
        on_device, mesh=mesh, in_specs=placed, out_specs=P(None, "gz", "gy", "gx"), check_vma=False
    )
```

```python
import functools

import jax
import jax.numpy as jnp
from jax import lax
from jax.experimental import pallas as pl
from jax.experimental.pallas import tpu as pltpu
from jax.sharding import PartitionSpec as P

AXES = ("gx", "gy", "gz")
COARSE_ITERS = 8
SMOOTH_RATIO = 20.0
COARSE_RATIO = 200.0
F32, BF16 = jnp.float32, jnp.bfloat16
VM = pl.BlockSpec(memory_space=pltpu.VMEM)
SM = pl.BlockSpec(memory_space=pltpu.SMEM)
LANES = 256
LINE = 384
PAD = 3


def call(kernel, outs, specs=None, scratch=(), flops=1000000, size=100000, grant=None):
    params = pltpu.CompilerParams(vmem_limit_bytes=grant * 1024 * 1024) if grant else None
    outs = [jax.ShapeDtypeStruct(shape, dtype) for shape, dtype in outs]

    def run(*args):
        return pl.pallas_call(
            kernel,
            out_shape=outs,
            in_specs=specs or [VM] * len(args),
            out_specs=[VM] * len(outs),
            scratch_shapes=scratch,
            compiler_params=params,
            cost_estimate=pl.CostEstimate(flops=flops, bytes_accessed=size, transcendentals=0),
        )(*args)

    return run


def iota(shape, dim):
    return lax.broadcasted_iota(jnp.int32, shape, dim)


def ones_where(mask):
    return jnp.where(mask, 1.0, 0.0).astype(BF16)


def split(values):
    high = values.astype(BF16)
    return high, (values - high.astype(F32)).astype(BF16)


def dot(left, right):
    return jnp.dot(left, right, preferred_element_type=F32)


def lanes_apply(values, stacked):
    return dot(jnp.concatenate(split(values), axis=1), stacked)


def rows_apply(selection, values):
    width = values.shape[1]
    product = dot(selection, jnp.concatenate(split(values), axis=1))
    return product[:, :width] + product[:, width:]


def banded_stacked(matrix, values):
    high, low = split(values)
    return dot(matrix, jnp.concatenate([high, high, low], axis=0))


def banded_planes(matrix, values, planes, step):
    slab, lanes = values.shape[0] // planes, values.shape[1]
    edge = jnp.zeros((slab, lanes), F32)
    padded = jnp.concatenate([edge, values, edge], axis=0)
    beside = jnp.concatenate([padded[at * slab : (at + 3) * slab] for at in range(planes)], axis=1)
    high = beside.astype(BF16).astype(F32)
    stacked = jnp.concatenate([high, high, beside - high], axis=0).astype(BF16)
    product = dot(matrix[:, : 9 * slab], stacked)
    outs = []
    for at in range(planes):
        below, here, above = (
            product[part * slab : part * slab + slab, at * lanes : at * lanes + lanes] for part in range(3)
        )
        outs.append(here + pltpu.roll(below, step, 1) + pltpu.roll(above, lanes - step, 1))
    return jnp.concatenate(outs, axis=0)


def paired_lanes(values):
    even = iota(values.shape, 1) % 2 == 0
    return values + jnp.where(even, pltpu.roll(values, values.shape[1] - 1, 1), pltpu.roll(values, 1, 1))


def shifted_sum(product, slabs, rows, lanes):
    parts = product.reshape(slabs, 3, rows, lanes)
    below = parts[:, 0].reshape(slabs * rows, lanes)
    above = parts[:, 2].reshape(slabs * rows, lanes)
    here = parts[:, 1].reshape(slabs * rows, lanes)
    return here + pltpu.roll(below, 1, 1) + pltpu.roll(above, lanes - 1, 1)


def group_of(slab):
    return max(1, 256 // slab - 2)


def groups(planes, most):
    sizes = []
    while planes:
        size = min(most, planes)
        if most > 2 and planes == most + 1:
            size = 2
        sizes.append(size)
        planes -= size
    return sizes


def fine_operator(matrix, scale_of, mass_of, weighted_of, value_of, planes, rows, finish):
    slab = 3 * rows
    parts = {}
    for plane in range(planes):
        near = range(plane - 1, plane + 2)
        for i in near:
            if i not in parts:
                parts[i] = split(weighted_of(i).reshape(slab, LANES))
        high = [parts[i][0] for i in near]
        low = [parts[i][1] for i in near]
        product = dot(matrix[:, : 9 * slab], jnp.concatenate(high + high + low, axis=0))
        total = shifted_sum(product, 1, slab, LANES).reshape(3, rows, LANES)
        finish(plane, scale_of(plane)[None] * total + mass_of(plane)[None] * value_of(plane))


def panels(value_of, others, rows, width):
    column = iota((8, width), 1)
    which = column // rows
    row_in = column % rows
    result = {}
    for step_x in range(3):
        for comp in range(3):
            coeffs = []
            for step_y in range(3):
                coeff = jnp.zeros((8, width), F32)
                for plane in range(3):
                    for other in range(others):
                        value = value_of(plane * 9 + step_y * 3 + step_x, comp, other)
                        coeff = jnp.where(which == plane * others + other, value, coeff)
                coeffs.append(coeff)
            pieces = []
            for block in range(rows // 8):
                gap = row_in - (iota((8, width), 0) + block * 8)
                piece = jnp.zeros((8, width), F32)
                for step_y in range(3):
                    piece = jnp.where(gap == step_y - 1, coeffs[step_y], piece)
                pieces.append(piece)
            result[step_x, comp] = jnp.concatenate(pieces, axis=0)
    return result


def turned(value, turn):
    turn %= value.shape[1]
    return pltpu.roll(value, turn, 1) if turn else value


def parts_of(value):
    high = value.astype(BF16).astype(F32)
    return high, value - high


def stack3(value, size):
    high, low = parts_of(value)
    return (high + turned(low, size) + turned(high, 2 * size)).astype(BF16)


def up128(size):
    return -(-size // 128) * 128


def coarse_slab(few):
    return -(-3 * few // 16) * 16


def matrices_kernel(
    rows, planes, blocks, fine, fine_bound, mid, mid_bound, coarse, coarse_bound, coarse_diag,
    gather_rows, spread_rows, squeeze, squeeze_line, stretch,
):
    def direct(offset, comp, other):
        return blocks[offset * 9 + comp * 3 + other]

    def absolute(offset, comp, other):
        at = offset * 9 + comp * 3
        return jnp.abs(blocks[at]) + jnp.abs(blocks[at + 1]) + jnp.abs(blocks[at + 2])

    slab = 3 * rows
    group = group_of(slab)
    width = up128(3 * slab)
    found = panels(direct, 3, rows, width)
    value = jnp.concatenate([found[step_x, comp] for step_x in range(3) for comp in range(3)], axis=0)
    if fine.shape[1] > width:
        value = jnp.concatenate([value, jnp.zeros((3 * slab, fine.shape[1] - width), F32)], axis=1)
    fine[...] = stack3(value, 3 * slab)
    bound = panels(absolute, 1, rows, fine_bound.shape[1])
    for plane in range(group):
        for step_x in range(3):
            start = (plane * 3 + step_x) * slab
            value = turned(jnp.concatenate([bound[step_x, comp] for comp in range(3)], axis=0), plane * rows)
            fine_bound[start : start + slab, :] = stack3(value, (group + 2) * rows)

    rows, planes = rows // 2, planes // 2
    slab = 3 * rows
    found = panels(direct, 3, rows, mid.shape[1])
    whole = jnp.concatenate([found[step_x, comp] for step_x in range(3) for comp in range(3)], axis=0)
    few, half = rows // 2, planes // 2
    size = coarse_slab(few)

    def choose(out, source):
        place = out % size
        wanted = out // size * slab + place // few * rows + place % few
        return ones_where(jnp.logical_and(source == wanted, place < 3 * few))

    shape = (3 * size, 3 * slab)
    choose_rows = choose(iota(shape, 0), iota(shape, 1))
    shape = (mid.shape[1], up128(3 * size))
    choose_columns = jnp.where(iota(shape, 1) < 3 * size, choose(iota(shape, 1), iota(shape, 0)), 0.0).astype(BF16)

    def smaller(matrix):
        return dot(dot(choose_rows, matrix.astype(BF16)).astype(BF16), choose_columns)

    for target, small_target, value in ((mid, coarse, whole), (mid_bound, coarse_bound, jnp.abs(whole))):
        target[...] = stack3(value, 3 * slab)
        high, low = parts_of(value)
        high, low = smaller(high), smaller(low)
        width = small_target.shape[1]
        if width > high.shape[1]:
            more = jnp.zeros((3 * size, width - high.shape[1]), F32)
            high, low = jnp.concatenate([high, more], axis=1), jnp.concatenate([low, more], axis=1)
        small_target[...] = (high + turned(low, 3 * size) + turned(high, 6 * size)).astype(BF16)
    comp = iota((half * size, 128), 0) % size // few
    diag = [blocks[13 * 9 + 4 * at] for at in range(3)]
    coarse_diag[...] = jnp.where(comp == 0, diag[0], jnp.where(comp == 1, diag[1], diag[2]))

    def same_aggregate(small, large):
        place, inner = small % size, large % slab
        same = jnp.logical_and(small // size == large // (2 * slab), place // few == inner // rows)
        return jnp.logical_and(same, place % few == inner % rows // 2)

    shape = (half * size, planes * slab)
    gather_rows[...] = ones_where(same_aggregate(iota(shape, 0), iota(shape, 1)))
    shape = (planes * slab, 2 * half * size)
    spread_rows[...] = ones_where(same_aggregate(iota(shape, 1) % (half * size), iota(shape, 0)))
    shape = (2 * LANES, 128)
    squeeze[...] = ones_where(iota(shape, 0) % LANES // 2 == iota(shape, 1))
    shape = (2 * LINE, 256)
    lane = iota(shape, 0) % LINE
    squeeze_line[...] = ones_where(jnp.where(lane < 256, lane // 2, lane // 2 + 64) == iota(shape, 1))
    shape = (256, LANES)
    stretch[...] = ones_where(iota(shape, 0) % 128 == iota(shape, 1) // 2)


def halves(planes):
    count = planes.shape[0] // 2
    low = iota((count, 8, 128), 2) < 64
    first, second = planes[:count], pltpu.roll(planes[count:], 64, 2)
    return jnp.where(low, second, first), jnp.where(low, first, second)


def pack_kernel(main, send_a, send_b):
    high, low = halves(main[...])
    more_high, more_low = halves(main[12:])
    even = lax.rem(lax.axis_index("gx"), 2) == 0
    send_a[:10] = jnp.where(even, high, low)
    send_a[10:] = jnp.where(even, more_low, more_high)
    send_b[:10] = jnp.where(even, low, high)
    send_b[10:] = jnp.zeros((4, 8, 128), F32)


def widen_kernel(count, main, got_b, got_a, wide):
    index = lax.axis_index("gx")
    even = lax.rem(index, 2) == 0
    first, second, more = got_a[:10], got_b[:10], got_a[10:]
    above = jnp.where(index < count - 1, jnp.where(even, first, second), 0.0)
    below = jnp.where(index > 0, jnp.where(even, second, first), 0.0)
    low = iota((10, 8, 128), 2) < 64
    wide[:20] = main[...]
    wide[20:30] = jnp.where(low, above, below)
    wide[30:40] = jnp.where(low, pltpu.roll(above, 64, 2), pltpu.roll(below, 64, 2))
    wide[40:] = jnp.where(even, pltpu.roll(more, 64, 2), more)


def inverse_diagonal(scale, mass, blocks, factor):
    square = scale * scale
    parts = []
    for comp in range(3):
        diag = factor * blocks[13 * 9 + comp * 4] * square + mass
        parts.append(jnp.where(scale > 0.0, 1.0 / diag, 0.0)[:, None])
    return jnp.concatenate(parts, axis=1)


def largest(ratio):
    width = ratio.shape[1]
    flat = jnp.max(ratio.reshape(-1, 8, width), axis=0)
    return functools.reduce(jnp.maximum, [flat[:, at : at + 128] for at in range(0, width, 128)])


def paired_planes(values):
    pairs = values.reshape((-1, 2) + values.shape[1:])
    return pairs[:, 0] + pairs[:, 1]


def paired_rows(held, values):
    parts, count = held.shape[0], held.shape[1] // 2
    for part in range(parts):
        held[part] = values[:, part * 128 : part * 128 + 128]
    return jnp.concatenate(
        [held[part, pl.ds(0, count, stride=2)] + held[part, pl.ds(1, count, stride=2)] for part in range(parts)], axis=1
    )


def window_kernel(
    gys, ordered, blocks, *refs
):
    (*blocks_in, fine_bound, mid_bound, coarse_bound, coarse_diag, gather_rows, squeeze_line, source_w, scale_w, mass_w, inverse_w,
     spread_1w, weight_1w, inverse_1w, spread_2w, weight_2w, inverse_2w, bounds, scale_x, mass_x, held) = refs
    planes, rows = scale_w.shape[0] - 2 * PAD, scale_w.shape[1]
    gz, gy = lax.axis_index("gz"), lax.axis_index("gy")
    even = lax.rem(lax.axis_index("gx"), 2) == 0
    low = iota((4, 8, 128), 2) < 64
    for at in (0, planes + 1):
        scale_x[at] = jnp.zeros((rows, LINE), F32)
    for at in (0, planes + PAD):
        source_w[at : at + PAD] = jnp.zeros((PAD, 3, rows, LANES), F32)
        inverse_w[at : at + PAD] = jnp.zeros((PAD, 3, rows, LANES), F32)
        scale_w[at : at + PAD] = jnp.zeros((PAD, rows, LANES), F32)
        mass_w[at : at + PAD] = jnp.zeros((PAD, rows, LANES), F32)
    number = 0
    for ref in blocks_in:
        for block in range(ref.shape[0]):
            if ordered:
                place_z, place_y = number // gys, number % gys
            else:
                place_z = lax.bitwise_xor(gz, number // 4 + 2 * (number % 2))
                place_y = lax.bitwise_xor(gy, number % 4 // 2)
            at_z = pl.ds(PAD + 4 * place_z, 4)
            at_y = pl.ds(pl.multiple_of(8 * place_y, 8), 8)
            for half in (0, 1):
                lanes = slice(half * 128, half * 128 + 128)
                part = ref.at[block, half * 20 : half * 20 + 20]
                for comp in range(3):
                    source_w[at_z, comp, at_y, lanes] = part[comp * 4 : comp * 4 + 4]
                scale_w[at_z, at_y, lanes] = part[12:16]
                mass_w[at_z, at_y, lanes] = part[16:20]
            here, more = ref.at[block], ref[block, 40:44]
            turned_more = pltpu.roll(more, 64, 2)
            for target, own, start, at_low, at_high in (
                (scale_x, 12, 1, more, turned_more),
                (mass_x, 16, 0, turned_more, more),
            ):
                at_x = pl.ds(start + 4 * place_z, 4)
                halo = here[own + 20 : own + 24]
                target[at_x, at_y, :128] = here[own : own + 4]
                target[at_x, at_y, 128:256] = jnp.where(low, halo, jnp.where(even, at_high, 0.0))
                target[at_x, at_y, 256:] = jnp.where(low, jnp.where(even, 0.0, at_low), halo)
            number += 1

    scale, mass = scale_x[1 : 1 + planes], mass_x[...]
    inverse = inverse_diagonal(scale, mass, blocks, 1.0)
    inverse_w[PAD : PAD + planes, :, :, :128] = inverse[..., :128]
    wide_low = iota(inverse.shape[:3] + (128,), 3) < 64
    inverse_w[PAD : PAD + planes, :, :, 128:] = jnp.where(wide_low, inverse[..., 128:256], inverse[..., 256:])
    slab = 3 * rows
    outs = []
    at = 0
    for size in groups(planes, group_of(slab)):
        near = scale_x[at : at + size + 2].reshape((size + 2) * rows, LINE)
        if size < group_of(slab):
            near = jnp.concatenate([near, jnp.zeros(((group_of(slab) - size) * rows, LINE), F32)], axis=0)
        depth = 3 * (group_of(slab) + 2) * rows
        outs.append(shifted_sum(banded_stacked(fine_bound[: size * 3 * slab, :depth], near), size, slab, LINE))
        at += size
    total = jnp.concatenate(outs, axis=0).reshape(planes, 3, rows, LINE)
    ratio = (scale[:, None] * total + mass[:, None]) * inverse
    bounds[0] = largest(ratio.reshape(planes * slab, LINE))

    rows, planes = rows // 2, planes // 2
    slab = 3 * rows
    count = planes * rows
    pairs = [
        paired_rows(held.at[at], paired_planes(values).reshape(2 * count, LINE))
        for at, values in enumerate((scale, mass))
    ]
    middle = lanes_apply(jnp.concatenate(pairs, axis=0), squeeze_line[...])
    scale_1 = (middle[:count] * 0.125).reshape(planes, rows, 256)
    mass_1 = middle[count:].reshape(planes, rows, 256)
    inverse_1 = inverse_diagonal(scale_1, mass_1, blocks, 2.0).reshape(planes * slab, 256)
    spread_1 = jnp.broadcast_to(scale_1[:, None], (planes, 3, rows, 256)).reshape(planes * slab, 256)
    weight_1 = jnp.broadcast_to(mass_1[:, None], (planes, 3, rows, 256)).reshape(planes * slab, 256)
    total = banded_planes(mid_bound, spread_1, planes, 1)
    bounds[1] = largest((2.0 * spread_1 * total + weight_1) * inverse_1)

    def window(values):
        return jnp.where(iota((values.shape[0], 128), 1) < 96, values[:, :128], values[:, 128:])

    spread_1w[...], weight_1w[...], inverse_1w[...] = window(spread_1), window(weight_1), window(inverse_1)

    both = rows_apply(gather_rows[...], jnp.concatenate([spread_1, weight_1], axis=1))
    spread_2 = paired_lanes(both[:, :256]) * 0.125
    weight_2 = paired_lanes(both[:, 256:])
    diag = jnp.concatenate([coarse_diag[...]] * 2, axis=1)
    inverse_2 = jnp.where(spread_2 > 0.0, 1.0 / (4.0 * diag * spread_2 * spread_2 + weight_2), 0.0)
    total = banded_planes(coarse_bound, spread_2, planes // 2, 2)
    bounds[2] = largest((4.0 * spread_2 * total + weight_2) * inverse_2)
    spread_2w[...], weight_2w[...], inverse_2w[...] = window(spread_2), window(weight_2), window(inverse_2)


def inner_power(scale_w, mass_w, inverse_w, matrix, values, finish):
    planes, rows = scale_w.shape[0] - 2 * PAD, scale_w.shape[1]
    fine_operator(
        matrix,
        lambda i: scale_w[PAD + i],
        lambda i: mass_w[PAD + i],
        lambda i: scale_w[PAD + i][None] * (inverse_w[PAD + i] * values[PAD + i]),
        lambda i: inverse_w[PAD + i] * values[PAD + i],
        planes,
        rows,
        finish,
    )


def power_kernel(scale_w, mass_w, inverse_w, source_w, fine, power):
    planes, shape = scale_w.shape[0] - 2 * PAD, power.shape[1:]
    power[:PAD] = jnp.zeros((PAD,) + shape, F32)
    power[PAD + planes :] = jnp.zeros((PAD,) + shape, F32)

    def finish(at, values):
        power[PAD + at] = values

    inner_power(scale_w, mass_w, inverse_w, fine, source_w, finish)


def restrict_kernel(scale_w, mass_w, inverse_w, source_w, power_1, fine, squeeze, basis, power_2, held):
    planes, rows = scale_w.shape[0] - 2 * PAD, scale_w.shape[1]
    power_kernel(scale_w, mass_w, inverse_w, power_1, fine, power_2)
    third = []
    inner_power(scale_w, mass_w, inverse_w, fine, power_2, lambda at, values: third.append(values))
    third = jnp.stack(third, axis=0)
    inner = slice(PAD, PAD + planes)
    size = planes // 2 * 3 * rows
    for at, values in enumerate((source_w[inner], power_1[inner], power_2[inner], third)):
        pairs = paired_rows(held.at[at], paired_planes(values).reshape(size, LANES))
        basis[at] = lanes_apply(pairs, squeeze[...])


def chebyshev_constants(ratio, degree):
    sigma = (ratio + 1.0) / (ratio - 1.0)
    rho = 1.0 / sigma
    steps = []
    for _ in range(degree - 1):
        rho_next = 1.0 / (2.0 * sigma - rho)
        steps.append((rho_next * rho, 4.0 * rho_next / (1.0 - 1.0 / ratio)))
        rho = rho_next
    return 2.0 / (1.0 + 1.0 / ratio), steps


def chebyshev(residue, degree, inverse, ratio, operate, keep):
    first, steps = chebyshev_constants(ratio, degree)
    direction = first * (inverse * residue)
    total = direction
    for hold, push in steps:
        residue = residue - operate(direction)
        direction = hold * direction + push * (inverse * residue)
        total = total + direction
    if keep:
        residue = residue - operate(direction)
    return total, residue


def scaled(coeff, values):
    lanes = values.shape[-1]
    if lanes != 128:
        coeff = jnp.concatenate([coeff] * (lanes // 128), axis=1)
    flat = values.reshape(-1, 8, lanes)
    return (coeff[None] * flat).reshape(values.shape)


def final_kernel(
    bounds_a, bounds_b, source_w, scale_w, mass_w, inverse_w, power_1, basis,
    spread_1w, weight_1w, inverse_1w, spread_2w, weight_2w, inverse_2w,
    fine, mid, coarse, gather_rows, spread_rows, stretch, result, lifted_w, doubled_w, answer_w,
):
    rows = scale_w.shape[1] // 2
    planes = (scale_w.shape[0] - 2 * PAD) // 2
    slab = 3 * rows
    gz, gy = lax.axis_index("gz"), lax.axis_index("gy")
    worst = jnp.maximum(bounds_a[...], bounds_b[...])
    inverse_bounds = [1.0 / jnp.full((8, 128), jnp.max(worst[level]), F32) for level in range(3)]
    over_0 = inverse_bounds[0]

    first, ((hold, push),) = chebyshev_constants(SMOOTH_RATIO, 2)
    beta = push * first
    gamma = first * (1.0 + hold) + push
    omega = 4.0 / 3.0
    source_1 = basis[0] - scaled(
        over_0,
        (gamma + omega) * basis[1]
        - scaled(over_0, (beta + omega * gamma) * basis[2] - scaled(over_0, (omega * beta) * basis[3])),
    )

    spread_1, weight_1 = spread_1w[...], weight_1w[...]
    spread_2, weight_2 = spread_2w[...], weight_2w[...]
    inverse_1 = scaled(inverse_bounds[1], inverse_1w[...])
    inverse_2 = scaled(inverse_bounds[2], inverse_2w[...])
    double_1, double_2 = 2.0 * spread_1, 4.0 * spread_2

    def operate_1(values):
        return double_1 * banded_planes(mid, spread_1 * values, planes, 1) + weight_1 * values

    def operate_2(values):
        return double_2 * banded_planes(coarse, spread_2 * values, planes // 2, 2) + weight_2 * values

    iterate, residue = chebyshev(source_1, 2, inverse_1, SMOOTH_RATIO, operate_1, True)
    smoothed = residue - omega * operate_1(inverse_1 * residue)
    source_2 = paired_lanes(rows_apply(gather_rows[...], smoothed))
    error_2, _ = chebyshev(source_2, COARSE_ITERS, inverse_2, COARSE_RATIO, operate_2, False)
    lifted = dot(spread_rows[...], jnp.concatenate(split(error_2), axis=0))
    iterate = iterate + lifted - omega * (inverse_1 * operate_1(lifted))
    residue = source_1 - operate_1(iterate)
    more, _ = chebyshev(residue, 2, inverse_1, SMOOTH_RATIO, operate_1, False)
    error_1 = iterate + more

    lifted_w[0:2] = jnp.zeros((2, slab, 128), F32)
    lifted_w[planes + 2 : planes + 4] = jnp.zeros((2, slab, 128), F32)
    lifted_w[2 : planes + 2] = error_1.reshape(planes, slab, 128)
    near = lifted_w[pl.ds(2 * gz, 6)].reshape(6 * slab, 128)
    wide = lanes_apply(near, stretch[...])
    for half in (0, 1):
        for odd in (0, 1):
            doubled_w[half, pl.ds(odd, 6 * slab, stride=2)] = wide[:, half * 128 : half * 128 + 128]
    slabs = jnp.concatenate([doubled_w[0], doubled_w[1]], axis=1).reshape(6, 3, 2 * rows, LANES)
    error = jnp.stack([slabs[(plane + 1) // 2] for plane in range(10)], axis=0)

    def near_own(ref, reach):
        return ref[pl.ds(4 * gz + PAD - reach, 4 + 2 * reach)]

    scale, mass = near_own(scale_w, 3), near_own(mass_w, 2)
    inverse = scaled(over_0, near_own(inverse_w, 2))
    source = near_own(source_w, 2)
    before = gamma * source - scaled(over_0, beta * near_own(power_1, 2))

    def apply(values, edge):
        outs = []
        fine_operator(
            fine,
            lambda i: scale[i + 4 - edge],
            lambda i: mass[i + 3 - edge],
            lambda i: scale[i + 4 - edge][None] * values[i + 1],
            lambda i: values[i + 1],
            2 + 2 * edge,
            2 * rows,
            lambda at, result: outs.append(result),
        )
        return jnp.stack(outs, axis=0)

    image = apply(error, 3)
    iterate = inverse * (before - omega * image) + error[1:9]
    residue = source[1:7] - apply(iterate, 2)
    direction = first * (inverse[1:7] * residue)
    last = residue[1:5] - apply(direction, 1)
    answer = iterate[2:6] + (1.0 + hold) * direction[1:5] + push * (inverse[2:6] * last)
    answer_w[...] = answer[:, :, :, :128]
    for comp in range(3):
        result[comp] = answer_w[:, comp, pl.ds(pl.multiple_of(8 * gy, 8), 8), :]


def swap_pairs(counts, target):
    def number(place):
        return (place[0] * counts[1] + place[1]) * counts[2] + place[2]

    places = [(x, y, z) for x in range(counts[0]) for y in range(counts[1]) for z in range(counts[2])]
    return [(number(place), number(target(*place))) for place in places]


def odd_partner(index):
    return index - 1 if index % 2 == 0 else index + 1


def on_device(right_side, stiff_scale, nodal_mass, stencil_blocks):
    counts = tuple(lax.axis_size(axis) for axis in AXES)
    gxs, gys, gzs = counts
    blocks = stencil_blocks.reshape(243)

    def send(values, target):
        return lax.ppermute(values, AXES, swap_pairs(counts, target))

    def x_second(x, y, z):
        return (x, y, z ^ 1) if x in (0, gxs - 1) else (odd_partner(x), y, z)

    rows, planes = 8 * gys, 4 * gzs
    grant = 20 if planes * rows <= 256 else 48
    slab = 3 * rows
    group = group_of(slab)
    size_1 = planes * slab // 4
    size = coarse_slab(rows // 4)
    size_2 = planes // 4 * size
    (
        fine, fine_bound, mid, mid_bound, coarse, coarse_bound, coarse_diag, gather_rows, spread_rows, squeeze,
        squeeze_line, stretch,
    ) = call(
        functools.partial(matrices_kernel, rows, planes),
        [
            ((3 * slab, up128(9 * slab)), BF16),
            ((group * 3 * slab, up128(3 * (group + 2) * rows)), BF16),
            ((3 * slab // 2, up128(9 * slab // 2)), BF16),
            ((3 * slab // 2, up128(9 * slab // 2)), BF16),
            ((3 * size, up128(9 * size)), BF16),
            ((3 * size, up128(9 * size)), BF16),
            ((size_2, 128), F32),
            ((size_2, size_1), BF16),
            ((size_1, 2 * size_2), BF16),
            ((2 * LANES, 128), BF16),
            ((2 * LINE, 256), BF16),
            ((256, LANES), BF16),
        ],
        specs=[SM],
        flops=5000000000,
        size=8000000,
        grant=grant,
    )(blocks)

    half = ((14, 8, 128), F32)
    main = jnp.concatenate([right_side.reshape(12, 8, 128), stiff_scale, nodal_mass], axis=0)
    send_a, send_b = call(pack_kernel, [half, half], grant=8)(main)
    got_b = send(send_b, x_second)
    got_a = send(send_a, lambda x, y, z: (x ^ 1, y, z))
    (wide,) = call(functools.partial(widen_kernel, gxs), [((44, 8, 128), F32)], grant=8)(main, got_b, got_a)
    ordered = not (gys == 2 and gzs == 4)
    if ordered:
        gathered = [lax.all_gather(wide, ("gz", "gy"), tiled=False)]
    else:
        near = [
            wide,
            send(wide, lambda x, y, z: (x, y, z ^ 2)),
            send(wide, lambda x, y, z: (x, y ^ 1, z)),
            send(wide, lambda x, y, z: (x, y ^ 1, z ^ 2)),
        ]
        near[3], fine = lax.optimization_barrier((near[3], fine))
        gathered = [block[None] for block in near + [send(block, lambda x, y, z: (x, y, z ^ 1)) for block in near]]

    field = ((planes + 2 * PAD, 3, rows, LANES), F32)
    single = ((planes + 2 * PAD, rows, LANES), F32)
    source_w, scale_w, mass_w, inverse_w, *levels, bounds = call(
        functools.partial(window_kernel, gys, ordered),
        [field, single, single, field] + [((size_1, 128), F32)] * 3 + [((size_2, 128), F32)] * 3 + [((3, 8, 128), F32)],
        specs=[SM] + [VM] * (len(gathered) + 6),
        scratch=[
            pltpu.VMEM((planes + 2, rows, LINE), F32),
            pltpu.VMEM((planes, rows, LINE), F32),
            pltpu.VMEM((2, LINE // 128, planes * rows // 2, 128), F32),
        ],
        grant=grant,
    )(blocks, *gathered, fine_bound, mid_bound, coarse_bound, coarse_diag, gather_rows, squeeze_line)

    step, other = 2, bounds
    while step < gxs:
        bounds = jnp.maximum(bounds, other)
        other = send(bounds, lambda x, y, z: (x ^ step, y, z ^ 1))
        step *= 2
    (power_1,) = call(power_kernel, [field], flops=1000000000, size=4000000, grant=grant)(scale_w, mass_w, inverse_w, source_w, fine)
    (basis,) = call(
        restrict_kernel,
        [((4, size_1, 128), F32)],
        scratch=[pltpu.VMEM(*field), pltpu.VMEM((4, 2, 2 * size_1, 128), F32)],
        flops=2000000000,
        size=8000000,
        grant=grant,
    )(scale_w, mass_w, inverse_w, source_w, power_1, fine, squeeze)
    (result,) = call(
        final_kernel,
        [(right_side.shape, F32)],
        scratch=[
            pltpu.VMEM((planes // 2 + 4, slab // 2, 128), F32),
            pltpu.VMEM((2, 6 * slab, 128), F32),
            pltpu.VMEM((4, 3, rows, 128), F32),
        ],
        grant=grant,
    )(
        bounds, other, source_w, scale_w, mass_w, inverse_w, power_1, basis, *levels,
        fine, mid, coarse, gather_rows, spread_rows, stretch,
    )
    return result


def solution(mesh):
    placed = (P(None, "gz", "gy", "gx"), P("gz", "gy", "gx"), P("gz", "gy", "gx"), P())
    return jax.shard_map(
        on_device, mesh=mesh, in_specs=placed, out_specs=P(None, "gz", "gy", "gx"), check_vma=False
    )
```

```python
import functools

import jax
import jax.numpy as jnp
from jax import lax
from jax.experimental import pallas as pl
from jax.experimental.pallas import tpu as pltpu
from jax.sharding import PartitionSpec as P

AXES = ("gx", "gy", "gz")
COARSE_ITERS = 8
SMOOTH_RATIO = 20.0
COARSE_RATIO = 200.0
F32, BF16 = jnp.float32, jnp.bfloat16
VM = pl.BlockSpec(memory_space=pltpu.VMEM)
SM = pl.BlockSpec(memory_space=pltpu.SMEM)
LANES = 256
LINE = 384
PAD = 3


def call(kernel, outs, specs=None, scratch=(), flops=1000000, size=100000, grant=None):
    params = pltpu.CompilerParams(vmem_limit_bytes=grant * 1024 * 1024) if grant else None
    outs = [jax.ShapeDtypeStruct(shape, dtype) for shape, dtype in outs]

    def run(*args):
        return pl.pallas_call(
            kernel,
            out_shape=outs,
            in_specs=specs or [VM] * len(args),
            out_specs=[VM] * len(outs),
            scratch_shapes=scratch,
            compiler_params=params,
            cost_estimate=pl.CostEstimate(flops=flops, bytes_accessed=size, transcendentals=0),
        )(*args)

    return run


def iota(shape, dim):
    return lax.broadcasted_iota(jnp.int32, shape, dim)


def ones_where(mask):
    return jnp.where(mask, 1.0, 0.0).astype(BF16)


def split(values):
    high = values.astype(BF16)
    return high, (values - high.astype(F32)).astype(BF16)


def dot(left, right):
    return jnp.dot(left, right, preferred_element_type=F32)


def lanes_apply(values, stacked):
    return dot(jnp.concatenate(split(values), axis=1), stacked)


def rows_apply(selection, values):
    width = values.shape[1]
    product = dot(selection, jnp.concatenate(split(values), axis=1))
    return product[:, :width] + product[:, width:]


def banded_stacked(matrix, values):
    high, low = split(values)
    return dot(matrix, jnp.concatenate([high, high, low], axis=0))


def banded_planes(matrix, values, planes, step):
    slab, lanes = values.shape[0] // planes, values.shape[1]
    edge = jnp.zeros((slab, lanes), F32)
    padded = jnp.concatenate([edge, values, edge], axis=0)
    beside = jnp.concatenate([padded[at * slab : (at + 3) * slab] for at in range(planes)], axis=1)
    high = beside.astype(BF16).astype(F32)
    stacked = jnp.concatenate([high, high, beside - high], axis=0).astype(BF16)
    product = dot(matrix[:, : 9 * slab], stacked)
    outs = []
    for at in range(planes):
        below, here, above = (
            product[part * slab : part * slab + slab, at * lanes : at * lanes + lanes] for part in range(3)
        )
        outs.append(here + pltpu.roll(below, step, 1) + pltpu.roll(above, lanes - step, 1))
    return jnp.concatenate(outs, axis=0)


def paired_lanes(values):
    even = iota(values.shape, 1) % 2 == 0
    return values + jnp.where(even, pltpu.roll(values, values.shape[1] - 1, 1), pltpu.roll(values, 1, 1))


def shifted_sum(product, slabs, rows, lanes):
    parts = product.reshape(slabs, 3, rows, lanes)
    below = parts[:, 0].reshape(slabs * rows, lanes)
    above = parts[:, 2].reshape(slabs * rows, lanes)
    here = parts[:, 1].reshape(slabs * rows, lanes)
    return here + pltpu.roll(below, 1, 1) + pltpu.roll(above, lanes - 1, 1)


def group_of(slab):
    return max(1, 256 // slab - 2)


def groups(planes, most):
    sizes = []
    half = planes // 2
    while half:
        size = min(most, half)
        sizes += [size, size]
        half -= size
    return sizes


def fine_operator(matrix, scale_of, mass_of, weighted_of, value_of, planes, rows, finish):
    slab = 3 * rows
    parts = {}
    for plane in range(planes):
        near = range(plane - 1, plane + 2)
        for i in near:
            if i not in parts:
                parts[i] = split(weighted_of(i).reshape(slab, LANES))
        high = [parts[i][0] for i in near]
        low = [parts[i][1] for i in near]
        product = dot(matrix[:, : 9 * slab], jnp.concatenate(high + high + low, axis=0))
        total = shifted_sum(product, 1, slab, LANES).reshape(3, rows, LANES)
        finish(plane, scale_of(plane)[None] * total + mass_of(plane)[None] * value_of(plane))


def panels(value_of, others, rows, width):
    column = iota((8, width), 1)
    which = column // rows
    row_in = column % rows
    result = {}
    for step_x in range(3):
        for comp in range(3):
            coeffs = []
            for step_y in range(3):
                coeff = jnp.zeros((8, width), F32)
                for plane in range(3):
                    for other in range(others):
                        value = value_of(plane * 9 + step_y * 3 + step_x, comp, other)
                        coeff = jnp.where(which == plane * others + other, value, coeff)
                coeffs.append(coeff)
            pieces = []
            for block in range(rows // 8):
                gap = row_in - (iota((8, width), 0) + block * 8)
                piece = jnp.zeros((8, width), F32)
                for step_y in range(3):
                    piece = jnp.where(gap == step_y - 1, coeffs[step_y], piece)
                pieces.append(piece)
            result[step_x, comp] = jnp.concatenate(pieces, axis=0)
    return result


def turned(value, turn):
    turn %= value.shape[1]
    return pltpu.roll(value, turn, 1) if turn else value


def parts_of(value):
    high = value.astype(BF16).astype(F32)
    return high, value - high


def stack3(value, size):
    high, low = parts_of(value)
    return (high + turned(low, size) + turned(high, 2 * size)).astype(BF16)


def up128(size):
    return -(-size // 128) * 128


def coarse_slab(few):
    return -(-3 * few // 16) * 16


def own_rows(values, count):
    index = lax.axis_index("gy")
    found = values[..., :8, :]
    for block in range(1, count):
        found = jnp.where(index == block, values[..., block * 8 : block * 8 + 8, :], found)
    return found


def matrices_kernel(
    rows, planes, blocks, fine, fine_own, fine_bound, mid, mid_bound, coarse, coarse_bound, coarse_diag,
    gather_rows, spread_rows, squeeze, squeeze_line, stretch,
):
    def direct(offset, comp, other):
        return blocks[offset * 9 + comp * 3 + other]

    def absolute(offset, comp, other):
        at = offset * 9 + comp * 3
        return jnp.abs(blocks[at]) + jnp.abs(blocks[at + 1]) + jnp.abs(blocks[at + 2])

    slab = 3 * rows
    group = group_of(slab)
    width = up128(3 * slab)
    found = panels(direct, 3, rows, width)
    every = [found[step_x, comp] for step_x in range(3) for comp in range(3)]
    for target, parts in ((fine, every), (fine_own, [own_rows(part, rows // 8) for part in every])):
        value = jnp.concatenate(parts, axis=0)
        if target.shape[1] > width:
            value = jnp.concatenate([value, jnp.zeros((value.shape[0], target.shape[1] - width), F32)], axis=1)
        target[...] = stack3(value, 3 * slab)
    bound = panels(absolute, 1, rows, fine_bound.shape[1])
    for plane in range(group):
        for step_x in range(3):
            start = (plane * 3 + step_x) * slab
            value = turned(jnp.concatenate([bound[step_x, comp] for comp in range(3)], axis=0), plane * rows)
            fine_bound[start : start + slab, :] = stack3(value, (group + 2) * rows)

    rows, planes = rows // 2, planes // 2
    slab = 3 * rows
    found = panels(direct, 3, rows, mid.shape[1])
    whole = jnp.concatenate([found[step_x, comp] for step_x in range(3) for comp in range(3)], axis=0)
    few, half = rows // 2, planes // 2
    size = coarse_slab(few)

    def choose(out, source):
        place = out % size
        wanted = out // size * slab + place // few * rows + place % few
        return ones_where(jnp.logical_and(source == wanted, place < 3 * few))

    shape = (3 * size, 3 * slab)
    choose_rows = choose(iota(shape, 0), iota(shape, 1))
    shape = (mid.shape[1], up128(3 * size))
    choose_columns = jnp.where(iota(shape, 1) < 3 * size, choose(iota(shape, 1), iota(shape, 0)), 0.0).astype(BF16)

    def smaller(matrix):
        return dot(dot(choose_rows, matrix.astype(BF16)).astype(BF16), choose_columns)

    for target, small_target, value in ((mid, coarse, whole), (mid_bound, coarse_bound, jnp.abs(whole))):
        target[...] = stack3(value, 3 * slab)
        high, low = parts_of(value)
        high, low = smaller(high), smaller(low)
        width = small_target.shape[1]
        if width > high.shape[1]:
            more = jnp.zeros((3 * size, width - high.shape[1]), F32)
            high, low = jnp.concatenate([high, more], axis=1), jnp.concatenate([low, more], axis=1)
        small_target[...] = (high + turned(low, 3 * size) + turned(high, 6 * size)).astype(BF16)
    comp = iota((half * size, 128), 0) % size // few
    diag = [blocks[13 * 9 + 4 * at] for at in range(3)]
    coarse_diag[...] = jnp.where(comp == 0, diag[0], jnp.where(comp == 1, diag[1], diag[2]))

    def same_aggregate(small, large):
        place, inner = small % size, large % slab
        same = jnp.logical_and(small // size == large // (2 * slab), place // few == inner // rows)
        return jnp.logical_and(same, place % few == inner % rows // 2)

    shape = (half * size, planes * slab)
    gather_rows[...] = ones_where(same_aggregate(iota(shape, 0), iota(shape, 1)))
    shape = (planes * slab, 2 * half * size)
    spread_rows[...] = ones_where(same_aggregate(iota(shape, 1) % (half * size), iota(shape, 0)))
    shape = (2 * LANES, 128)
    squeeze[...] = ones_where(iota(shape, 0) % LANES // 2 == iota(shape, 1))
    shape = (2 * LINE, 256)
    lane = iota(shape, 0) % LINE
    squeeze_line[...] = ones_where(jnp.where(lane < 256, lane // 2, lane // 2 + 64) == iota(shape, 1))
    shape = (256, LANES)
    stretch[...] = ones_where(iota(shape, 0) % 128 == iota(shape, 1) // 2)


def halves(planes):
    count = planes.shape[0] // 2
    low = iota((count, 8, 128), 2) < 64
    first, second = planes[:count], pltpu.roll(planes[count:], 64, 2)
    return jnp.where(low, second, first), jnp.where(low, first, second)


def pack_kernel(main, send_a, send_b):
    high, low = halves(main[...])
    more_high, more_low = halves(main[12:])
    even = lax.rem(lax.axis_index("gx"), 2) == 0
    send_a[:10] = jnp.where(even, high, low)
    send_a[10:] = jnp.where(even, more_low, more_high)
    send_b[:10] = jnp.where(even, low, high)
    send_b[10:] = jnp.zeros((4, 8, 128), F32)


def widen_kernel(count, main, got_b, got_a, wide):
    index = lax.axis_index("gx")
    even = lax.rem(index, 2) == 0
    first, second, more = got_a[:10], got_b[:10], got_a[10:]
    above = jnp.where(index < count - 1, jnp.where(even, first, second), 0.0)
    below = jnp.where(index > 0, jnp.where(even, second, first), 0.0)
    low = iota((10, 8, 128), 2) < 64
    wide[:20] = main[...]
    wide[20:30] = jnp.where(low, above, below)
    wide[30:40] = jnp.where(low, pltpu.roll(above, 64, 2), pltpu.roll(below, 64, 2))
    wide[40:] = jnp.where(even, pltpu.roll(more, 64, 2), more)


def inverse_diagonal(scale, mass, blocks, factor):
    square = scale * scale
    parts = []
    for comp in range(3):
        diag = factor * blocks[13 * 9 + comp * 4] * square + mass
        parts.append(jnp.where(scale > 0.0, 1.0 / diag, 0.0)[:, None])
    return jnp.concatenate(parts, axis=1)


def line_lanes(shape, count, above, more_above, more_below, below, seam):
    index = lax.axis_index("gx")
    even = lax.rem(index, 2) == 0
    odd = jnp.logical_not(even)
    lane = iota(shape, 1)
    end_above = more_above + (more_above - above) - jnp.where(index + 1 == count - 1, 0, seam)
    start_below = more_below + jnp.where(index - 1 == 0, 0, seam)

    def within(first, last, condition):
        return jnp.logical_and(jnp.logical_and(lane >= first, lane < last), condition)

    found = lane < above
    for part in (
        within(above, more_above - jnp.where(even, 0, seam), index < count - 1),
        within(more_above, end_above, even),
        within(start_below, below, odd),
        within(below + jnp.where(even, seam, 0), shape[1], index > 0),
    ):
        found = jnp.logical_or(found, part)
    return found


def largest(ratio, *lanes):
    width = ratio.shape[1]
    flat = jnp.max(ratio.reshape(-1, 8, width), axis=0)
    flat = jnp.where(line_lanes(flat.shape, *lanes), flat, -jnp.inf)
    return functools.reduce(jnp.maximum, [flat[:, at : at + 128] for at in range(0, width, 128)])


def clear_pads(ref):
    planes = ref.shape[0] - 2 * PAD
    for at in (0, planes + PAD):
        ref[at : at + PAD] = jnp.zeros((PAD,) + ref.shape[1:], F32)


def paired_planes(values):
    pairs = values.reshape((-1, 2) + values.shape[1:])
    return pairs[:, 0] + pairs[:, 1]


def paired_rows(held, values):
    parts, count = held.shape[0], held.shape[1] // 2
    for part in range(parts):
        held[part] = values[:, part * 128 : part * 128 + 128]
    return jnp.concatenate(
        [held[part, pl.ds(0, count, stride=2)] + held[part, pl.ds(1, count, stride=2)] for part in range(parts)], axis=1
    )


def window_kernel(
    gxs, gys, ordered, blocks, *refs
):
    (*blocks_in, fine_bound, mid_bound, coarse_bound, coarse_diag, gather_rows, squeeze_line, source_w, scale_w, mass_w, inverse_w,
     spread_1w, weight_1w, inverse_1w, spread_2w, weight_2w, inverse_2w, bounds, scale_x, mass_x, held) = refs
    planes, rows = scale_w.shape[0] - 2 * PAD, scale_w.shape[1]
    gz, gy = lax.axis_index("gz"), lax.axis_index("gy")
    even = lax.rem(lax.axis_index("gx"), 2) == 0
    low = iota((4, 8, 128), 2) < 64
    for at in (0, planes + 1):
        scale_x[at] = jnp.zeros((rows, LINE), F32)
    for ref in (source_w, inverse_w, scale_w, mass_w):
        clear_pads(ref)
    number = 0
    for ref in blocks_in:
        for block in range(ref.shape[0]):
            if ordered:
                place_z, place_y = number // gys, number % gys
            else:
                place_z = lax.bitwise_xor(gz, number // 4 + 2 * (number % 2))
                place_y = lax.bitwise_xor(gy, number % 4 // 2)
            at_z = pl.ds(PAD + 4 * place_z, 4)
            at_y = pl.ds(pl.multiple_of(8 * place_y, 8), 8)
            for half in (0, 1):
                lanes = slice(half * 128, half * 128 + 128)
                part = ref.at[block, half * 20 : half * 20 + 20]
                for comp in range(3):
                    source_w[at_z, comp, at_y, lanes] = part[comp * 4 : comp * 4 + 4]
                scale_w[at_z, at_y, lanes] = part[12:16]
                mass_w[at_z, at_y, lanes] = part[16:20]
            here, more = ref.at[block], ref[block, 40:44]
            turned_more = pltpu.roll(more, 64, 2)
            for target, own, start, at_low, at_high in (
                (scale_x, 12, 1, more, turned_more),
                (mass_x, 16, 0, turned_more, more),
            ):
                at_x = pl.ds(start + 4 * place_z, 4)
                halo = here[own + 20 : own + 24]
                target[at_x, at_y, :128] = here[own : own + 4]
                target[at_x, at_y, 128:256] = jnp.where(low, halo, jnp.where(even, at_high, 0.0))
                target[at_x, at_y, 256:] = jnp.where(low, jnp.where(even, 0.0, at_low), halo)
            number += 1

    scale, mass = scale_x[1 : 1 + planes], mass_x[...]
    inverse = inverse_diagonal(scale, mass, blocks, 1.0)
    inverse_w[PAD : PAD + planes, :, :, :128] = inverse[..., :128]
    wide_low = iota(inverse.shape[:3] + (128,), 3) < 64
    inverse_w[PAD : PAD + planes, :, :, 128:] = jnp.where(wide_low, inverse[..., 128:256], inverse[..., 256:])
    slab = 3 * rows
    outs = []
    at = 0
    for size in groups(planes, group_of(slab))[::2]:
        beside = []
        for _ in range(2):
            near = scale_x[at : at + size + 2].reshape((size + 2) * rows, LINE)
            if size < group_of(slab):
                near = jnp.concatenate([near, jnp.zeros(((group_of(slab) - size) * rows, LINE), F32)], axis=0)
            beside.append(near)
            at += size
        depth = 3 * (group_of(slab) + 2) * rows
        product = banded_stacked(fine_bound[: size * 3 * slab, :depth], jnp.concatenate(beside, axis=1))
        outs += [shifted_sum(product[:, half * LINE : half * LINE + LINE], size, slab, LINE) for half in (0, 1)]
    total = jnp.concatenate(outs, axis=0).reshape(planes, 3, rows, LINE)
    ratio = (scale[:, None] * total + mass[:, None]) * inverse
    bounds[0] = largest(ratio.reshape(planes * slab, LINE), gxs, 128, 192, 256, 320, 1)

    rows, planes = rows // 2, planes // 2
    slab = 3 * rows
    count = planes * rows
    pairs = [
        paired_rows(held.at[at], paired_planes(values).reshape(2 * count, LINE))
        for at, values in enumerate((scale, mass))
    ]
    middle = lanes_apply(jnp.concatenate(pairs, axis=0), squeeze_line[...])
    scale_1 = (middle[:count] * 0.125).reshape(planes, rows, 256)
    mass_1 = middle[count:].reshape(planes, rows, 256)
    inverse_1 = inverse_diagonal(scale_1, mass_1, blocks, 2.0).reshape(planes * slab, 256)
    spread_1 = jnp.broadcast_to(scale_1[:, None], (planes, 3, rows, 256)).reshape(planes * slab, 256)
    weight_1 = jnp.broadcast_to(mass_1[:, None], (planes, 3, rows, 256)).reshape(planes * slab, 256)
    total = banded_planes(mid_bound, spread_1, planes, 1)
    bounds[1] = largest((2.0 * spread_1 * total + weight_1) * inverse_1, gxs, 64, 96, 192, 224, 1)

    def window(values):
        return jnp.where(iota((values.shape[0], 128), 1) < 96, values[:, :128], values[:, 128:])

    spread_1w[...], weight_1w[...], inverse_1w[...] = window(spread_1), window(weight_1), window(inverse_1)

    both = rows_apply(gather_rows[...], jnp.concatenate([spread_1, weight_1], axis=1))
    spread_2 = paired_lanes(both[:, :256]) * 0.125
    weight_2 = paired_lanes(both[:, 256:])
    diag = jnp.concatenate([coarse_diag[...]] * 2, axis=1)
    inverse_2 = jnp.where(spread_2 > 0.0, 1.0 / (4.0 * diag * spread_2 * spread_2 + weight_2), 0.0)
    total = banded_planes(coarse_bound, spread_2, planes // 2, 2)
    bounds[2] = largest((4.0 * spread_2 * total + weight_2) * inverse_2, gxs, 64, 96, 192, 224, 2)
    spread_2w[...], weight_2w[...], inverse_2w[...] = window(spread_2), window(weight_2), window(inverse_2)


def inner_power(scale_w, mass_w, inverse_w, matrix, values, finish):
    planes, rows = scale_w.shape[0] - 2 * PAD, scale_w.shape[1]
    fine_operator(
        matrix,
        lambda i: scale_w[PAD + i],
        lambda i: mass_w[PAD + i],
        lambda i: scale_w[PAD + i][None] * (inverse_w[PAD + i] * values[PAD + i]),
        lambda i: inverse_w[PAD + i] * values[PAD + i],
        planes,
        rows,
        finish,
    )


def powers_kernel(scale_w, mass_w, inverse_w, source_w, fine, squeeze, power_1, basis, power_2, held):
    planes, rows = scale_w.shape[0] - 2 * PAD, scale_w.shape[1]
    third = []
    for source, target in ((source_w, power_1), (power_1, power_2)):
        clear_pads(target)

        def finish(at, values, target=target):
            target[PAD + at] = values

        inner_power(scale_w, mass_w, inverse_w, fine, source, finish)
    inner_power(scale_w, mass_w, inverse_w, fine, power_2, lambda at, values: third.append(values))
    inner = slice(PAD, PAD + planes)
    size = planes // 2 * 3 * rows
    pairs = []
    for at, values in enumerate((source_w[inner], power_1[inner], power_2[inner], jnp.stack(third, axis=0))):
        pairs.append(paired_rows(held.at[at], paired_planes(values).reshape(size, LANES)))
    restricted = lanes_apply(jnp.concatenate(pairs, axis=0), squeeze[...])
    for at in range(4):
        basis[at] = restricted[at * size // 2 : (at + 1) * size // 2]


def chebyshev_constants(ratio, degree):
    sigma = (ratio + 1.0) / (ratio - 1.0)
    rho = 1.0 / sigma
    steps = []
    for _ in range(degree - 1):
        rho_next = 1.0 / (2.0 * sigma - rho)
        steps.append((rho_next * rho, 4.0 * rho_next / (1.0 - 1.0 / ratio)))
        rho = rho_next
    return 2.0 / (1.0 + 1.0 / ratio), steps


def chebyshev(residue, degree, inverse, ratio, operate, keep):
    first, steps = chebyshev_constants(ratio, degree)
    direction = first * (inverse * residue)
    total = direction
    for hold, push in steps:
        residue = residue - operate(direction)
        direction = hold * direction + push * (inverse * residue)
        total = total + direction
    if keep:
        residue = residue - operate(direction)
    return total, residue


def scaled(coeff, values):
    lanes = values.shape[-1]
    if lanes != 128:
        coeff = jnp.concatenate([coeff] * (lanes // 128), axis=1)
    flat = values.reshape(-1, 8, lanes)
    return (coeff[None] * flat).reshape(values.shape)


def final_kernel(
    bounds_a, bounds_b, source_w, scale_w, mass_w, inverse_w, power_1, basis,
    spread_1w, weight_1w, inverse_1w, spread_2w, weight_2w, inverse_2w,
    fine, fine_own, mid, coarse, gather_rows, spread_rows, stretch, result, lifted_w, doubled_w,
):
    rows = scale_w.shape[1] // 2
    planes = (scale_w.shape[0] - 2 * PAD) // 2
    slab = 3 * rows
    gz = lax.axis_index("gz")
    worst = jnp.maximum(bounds_a[...], bounds_b[...])
    inverse_bounds = [1.0 / jnp.full((8, 128), jnp.max(worst[level]), F32) for level in range(3)]
    over_0 = inverse_bounds[0]

    first, ((hold, push),) = chebyshev_constants(SMOOTH_RATIO, 2)
    beta = push * first
    gamma = first * (1.0 + hold) + push
    omega = 4.0 / 3.0
    source_1 = basis[0] - scaled(
        over_0,
        (gamma + omega) * basis[1]
        - scaled(over_0, (beta + omega * gamma) * basis[2] - scaled(over_0, (omega * beta) * basis[3])),
    )

    spread_1, weight_1 = spread_1w[...], weight_1w[...]
    spread_2, weight_2 = spread_2w[...], weight_2w[...]
    inverse_1 = scaled(inverse_bounds[1], inverse_1w[...])
    inverse_2 = scaled(inverse_bounds[2], inverse_2w[...])
    double_1, double_2 = 2.0 * spread_1, 4.0 * spread_2

    def operate_1(values):
        return double_1 * banded_planes(mid, spread_1 * values, planes, 1) + weight_1 * values

    def operate_2(values):
        return double_2 * banded_planes(coarse, spread_2 * values, planes // 2, 2) + weight_2 * values

    iterate, residue = chebyshev(source_1, 2, inverse_1, SMOOTH_RATIO, operate_1, True)
    smoothed = residue - omega * operate_1(inverse_1 * residue)
    source_2 = paired_lanes(rows_apply(gather_rows[...], smoothed))
    error_2, _ = chebyshev(source_2, COARSE_ITERS, inverse_2, COARSE_RATIO, operate_2, False)
    lifted = dot(spread_rows[...], jnp.concatenate(split(error_2), axis=0))
    iterate = iterate + lifted - omega * (inverse_1 * operate_1(lifted))
    residue = source_1 - operate_1(iterate)
    more, _ = chebyshev(residue, 2, inverse_1, SMOOTH_RATIO, operate_1, False)
    error_1 = iterate + more

    lifted_w[0:2] = jnp.zeros((2, slab, 128), F32)
    lifted_w[planes + 2 : planes + 4] = jnp.zeros((2, slab, 128), F32)
    lifted_w[2 : planes + 2] = error_1.reshape(planes, slab, 128)
    near = lifted_w[pl.ds(2 * gz, 6)].reshape(6 * slab, 128)
    wide = lanes_apply(near, stretch[...])
    for half in (0, 1):
        for odd in (0, 1):
            doubled_w[half, pl.ds(odd, 6 * slab, stride=2)] = wide[:, half * 128 : half * 128 + 128]
    slabs = jnp.concatenate([doubled_w[0], doubled_w[1]], axis=1).reshape(6, 3, 2 * rows, LANES)
    error = jnp.stack([slabs[(plane + 1) // 2] for plane in range(10)], axis=0)

    def near_own(ref, reach):
        return ref[pl.ds(4 * gz + PAD - reach, 4 + 2 * reach)]

    scale, mass = near_own(scale_w, 3), near_own(mass_w, 2)
    inverse = scaled(over_0, near_own(inverse_w, 2))
    source = near_own(source_w, 2)
    before = gamma * source - scaled(over_0, beta * near_own(power_1, 2))

    def apply(values, edge):
        outs = []
        fine_operator(
            fine,
            lambda i: scale[i + 4 - edge],
            lambda i: mass[i + 3 - edge],
            lambda i: scale[i + 4 - edge][None] * values[i + 1],
            lambda i: values[i + 1],
            2 + 2 * edge,
            2 * rows,
            lambda at, result: outs.append(result),
        )
        return jnp.stack(outs, axis=0)

    image = apply(error, 3)
    iterate = inverse * (before - omega * image) + error[1:9]
    residue = source[1:7] - apply(iterate, 2)
    direction = first * (inverse[1:7] * residue)

    def own(values):
        return own_rows(values, 2 * rows // 8)

    for plane in range(4):
        near = [split((scale[plane + 2 + i][None] * direction[plane + i]).reshape(6 * rows, LANES)) for i in range(3)]
        stacked = jnp.concatenate([part[0] for part in near] * 2 + [part[1] for part in near], axis=0)
        product = dot(fine_own[:, : 18 * slab], stacked)
        total = shifted_sum(product, 1, 24, LANES).reshape(3, 8, LANES)[..., :128]
        here = own(direction[plane + 1])[..., :128]
        image = own(scale[plane + 3])[None, :, :128] * total + own(mass[plane + 2])[None, :, :128] * here
        last = own(residue[plane + 1])[..., :128] - image
        answer = own(iterate[plane + 2])[..., :128] + (1.0 + hold) * here
        result[:, plane] = answer + push * (own(inverse[plane + 2])[..., :128] * last)


def swap_pairs(counts, target):
    def number(place):
        return (place[0] * counts[1] + place[1]) * counts[2] + place[2]

    places = [(x, y, z) for x in range(counts[0]) for y in range(counts[1]) for z in range(counts[2])]
    return [(number(place), number(target(*place))) for place in places]


def odd_partner(index):
    return index - 1 if index % 2 == 0 else index + 1


def on_device(right_side, stiff_scale, nodal_mass, stencil_blocks):
    counts = tuple(lax.axis_size(axis) for axis in AXES)
    gxs, gys, gzs = counts
    blocks = stencil_blocks.reshape(243)

    def send(values, target):
        return lax.ppermute(values, AXES, swap_pairs(counts, target))

    def x_second(x, y, z):
        return (x, y, z ^ 1) if x in (0, gxs - 1) else (odd_partner(x), y, z)

    rows, planes = 8 * gys, 4 * gzs
    grant = 20 if planes * rows <= 256 else 48
    slab = 3 * rows
    group = group_of(slab)
    size_1 = planes * slab // 4
    size = coarse_slab(rows // 4)
    size_2 = planes // 4 * size
    (
        fine, fine_own, fine_bound, mid, mid_bound, coarse, coarse_bound, coarse_diag, gather_rows, spread_rows, squeeze,
        squeeze_line, stretch,
    ) = call(
        functools.partial(matrices_kernel, rows, planes),
        [
            ((3 * slab, up128(9 * slab)), BF16),
            ((72, up128(9 * slab)), BF16),
            ((group * 3 * slab, up128(3 * (group + 2) * rows)), BF16),
            ((3 * slab // 2, up128(9 * slab // 2)), BF16),
            ((3 * slab // 2, up128(9 * slab // 2)), BF16),
            ((3 * size, up128(9 * size)), BF16),
            ((3 * size, up128(9 * size)), BF16),
            ((size_2, 128), F32),
            ((size_2, size_1), BF16),
            ((size_1, 2 * size_2), BF16),
            ((2 * LANES, 128), BF16),
            ((2 * LINE, 256), BF16),
            ((256, LANES), BF16),
        ],
        specs=[SM],
        flops=5000000000,
        size=8000000,
        grant=grant,
    )(blocks)

    half = ((14, 8, 128), F32)
    main = jnp.concatenate([right_side.reshape(12, 8, 128), stiff_scale, nodal_mass], axis=0)
    send_a, send_b = call(pack_kernel, [half, half], grant=8)(main)
    got_b = send(send_b, x_second)
    got_a = send(send_a, lambda x, y, z: (x ^ 1, y, z))
    (wide,) = call(functools.partial(widen_kernel, gxs), [((44, 8, 128), F32)], grant=8)(main, got_b, got_a)
    ordered = not (gys == 2 and gzs == 4)
    if ordered:
        gathered = [lax.all_gather(wide, ("gz", "gy"), tiled=False)]
    else:
        near = [
            wide,
            send(wide, lambda x, y, z: (x, y, z ^ 2)),
            send(wide, lambda x, y, z: (x, y ^ 1, z)),
            send(wide, lambda x, y, z: (x, y ^ 1, z ^ 2)),
        ]
        near[3], fine = lax.optimization_barrier((near[3], fine))
        gathered = [block[None] for block in near + [send(block, lambda x, y, z: (x, y, z ^ 1)) for block in near]]

    field = ((planes + 2 * PAD, 3, rows, LANES), F32)
    single = ((planes + 2 * PAD, rows, LANES), F32)
    source_w, scale_w, mass_w, inverse_w, *levels, bounds = call(
        functools.partial(window_kernel, gxs, gys, ordered),
        [field, single, single, field] + [((size_1, 128), F32)] * 3 + [((size_2, 128), F32)] * 3 + [((3, 8, 128), F32)],
        specs=[SM] + [VM] * (len(gathered) + 6),
        scratch=[
            pltpu.VMEM((planes + 2, rows, LINE), F32),
            pltpu.VMEM((planes, rows, LINE), F32),
            pltpu.VMEM((2, LINE // 128, planes * rows // 2, 128), F32),
        ],
        grant=grant,
    )(blocks, *gathered, fine_bound, mid_bound, coarse_bound, coarse_diag, gather_rows, squeeze_line)

    step, other = 2, bounds
    while step < gxs:
        bounds = jnp.maximum(bounds, other)
        other = send(bounds, lambda x, y, z: (x ^ step, y, z ^ 1))
        step *= 2
    power_1, basis = call(
        powers_kernel,
        [field, ((4, size_1, 128), F32)],
        scratch=[pltpu.VMEM(*field), pltpu.VMEM((4, 2, 2 * size_1, 128), F32)],
        flops=3000000000,
        size=12000000,
        grant=grant,
    )(scale_w, mass_w, inverse_w, source_w, fine, squeeze)
    (result,) = call(
        final_kernel,
        [(right_side.shape, F32)],
        scratch=[
            pltpu.VMEM((planes // 2 + 4, slab // 2, 128), F32),
            pltpu.VMEM((2, 6 * slab, 128), F32),
        ],
        grant=grant,
    )(
        bounds, other, source_w, scale_w, mass_w, inverse_w, power_1, basis, *levels,
        fine, fine_own, mid, coarse, gather_rows, spread_rows, stretch,
    )
    return result


def solution(mesh):
    placed = (P(None, "gz", "gy", "gx"), P("gz", "gy", "gx"), P("gz", "gy", "gx"), P())
    return jax.shard_map(
        on_device, mesh=mesh, in_specs=placed, out_specs=P(None, "gz", "gy", "gx"), check_vma=False
    )
```

```python
import functools

import jax
import jax.numpy as jnp
from jax import lax
from jax.experimental import pallas as pl
from jax.experimental.pallas import tpu as pltpu
from jax.sharding import PartitionSpec as P

AXES = ("gx", "gy", "gz")
COARSE_ITERS = 8
SMOOTH_RATIO = 20.0
COARSE_RATIO = 200.0
F32, BF16 = jnp.float32, jnp.bfloat16
VM = pl.BlockSpec(memory_space=pltpu.VMEM)
SM = pl.BlockSpec(memory_space=pltpu.SMEM)
LANES = 256
LINE = 384
FREE, PIECES = 52, (0, 25, 79, 104)
PAD = 3


def call(kernel, outs, specs=None, scratch=(), flops=1000000, size=100000, grant=None):
    params = pltpu.CompilerParams(vmem_limit_bytes=grant * 1024 * 1024) if grant else None
    outs = [jax.ShapeDtypeStruct(shape, dtype) for shape, dtype in outs]

    def run(*args):
        return pl.pallas_call(
            kernel,
            out_shape=outs,
            in_specs=specs or [VM] * len(args),
            out_specs=[VM] * len(outs),
            scratch_shapes=scratch,
            compiler_params=params,
            cost_estimate=pl.CostEstimate(flops=flops, bytes_accessed=size, transcendentals=0),
        )(*args)

    return run


def iota(shape, dim):
    return lax.broadcasted_iota(jnp.int32, shape, dim)


def ones_where(mask):
    return jnp.where(mask, 1.0, 0.0).astype(BF16)


def split(values):
    high = values.astype(BF16)
    return high, (values - high.astype(F32)).astype(BF16)


def dot(left, right):
    return jnp.dot(left, right, preferred_element_type=F32)


def lanes_apply(values, stacked):
    return dot(jnp.concatenate(split(values), axis=1), stacked)


def rows_apply(selection, values):
    width = values.shape[1]
    product = dot(selection, jnp.concatenate(split(values), axis=1))
    return product[:, :width] + product[:, width:]


def banded_stacked(matrix, values):
    high, low = split(values)
    return dot(matrix, jnp.concatenate([high, high, low], axis=0))


def banded_planes(matrix, values, planes, step):
    slab, lanes = values.shape[0] // planes, values.shape[1]
    edge = jnp.zeros((slab, lanes), F32)
    padded = jnp.concatenate([edge, values, edge], axis=0)
    beside = jnp.concatenate([padded[at * slab : (at + 3) * slab] for at in range(planes)], axis=1)
    high = beside.astype(BF16).astype(F32)
    stacked = jnp.concatenate([high, high, beside - high], axis=0).astype(BF16)
    product = dot(matrix[:, : 9 * slab], stacked)
    outs = []
    for at in range(planes):
        below, here, above = (
            product[part * slab : part * slab + slab, at * lanes : at * lanes + lanes] for part in range(3)
        )
        outs.append(here + pltpu.roll(below, step, 1) + pltpu.roll(above, lanes - step, 1))
    return jnp.concatenate(outs, axis=0)


def paired_lanes(values):
    even = iota(values.shape, 1) % 2 == 0
    return values + jnp.where(even, pltpu.roll(values, values.shape[1] - 1, 1), pltpu.roll(values, 1, 1))


def shifted_sum(product, slabs, rows, lanes):
    parts = product.reshape(slabs, 3, rows, lanes)
    below = parts[:, 0].reshape(slabs * rows, lanes)
    above = parts[:, 2].reshape(slabs * rows, lanes)
    here = parts[:, 1].reshape(slabs * rows, lanes)
    return here + pltpu.roll(below, 1, 1) + pltpu.roll(above, lanes - 1, 1)


def group_of(slab):
    return max(1, 256 // slab - 2)


def groups(planes, most):
    sizes = []
    half = planes // 2
    while half:
        size = min(most, half)
        sizes += [size, size]
        half -= size
    return sizes


def fine_operator(matrix, scale_of, mass_of, weighted_of, value_of, planes, rows, finish):
    slab = 3 * rows
    parts = {}
    for plane in range(planes):
        near = range(plane - 1, plane + 2)
        for i in near:
            if i not in parts:
                parts[i] = split(weighted_of(i).reshape(slab, LANES))
        high = [parts[i][0] for i in near]
        low = [parts[i][1] for i in near]
        product = dot(matrix[:, : 9 * slab], jnp.concatenate(high + high + low, axis=0))
        total = shifted_sum(product, 1, slab, LANES).reshape(3, rows, LANES)
        finish(plane, scale_of(plane)[None] * total + mass_of(plane)[None] * value_of(plane))


def panels(value_of, others, rows, width):
    column = iota((8, width), 1)
    which = column // rows
    row_in = column % rows
    result = {}
    for step_x in range(3):
        for comp in range(3):
            coeffs = []
            for step_y in range(3):
                coeff = jnp.zeros((8, width), F32)
                for plane in range(3):
                    for other in range(others):
                        value = value_of(plane * 9 + step_y * 3 + step_x, comp, other)
                        coeff = jnp.where(which == plane * others + other, value, coeff)
                coeffs.append(coeff)
            pieces = []
            for block in range(rows // 8):
                gap = row_in - (iota((8, width), 0) + block * 8)
                piece = jnp.zeros((8, width), F32)
                for step_y in range(3):
                    piece = jnp.where(gap == step_y - 1, coeffs[step_y], piece)
                pieces.append(piece)
            result[step_x, comp] = jnp.concatenate(pieces, axis=0)
    return result


def turned(value, turn):
    turn %= value.shape[1]
    return pltpu.roll(value, turn, 1) if turn else value


def parts_of(value):
    high = value.astype(BF16).astype(F32)
    return high, value - high


def stack3(value, size):
    high, low = parts_of(value)
    return (high + turned(low, size) + turned(high, 2 * size)).astype(BF16)


def up128(size):
    return -(-size // 128) * 128


def coarse_slab(few):
    return -(-3 * few // 16) * 16


def own_rows(values, count):
    index = lax.axis_index("gy")
    found = values[..., :8, :]
    for block in range(1, count):
        found = jnp.where(index == block, values[..., block * 8 : block * 8 + 8, :], found)
    return found


def matrices_kernel(
    rows, planes, blocks, fine, fine_own, fine_bound, mid, mid_bound, coarse, coarse_bound, coarse_diag,
    gather_rows, spread_rows, squeeze, squeeze_line, stretch,
):
    def direct(offset, comp, other):
        return blocks[offset * 9 + comp * 3 + other]

    def absolute(offset, comp, other):
        at = offset * 9 + comp * 3
        return jnp.abs(blocks[at]) + jnp.abs(blocks[at + 1]) + jnp.abs(blocks[at + 2])

    slab = 3 * rows
    group = group_of(slab)
    width = up128(3 * slab)
    found = panels(direct, 3, rows, width)
    every = [found[step_x, comp] for step_x in range(3) for comp in range(3)]
    for target, parts in ((fine, every), (fine_own, [own_rows(part, rows // 8) for part in every])):
        value = jnp.concatenate(parts, axis=0)
        if target.shape[1] > width:
            value = jnp.concatenate([value, jnp.zeros((value.shape[0], target.shape[1] - width), F32)], axis=1)
        target[...] = stack3(value, 3 * slab)
    bound = panels(absolute, 1, rows, fine_bound.shape[1])
    for plane in range(group):
        for step_x in range(3):
            start = (plane * 3 + step_x) * slab
            value = turned(jnp.concatenate([bound[step_x, comp] for comp in range(3)], axis=0), plane * rows)
            fine_bound[start : start + slab, :] = stack3(value, (group + 2) * rows)

    rows, planes = rows // 2, planes // 2
    slab = 3 * rows
    found = panels(direct, 3, rows, mid.shape[1])
    whole = jnp.concatenate([found[step_x, comp] for step_x in range(3) for comp in range(3)], axis=0)
    few, half = rows // 2, planes // 2
    size = coarse_slab(few)

    def choose(out, source):
        place = out % size
        wanted = out // size * slab + place // few * rows + place % few
        return ones_where(jnp.logical_and(source == wanted, place < 3 * few))

    shape = (3 * size, 3 * slab)
    choose_rows = choose(iota(shape, 0), iota(shape, 1))
    shape = (mid.shape[1], up128(3 * size))
    choose_columns = jnp.where(iota(shape, 1) < 3 * size, choose(iota(shape, 1), iota(shape, 0)), 0.0).astype(BF16)

    def smaller(matrix):
        return dot(dot(choose_rows, matrix.astype(BF16)).astype(BF16), choose_columns)

    for target, small_target, value in ((mid, coarse, whole), (mid_bound, coarse_bound, jnp.abs(whole))):
        target[...] = stack3(value, 3 * slab)
        high, low = parts_of(value)
        high, low = smaller(high), smaller(low)
        width = small_target.shape[1]
        if width > high.shape[1]:
            more = jnp.zeros((3 * size, width - high.shape[1]), F32)
            high, low = jnp.concatenate([high, more], axis=1), jnp.concatenate([low, more], axis=1)
        small_target[...] = (high + turned(low, 3 * size) + turned(high, 6 * size)).astype(BF16)
    comp = iota((half * size, 128), 0) % size // few
    diag = [blocks[13 * 9 + 4 * at] for at in range(3)]
    coarse_diag[...] = jnp.where(comp == 0, diag[0], jnp.where(comp == 1, diag[1], diag[2]))

    def same_aggregate(small, large):
        place, inner = small % size, large % slab
        same = jnp.logical_and(small // size == large // (2 * slab), place // few == inner // rows)
        return jnp.logical_and(same, place % few == inner % rows // 2)

    shape = (half * size, planes * slab)
    gather_rows[...] = ones_where(same_aggregate(iota(shape, 0), iota(shape, 1)))
    shape = (planes * slab, 2 * half * size)
    spread_rows[...] = ones_where(same_aggregate(iota(shape, 1) % (half * size), iota(shape, 0)))
    shape = (2 * LANES, 128)
    squeeze[...] = ones_where(iota(shape, 0) % LANES // 2 == iota(shape, 1))
    shape = (2 * LINE, 256)
    lane = iota(shape, 0) % LINE
    squeeze_line[...] = ones_where(jnp.where(lane < 256, lane // 2, lane // 2 + 64) == iota(shape, 1))
    shape = (256, LANES)
    stretch[...] = ones_where(iota(shape, 0) % 128 == iota(shape, 1) // 2)


def halves(planes):
    count = planes.shape[0] // 2
    low = iota((count, 8, 128), 2) < 64
    first, second = planes[:count], pltpu.roll(planes[count:], 64, 2)
    return jnp.where(low, second, first), jnp.where(low, first, second)


def pack_kernel(main, send_a, send_b):
    high, low = halves(main[...])
    more_high, more_low = halves(main[12:])
    even = lax.rem(lax.axis_index("gx"), 2) == 0
    send_a[:10] = jnp.where(even, high, low)
    send_a[10:] = jnp.where(even, more_low, more_high)
    send_b[:10] = jnp.where(even, low, high)
    send_b[10:] = jnp.zeros((4, 8, 128), F32)


def widen_kernel(count, main, got_b, got_a, wide):
    index = lax.axis_index("gx")
    even = lax.rem(index, 2) == 0
    first, second, more = got_a[:10], got_b[:10], got_a[10:]
    above = jnp.where(index < count - 1, jnp.where(even, first, second), 0.0)
    below = jnp.where(index > 0, jnp.where(even, second, first), 0.0)
    low = iota((10, 8, 128), 2) < 64
    wide[:20] = main[...]
    halo = jnp.concatenate(
        [jnp.where(low, above, below), jnp.where(low, pltpu.roll(above, 64, 2), pltpu.roll(below, 64, 2))], axis=0
    )
    lane = iota((8, 128), 1)
    free = jnp.logical_and(lane >= FREE, lane < FREE + 25)
    for guest in range(2):
        for piece, start in enumerate(PIECES):
            moved = pltpu.roll(halo[8 + guest], (FREE - start) % 128, 1)
            wide[20 + guest * 4 + piece] = jnp.where(free, moved, halo[guest * 4 + piece])
    wide[28:38] = halo[10:]
    wide[38:] = jnp.where(even, pltpu.roll(more, 64, 2), more)


def inverse_diagonal(scale, mass, blocks, factor):
    square = scale * scale
    parts = []
    for comp in range(3):
        diag = factor * blocks[13 * 9 + comp * 4] * square + mass
        parts.append(jnp.where(scale > 0.0, 1.0 / diag, 0.0)[:, None])
    return jnp.concatenate(parts, axis=1)


def line_lanes(shape, count, above, more_above, more_below, below, seam):
    index = lax.axis_index("gx")
    even = lax.rem(index, 2) == 0
    odd = jnp.logical_not(even)
    lane = iota(shape, 1)
    end_above = more_above + (more_above - above) - jnp.where(index + 1 == count - 1, 0, seam)
    start_below = more_below + jnp.where(index - 1 == 0, 0, seam)

    def within(first, last, condition):
        return jnp.logical_and(jnp.logical_and(lane >= first, lane < last), condition)

    found = lane < above
    for part in (
        within(above, more_above - jnp.where(even, 0, seam), index < count - 1),
        within(more_above, end_above, even),
        within(start_below, below, odd),
        within(below + jnp.where(even, seam, 0), shape[1], index > 0),
    ):
        found = jnp.logical_or(found, part)
    return found


def largest(ratio, *lanes):
    width = ratio.shape[1]
    flat = jnp.max(ratio.reshape(-1, 8, width), axis=0)
    flat = jnp.where(line_lanes(flat.shape, *lanes), flat, -jnp.inf)
    return functools.reduce(jnp.maximum, [flat[:, at : at + 128] for at in range(0, width, 128)])


def clear_pads(ref):
    planes = ref.shape[0] - 2 * PAD
    for at in (0, planes + PAD):
        ref[at : at + PAD] = jnp.zeros((PAD,) + ref.shape[1:], F32)


def paired_planes(values):
    pairs = values.reshape((-1, 2) + values.shape[1:])
    return pairs[:, 0] + pairs[:, 1]


def paired_rows(held, values):
    parts, count = held.shape[0], held.shape[1] // 2
    for part in range(parts):
        held[part] = values[:, part * 128 : part * 128 + 128]
    return jnp.concatenate(
        [held[part, pl.ds(0, count, stride=2)] + held[part, pl.ds(1, count, stride=2)] for part in range(parts)], axis=1
    )


def window_kernel(
    gxs, gys, ordered, blocks, *refs
):
    (*blocks_in, fine_bound, mid_bound, coarse_bound, coarse_diag, gather_rows, squeeze_line, source_w, scale_w, mass_w, inverse_w,
     spread_1w, weight_1w, inverse_1w, spread_2w, weight_2w, inverse_2w, bounds, scale_x, mass_x, held) = refs
    planes, rows = scale_w.shape[0] - 2 * PAD, scale_w.shape[1]
    gz, gy = lax.axis_index("gz"), lax.axis_index("gy")
    even = lax.rem(lax.axis_index("gx"), 2) == 0
    low = iota((4, 8, 128), 2) < 64
    lane = iota((8, 128), 1)
    for at in (0, planes + 1):
        scale_x[at] = jnp.zeros((rows, LINE), F32)
    for ref in (source_w, inverse_w, scale_w, mass_w):
        clear_pads(ref)
    number = 0
    for ref in blocks_in:
        for block in range(ref.shape[0]):
            if ordered:
                place_z, place_y = number // gys, number % gys
            else:
                place_z = lax.bitwise_xor(gz, number // 4 + 2 * (number % 2))
                place_y = lax.bitwise_xor(gy, number % 4 // 2)
            at_z = pl.ds(PAD + 4 * place_z, 4)
            at_y = pl.ds(pl.multiple_of(8 * place_y, 8), 8)
            here, more = ref.at[block], ref[block, 38:42]
            for comp in range(3):
                source_w[at_z, comp, at_y, :128] = here[comp * 4 : comp * 4 + 4]
            for comp in range(2):
                source_w[at_z, comp, at_y, 128:] = here[20 + comp * 4 : 24 + comp * 4]
            source_w[pl.ds(PAD + 4 * place_z + 2, 2), 2, at_y, 128:] = here[28:30]
            for guest in range(2):
                found = here[20 + guest * 4]
                for piece, start in enumerate(PIECES):
                    back = pltpu.roll(here[20 + guest * 4 + piece], (start - FREE) % 128, 1)
                    found = jnp.where(lane >= (0, 25, 64, 104)[piece], back, found)
                source_w[PAD + 4 * place_z + guest, 2, at_y, 128:] = found
            scale_w[at_z, at_y, :128], scale_w[at_z, at_y, 128:] = here[12:16], here[30:34]
            mass_w[at_z, at_y, :128], mass_w[at_z, at_y, 128:] = here[16:20], here[34:38]
            turned_more = pltpu.roll(more, 64, 2)
            for target, own, start, at_low, at_high in (
                (scale_x, 12, 1, more, turned_more),
                (mass_x, 16, 0, turned_more, more),
            ):
                at_x = pl.ds(start + 4 * place_z, 4)
                halo = here[own + 18 : own + 22]
                target[at_x, at_y, :128] = here[own : own + 4]
                target[at_x, at_y, 128:256] = jnp.where(low, halo, jnp.where(even, at_high, 0.0))
                target[at_x, at_y, 256:] = jnp.where(low, jnp.where(even, 0.0, at_low), halo)
            number += 1

    scale, mass = scale_x[1 : 1 + planes], mass_x[...]
    inverse = inverse_diagonal(scale, mass, blocks, 1.0)
    inverse_w[PAD : PAD + planes, :, :, :128] = inverse[..., :128]
    wide_low = iota(inverse.shape[:3] + (128,), 3) < 64
    inverse_w[PAD : PAD + planes, :, :, 128:] = jnp.where(wide_low, inverse[..., 128:256], inverse[..., 256:])
    slab = 3 * rows
    outs = []
    at = 0
    for size in groups(planes, group_of(slab))[::2]:
        beside = []
        for _ in range(2):
            near = scale_x[at : at + size + 2].reshape((size + 2) * rows, LINE)
            if size < group_of(slab):
                near = jnp.concatenate([near, jnp.zeros(((group_of(slab) - size) * rows, LINE), F32)], axis=0)
            beside.append(near)
            at += size
        depth = 3 * (group_of(slab) + 2) * rows
        product = banded_stacked(fine_bound[: size * 3 * slab, :depth], jnp.concatenate(beside, axis=1))
        outs += [shifted_sum(product[:, half * LINE : half * LINE + LINE], size, slab, LINE) for half in (0, 1)]
    total = jnp.concatenate(outs, axis=0).reshape(planes, 3, rows, LINE)
    ratio = (scale[:, None] * total + mass[:, None]) * inverse
    bounds[0] = largest(ratio.reshape(planes * slab, LINE), gxs, 128, 192, 256, 320, 1)

    rows, planes = rows // 2, planes // 2
    slab = 3 * rows
    count = planes * rows
    pairs = [
        paired_rows(held.at[at], paired_planes(values).reshape(2 * count, LINE))
        for at, values in enumerate((scale, mass))
    ]
    middle = lanes_apply(jnp.concatenate(pairs, axis=0), squeeze_line[...])
    scale_1 = (middle[:count] * 0.125).reshape(planes, rows, 256)
    mass_1 = middle[count:].reshape(planes, rows, 256)
    inverse_1 = inverse_diagonal(scale_1, mass_1, blocks, 2.0).reshape(planes * slab, 256)
    spread_1 = jnp.broadcast_to(scale_1[:, None], (planes, 3, rows, 256)).reshape(planes * slab, 256)
    weight_1 = jnp.broadcast_to(mass_1[:, None], (planes, 3, rows, 256)).reshape(planes * slab, 256)
    total = banded_planes(mid_bound, spread_1, planes, 1)
    bounds[1] = largest((2.0 * spread_1 * total + weight_1) * inverse_1, gxs, 64, 96, 192, 224, 1)

    def window(values):
        return jnp.where(iota((values.shape[0], 128), 1) < 96, values[:, :128], values[:, 128:])

    spread_1w[...], weight_1w[...], inverse_1w[...] = window(spread_1), window(weight_1), window(inverse_1)

    both = rows_apply(gather_rows[...], jnp.concatenate([spread_1, weight_1], axis=1))
    spread_2 = paired_lanes(both[:, :256]) * 0.125
    weight_2 = paired_lanes(both[:, 256:])
    diag = jnp.concatenate([coarse_diag[...]] * 2, axis=1)
    inverse_2 = jnp.where(spread_2 > 0.0, 1.0 / (4.0 * diag * spread_2 * spread_2 + weight_2), 0.0)
    total = banded_planes(coarse_bound, spread_2, planes // 2, 2)
    bounds[2] = largest((4.0 * spread_2 * total + weight_2) * inverse_2, gxs, 64, 96, 192, 224, 2)
    spread_2w[...], weight_2w[...], inverse_2w[...] = window(spread_2), window(weight_2), window(inverse_2)


def inner_power(scale_w, mass_w, inverse_w, matrix, values, finish):
    planes, rows = scale_w.shape[0] - 2 * PAD, scale_w.shape[1]
    fine_operator(
        matrix,
        lambda i: scale_w[PAD + i],
        lambda i: mass_w[PAD + i],
        lambda i: scale_w[PAD + i][None] * (inverse_w[PAD + i] * values[PAD + i]),
        lambda i: inverse_w[PAD + i] * values[PAD + i],
        planes,
        rows,
        finish,
    )


def powers_kernel(scale_w, mass_w, inverse_w, source_w, fine, squeeze, power_1, basis, power_2, held):
    planes, rows = scale_w.shape[0] - 2 * PAD, scale_w.shape[1]
    third = []
    for source, target in ((source_w, power_1), (power_1, power_2)):
        clear_pads(target)

        def finish(at, values, target=target):
            target[PAD + at] = values

        inner_power(scale_w, mass_w, inverse_w, fine, source, finish)
    inner_power(scale_w, mass_w, inverse_w, fine, power_2, lambda at, values: third.append(values))
    inner = slice(PAD, PAD + planes)
    size = planes // 2 * 3 * rows
    pairs = []
    for at, values in enumerate((source_w[inner], power_1[inner], power_2[inner], jnp.stack(third, axis=0))):
        pairs.append(paired_rows(held.at[at], paired_planes(values).reshape(size, LANES)))
    restricted = lanes_apply(jnp.concatenate(pairs, axis=0), squeeze[...])
    for at in range(4):
        basis[at] = restricted[at * size // 2 : (at + 1) * size // 2]


def chebyshev_constants(ratio, degree):
    sigma = (ratio + 1.0) / (ratio - 1.0)
    rho = 1.0 / sigma
    steps = []
    for _ in range(degree - 1):
        rho_next = 1.0 / (2.0 * sigma - rho)
        steps.append((rho_next * rho, 4.0 * rho_next / (1.0 - 1.0 / ratio)))
        rho = rho_next
    return 2.0 / (1.0 + 1.0 / ratio), steps


def chebyshev(residue, degree, inverse, ratio, operate, keep):
    first, steps = chebyshev_constants(ratio, degree)
    direction = first * (inverse * residue)
    total = direction
    for hold, push in steps:
        residue = residue - operate(direction)
        direction = hold * direction + push * (inverse * residue)
        total = total + direction
    if keep:
        residue = residue - operate(direction)
    return total, residue


def scaled(coeff, values):
    lanes = values.shape[-1]
    if lanes != 128:
        coeff = jnp.concatenate([coeff] * (lanes // 128), axis=1)
    flat = values.reshape(-1, 8, lanes)
    return (coeff[None] * flat).reshape(values.shape)


def final_kernel(
    bounds_a, bounds_b, source_w, scale_w, mass_w, inverse_w, power_1, basis,
    spread_1w, weight_1w, inverse_1w, spread_2w, weight_2w, inverse_2w,
    fine, fine_own, mid, coarse, gather_rows, spread_rows, stretch, result, lifted_w, doubled_w,
):
    rows = scale_w.shape[1] // 2
    planes = (scale_w.shape[0] - 2 * PAD) // 2
    slab = 3 * rows
    gz = lax.axis_index("gz")
    worst = jnp.maximum(bounds_a[...], bounds_b[...])
    inverse_bounds = [1.0 / jnp.full((8, 128), jnp.max(worst[level]), F32) for level in range(3)]
    over_0 = inverse_bounds[0]

    first, ((hold, push),) = chebyshev_constants(SMOOTH_RATIO, 2)
    beta = push * first
    gamma = first * (1.0 + hold) + push
    omega = 4.0 / 3.0
    source_1 = basis[0] - scaled(
        over_0,
        (gamma + omega) * basis[1]
        - scaled(over_0, (beta + omega * gamma) * basis[2] - scaled(over_0, (omega * beta) * basis[3])),
    )

    spread_1, weight_1 = spread_1w[...], weight_1w[...]
    spread_2, weight_2 = spread_2w[...], weight_2w[...]
    inverse_1 = scaled(inverse_bounds[1], inverse_1w[...])
    inverse_2 = scaled(inverse_bounds[2], inverse_2w[...])
    double_1, double_2 = 2.0 * spread_1, 4.0 * spread_2

    def operate_1(values):
        return double_1 * banded_planes(mid, spread_1 * values, planes, 1) + weight_1 * values

    def operate_2(values):
        return double_2 * banded_planes(coarse, spread_2 * values, planes // 2, 2) + weight_2 * values

    iterate, residue = chebyshev(source_1, 2, inverse_1, SMOOTH_RATIO, operate_1, True)
    smoothed = residue - omega * operate_1(inverse_1 * residue)
    source_2 = paired_lanes(rows_apply(gather_rows[...], smoothed))
    error_2, _ = chebyshev(source_2, COARSE_ITERS, inverse_2, COARSE_RATIO, operate_2, False)
    lifted = dot(spread_rows[...], jnp.concatenate(split(error_2), axis=0))
    iterate = iterate + lifted - omega * (inverse_1 * operate_1(lifted))
    residue = source_1 - operate_1(iterate)
    more, _ = chebyshev(residue, 2, inverse_1, SMOOTH_RATIO, operate_1, False)
    error_1 = iterate + more

    lifted_w[0:2] = jnp.zeros((2, slab, 128), F32)
    lifted_w[planes + 2 : planes + 4] = jnp.zeros((2, slab, 128), F32)
    lifted_w[2 : planes + 2] = error_1.reshape(planes, slab, 128)
    near = lifted_w[pl.ds(2 * gz, 6)].reshape(6 * slab, 128)
    wide = lanes_apply(near, stretch[...])
    for half in (0, 1):
        for odd in (0, 1):
            doubled_w[half, pl.ds(odd, 6 * slab, stride=2)] = wide[:, half * 128 : half * 128 + 128]
    slabs = jnp.concatenate([doubled_w[0], doubled_w[1]], axis=1).reshape(6, 3, 2 * rows, LANES)
    error = jnp.stack([slabs[(plane + 1) // 2] for plane in range(10)], axis=0)

    def near_own(ref, reach):
        return ref[pl.ds(4 * gz + PAD - reach, 4 + 2 * reach)]

    scale, mass = near_own(scale_w, 3), near_own(mass_w, 2)
    inverse = scaled(over_0, near_own(inverse_w, 2))
    source = near_own(source_w, 2)
    before = gamma * source - scaled(over_0, beta * near_own(power_1, 2))

    def apply(values, edge):
        outs = []
        fine_operator(
            fine,
            lambda i: scale[i + 4 - edge],
            lambda i: mass[i + 3 - edge],
            lambda i: scale[i + 4 - edge][None] * values[i + 1],
            lambda i: values[i + 1],
            2 + 2 * edge,
            2 * rows,
            lambda at, result: outs.append(result),
        )
        return jnp.stack(outs, axis=0)

    image = apply(error, 3)
    iterate = inverse * (before - omega * image) + error[1:9]
    residue = source[1:7] - apply(iterate, 2)
    direction = first * (inverse[1:7] * residue)

    def own(values):
        return own_rows(values, 2 * rows // 8)

    for plane in range(4):
        near = [split((scale[plane + 2 + i][None] * direction[plane + i]).reshape(6 * rows, LANES)) for i in range(3)]
        stacked = jnp.concatenate([part[0] for part in near] * 2 + [part[1] for part in near], axis=0)
        product = dot(fine_own[:, : 18 * slab], stacked)
        total = shifted_sum(product, 1, 24, LANES).reshape(3, 8, LANES)[..., :128]
        here = own(direction[plane + 1])[..., :128]
        image = own(scale[plane + 3])[None, :, :128] * total + own(mass[plane + 2])[None, :, :128] * here
        last = own(residue[plane + 1])[..., :128] - image
        answer = own(iterate[plane + 2])[..., :128] + (1.0 + hold) * here
        result[:, plane] = answer + push * (own(inverse[plane + 2])[..., :128] * last)


def swap_pairs(counts, target):
    def number(place):
        return (place[0] * counts[1] + place[1]) * counts[2] + place[2]

    places = [(x, y, z) for x in range(counts[0]) for y in range(counts[1]) for z in range(counts[2])]
    return [(number(place), number(target(*place))) for place in places]


def odd_partner(index):
    return index - 1 if index % 2 == 0 else index + 1


def on_device(right_side, stiff_scale, nodal_mass, stencil_blocks):
    counts = tuple(lax.axis_size(axis) for axis in AXES)
    gxs, gys, gzs = counts
    blocks = stencil_blocks.reshape(243)

    def send(values, target):
        return lax.ppermute(values, AXES, swap_pairs(counts, target))

    def x_second(x, y, z):
        return (x, y, z ^ 1) if x in (0, gxs - 1) else (odd_partner(x), y, z)

    rows, planes = 8 * gys, 4 * gzs
    grant = 20 if planes * rows <= 256 else 48
    slab = 3 * rows
    group = group_of(slab)
    size_1 = planes * slab // 4
    size = coarse_slab(rows // 4)
    size_2 = planes // 4 * size
    (
        fine, fine_own, fine_bound, mid, mid_bound, coarse, coarse_bound, coarse_diag, gather_rows, spread_rows, squeeze,
        squeeze_line, stretch,
    ) = call(
        functools.partial(matrices_kernel, rows, planes),
        [
            ((3 * slab, up128(9 * slab)), BF16),
            ((72, up128(9 * slab)), BF16),
            ((group * 3 * slab, up128(3 * (group + 2) * rows)), BF16),
            ((3 * slab // 2, up128(9 * slab // 2)), BF16),
            ((3 * slab // 2, up128(9 * slab // 2)), BF16),
            ((3 * size, up128(9 * size)), BF16),
            ((3 * size, up128(9 * size)), BF16),
            ((size_2, 128), F32),
            ((size_2, size_1), BF16),
            ((size_1, 2 * size_2), BF16),
            ((2 * LANES, 128), BF16),
            ((2 * LINE, 256), BF16),
            ((256, LANES), BF16),
        ],
        specs=[SM],
        flops=5000000000,
        size=8000000,
        grant=grant,
    )(blocks)

    half = ((14, 8, 128), F32)
    main = jnp.concatenate([right_side.reshape(12, 8, 128), stiff_scale, nodal_mass], axis=0)
    send_a, send_b = call(pack_kernel, [half, half], grant=8)(main)
    got_b = send(send_b, x_second)
    got_a = send(send_a, lambda x, y, z: (x ^ 1, y, z))
    (wide,) = call(functools.partial(widen_kernel, gxs), [((42, 8, 128), F32)], grant=8)(main, got_b, got_a)
    ordered = not (gys == 2 and gzs == 4)
    if ordered:
        gathered = [lax.all_gather(wide, ("gz", "gy"), tiled=False)]
    else:
        near = [
            wide,
            send(wide, lambda x, y, z: (x, y, z ^ 2)),
            send(wide, lambda x, y, z: (x, y ^ 1, z)),
            send(wide, lambda x, y, z: (x, y ^ 1, z ^ 2)),
        ]
        near[3], fine = lax.optimization_barrier((near[3], fine))
        gathered = [block[None] for block in near + [send(block, lambda x, y, z: (x, y, z ^ 1)) for block in near]]

    field = ((planes + 2 * PAD, 3, rows, LANES), F32)
    single = ((planes + 2 * PAD, rows, LANES), F32)
    source_w, scale_w, mass_w, inverse_w, *levels, bounds = call(
        functools.partial(window_kernel, gxs, gys, ordered),
        [field, single, single, field] + [((size_1, 128), F32)] * 3 + [((size_2, 128), F32)] * 3 + [((3, 8, 128), F32)],
        specs=[SM] + [VM] * (len(gathered) + 6),
        scratch=[
            pltpu.VMEM((planes + 2, rows, LINE), F32),
            pltpu.VMEM((planes, rows, LINE), F32),
            pltpu.VMEM((2, LINE // 128, planes * rows // 2, 128), F32),
        ],
        grant=grant,
    )(blocks, *gathered, fine_bound, mid_bound, coarse_bound, coarse_diag, gather_rows, squeeze_line)

    step, other = 2, bounds
    while step < gxs:
        bounds = jnp.maximum(bounds, other)
        other = send(bounds, lambda x, y, z: (x ^ step, y, z ^ 1))
        step *= 2
    power_1, basis = call(
        powers_kernel,
        [field, ((4, size_1, 128), F32)],
        scratch=[pltpu.VMEM(*field), pltpu.VMEM((4, 2, 2 * size_1, 128), F32)],
        flops=3000000000,
        size=12000000,
        grant=grant,
    )(scale_w, mass_w, inverse_w, source_w, fine, squeeze)
    (result,) = call(
        final_kernel,
        [(right_side.shape, F32)],
        scratch=[
            pltpu.VMEM((planes // 2 + 4, slab // 2, 128), F32),
            pltpu.VMEM((2, 6 * slab, 128), F32),
        ],
        grant=grant,
    )(
        bounds, other, source_w, scale_w, mass_w, inverse_w, power_1, basis, *levels,
        fine, fine_own, mid, coarse, gather_rows, spread_rows, stretch,
    )
    return result


def solution(mesh):
    placed = (P(None, "gz", "gy", "gx"), P("gz", "gy", "gx"), P("gz", "gy", "gx"), P())
    return jax.shard_map(
        on_device, mesh=mesh, in_specs=placed, out_specs=P(None, "gz", "gy", "gx"), check_vma=False
    )
```

```python
import functools

import jax
import jax.numpy as jnp
from jax import lax
from jax.experimental import pallas as pl
from jax.experimental.pallas import tpu as pltpu
from jax.sharding import PartitionSpec as P

AXES = ("gx", "gy", "gz")
COARSE_ITERS = 8
SMOOTH_RATIO = 20.0
COARSE_RATIO = 200.0
F32, BF16 = jnp.float32, jnp.bfloat16
VM = pl.BlockSpec(memory_space=pltpu.VMEM)
SM = pl.BlockSpec(memory_space=pltpu.SMEM)
LANES = 256
LINE = 384
FREE, PIECES = 52, (0, 25, 79, 104)
PAD = 3


def call(kernel, outs, specs=None, scratch=(), flops=1000000, size=100000, grant=None):
    params = pltpu.CompilerParams(vmem_limit_bytes=grant * 1024 * 1024) if grant else None
    outs = [jax.ShapeDtypeStruct(shape, dtype) for shape, dtype in outs]

    def run(*args):
        return pl.pallas_call(
            kernel,
            out_shape=outs,
            in_specs=specs or [VM] * len(args),
            out_specs=[VM] * len(outs),
            scratch_shapes=scratch,
            compiler_params=params,
            cost_estimate=pl.CostEstimate(flops=flops, bytes_accessed=size, transcendentals=0),
        )(*args)

    return run


def iota(shape, dim):
    return lax.broadcasted_iota(jnp.int32, shape, dim)


def ones_where(mask):
    return jnp.where(mask, 1.0, 0.0).astype(BF16)


def split(values):
    high = values.astype(BF16)
    return high, (values - high.astype(F32)).astype(BF16)


def dot(left, right):
    return jnp.dot(left, right, preferred_element_type=F32)


def lanes_apply(values, stacked):
    return dot(jnp.concatenate(split(values), axis=1), stacked)


def rows_apply(selection, values):
    width = values.shape[1]
    product = dot(selection, jnp.concatenate(split(values), axis=1))
    return product[:, :width] + product[:, width:]


def banded_stacked(matrix, values):
    high, low = split(values)
    return dot(matrix, jnp.concatenate([high, high, low], axis=0))


def banded_planes(matrix, values, planes, step):
    slab, lanes = values.shape[0] // planes, values.shape[1]
    edge = jnp.zeros((slab, lanes), F32)
    padded = jnp.concatenate([edge, values, edge], axis=0)
    beside = jnp.concatenate([padded[at * slab : (at + 3) * slab] for at in range(planes)], axis=1)
    if slab % 16 == 0:
        high, low = split(beside)
        stacked = jnp.concatenate([high, high, low], axis=0)
    else:
        high = beside.astype(BF16).astype(F32)
        stacked = jnp.concatenate([high, high, beside - high], axis=0).astype(BF16)
    product = dot(matrix[:, : 9 * slab], stacked)
    outs = []
    for at in range(planes):
        below, here, above = (
            product[part * slab : part * slab + slab, at * lanes : at * lanes + lanes] for part in range(3)
        )
        outs.append(here + pltpu.roll(below, step, 1) + pltpu.roll(above, lanes - step, 1))
    return jnp.concatenate(outs, axis=0)


def paired_lanes(values):
    even = iota(values.shape, 1) % 2 == 0
    return values + jnp.where(even, pltpu.roll(values, values.shape[1] - 1, 1), pltpu.roll(values, 1, 1))


def shifted_sum(product, slabs, rows, lanes):
    parts = product.reshape(slabs, 3, rows, lanes)
    below = parts[:, 0].reshape(slabs * rows, lanes)
    above = parts[:, 2].reshape(slabs * rows, lanes)
    here = parts[:, 1].reshape(slabs * rows, lanes)
    return here + pltpu.roll(below, 1, 1) + pltpu.roll(above, lanes - 1, 1)


def group_of(slab):
    return max(1, 256 // slab - 2)


def groups(planes, most):
    sizes = []
    half = planes // 2
    while half:
        size = min(most, half)
        sizes += [size, size]
        half -= size
    return sizes


def fine_operator(matrix, scale_of, mass_of, weighted_of, value_of, planes, rows, finish):
    slab = 3 * rows
    parts = {}
    for plane in range(planes):
        near = range(plane - 1, plane + 2)
        for i in near:
            if i not in parts:
                parts[i] = split(weighted_of(i).reshape(slab, LANES))
        high = [parts[i][0] for i in near]
        low = [parts[i][1] for i in near]
        product = dot(matrix[:, : 9 * slab], jnp.concatenate(high + high + low, axis=0))
        total = shifted_sum(product, 1, slab, LANES).reshape(3, rows, LANES)
        finish(plane, scale_of(plane)[None] * total + mass_of(plane)[None] * value_of(plane))


def panels(value_of, others, rows, width):
    column = iota((8, width), 1)
    which = column // rows
    row_in = column % rows
    result = {}
    for step_x in range(3):
        for comp in range(3):
            coeffs = []
            for step_y in range(3):
                coeff = jnp.zeros((8, width), F32)
                for plane in range(3):
                    for other in range(others):
                        value = value_of(plane * 9 + step_y * 3 + step_x, comp, other)
                        coeff = jnp.where(which == plane * others + other, value, coeff)
                coeffs.append(coeff)
            pieces = []
            for block in range(rows // 8):
                gap = row_in - (iota((8, width), 0) + block * 8)
                piece = jnp.zeros((8, width), F32)
                for step_y in range(3):
                    piece = jnp.where(gap == step_y - 1, coeffs[step_y], piece)
                pieces.append(piece)
            result[step_x, comp] = jnp.concatenate(pieces, axis=0)
    return result


def turned(value, turn):
    turn %= value.shape[1]
    return pltpu.roll(value, turn, 1) if turn else value


def parts_of(value):
    high = value.astype(BF16).astype(F32)
    return high, value - high


def stack3(value, size):
    high, low = parts_of(value)
    return (high + turned(low, size) + turned(high, 2 * size)).astype(BF16)


def up128(size):
    return -(-size // 128) * 128


def coarse_slab(few):
    return -(-3 * few // 16) * 16


def own_rows(values, count):
    index = lax.axis_index("gy")
    found = values[..., :8, :]
    for block in range(1, count):
        found = jnp.where(index == block, values[..., block * 8 : block * 8 + 8, :], found)
    return found


def matrices_kernel(
    rows, planes, blocks, fine, fine_own, fine_bound, mid, mid_bound, coarse, coarse_bound, coarse_diag,
    gather_rows, spread_rows, squeeze, squeeze_line, stretch,
):
    def direct(offset, comp, other):
        return blocks[offset * 9 + comp * 3 + other]

    def absolute(offset, comp, other):
        at = offset * 9 + comp * 3
        return jnp.abs(blocks[at]) + jnp.abs(blocks[at + 1]) + jnp.abs(blocks[at + 2])

    slab = 3 * rows
    group = group_of(slab)
    width = up128(3 * slab)
    found = panels(direct, 3, rows, width)
    every = [found[step_x, comp] for step_x in range(3) for comp in range(3)]
    for target, parts in ((fine, every), (fine_own, [own_rows(part, rows // 8) for part in every])):
        value = jnp.concatenate(parts, axis=0)
        if target.shape[1] > width:
            value = jnp.concatenate([value, jnp.zeros((value.shape[0], target.shape[1] - width), F32)], axis=1)
        target[...] = stack3(value, 3 * slab)
    bound = panels(absolute, 1, rows, fine_bound.shape[1])
    for plane in range(group):
        for step_x in range(3):
            start = (plane * 3 + step_x) * slab
            value = turned(jnp.concatenate([bound[step_x, comp] for comp in range(3)], axis=0), plane * rows)
            fine_bound[start : start + slab, :] = stack3(value, (group + 2) * rows)

    rows, planes = rows // 2, planes // 2
    slab = 3 * rows
    found = panels(direct, 3, rows, mid.shape[1])
    whole = jnp.concatenate([found[step_x, comp] for step_x in range(3) for comp in range(3)], axis=0)
    few, half = rows // 2, planes // 2
    size = coarse_slab(few)

    def choose(out, source):
        place = out % size
        wanted = out // size * slab + place // few * rows + place % few
        return ones_where(jnp.logical_and(source == wanted, place < 3 * few))

    shape = (3 * size, 3 * slab)
    choose_rows = choose(iota(shape, 0), iota(shape, 1))
    shape = (mid.shape[1], up128(3 * size))
    choose_columns = jnp.where(iota(shape, 1) < 3 * size, choose(iota(shape, 1), iota(shape, 0)), 0.0).astype(BF16)

    def smaller(matrix):
        return dot(dot(choose_rows, matrix.astype(BF16)).astype(BF16), choose_columns)

    for target, small_target, value in ((mid, coarse, whole), (mid_bound, coarse_bound, jnp.abs(whole))):
        target[...] = stack3(value, 3 * slab)
        high, low = parts_of(value)
        high, low = smaller(high), smaller(low)
        width = small_target.shape[1]
        if width > high.shape[1]:
            more = jnp.zeros((3 * size, width - high.shape[1]), F32)
            high, low = jnp.concatenate([high, more], axis=1), jnp.concatenate([low, more], axis=1)
        small_target[...] = (high + turned(low, 3 * size) + turned(high, 6 * size)).astype(BF16)
    comp = iota((half * size, 128), 0) % size // few
    diag = [blocks[13 * 9 + 4 * at] for at in range(3)]
    coarse_diag[...] = jnp.where(comp == 0, diag[0], jnp.where(comp == 1, diag[1], diag[2]))

    def same_aggregate(small, large):
        place, inner = small % size, large % slab
        same = jnp.logical_and(small // size == large // (2 * slab), place // few == inner // rows)
        return jnp.logical_and(same, place % few == inner % rows // 2)

    shape = (half * size, planes * slab)
    gather_rows[...] = ones_where(same_aggregate(iota(shape, 0), iota(shape, 1)))
    shape = (planes * slab, 2 * half * size)
    spread_rows[...] = ones_where(same_aggregate(iota(shape, 1) % (half * size), iota(shape, 0)))
    shape = (2 * LANES, 128)
    squeeze[...] = ones_where(iota(shape, 0) % LANES // 2 == iota(shape, 1))
    shape = (2 * LINE, 256)
    lane = iota(shape, 0) % LINE
    squeeze_line[...] = ones_where(jnp.where(lane < 256, lane // 2, lane // 2 + 64) == iota(shape, 1))
    shape = (256, LANES)
    stretch[...] = ones_where(iota(shape, 0) % 128 == iota(shape, 1) // 2)


def halves(planes):
    count = planes.shape[0] // 2
    low = iota((count, 8, 128), 2) < 64
    first, second = planes[:count], pltpu.roll(planes[count:], 64, 2)
    return jnp.where(low, second, first), jnp.where(low, first, second)


def pack_kernel(main, send_a, send_b):
    high, low = halves(main[...])
    more_high, more_low = halves(main[12:])
    even = lax.rem(lax.axis_index("gx"), 2) == 0
    send_a[:10] = jnp.where(even, high, low)
    send_a[10:] = jnp.where(even, more_low, more_high)
    send_b[:10] = jnp.where(even, low, high)
    send_b[10:] = jnp.zeros((4, 8, 128), F32)


def widen_kernel(count, main, got_b, got_a, wide):
    index = lax.axis_index("gx")
    even = lax.rem(index, 2) == 0
    first, second, more = got_a[:10], got_b[:10], got_a[10:]
    above = jnp.where(index < count - 1, jnp.where(even, first, second), 0.0)
    below = jnp.where(index > 0, jnp.where(even, second, first), 0.0)
    low = iota((10, 8, 128), 2) < 64
    wide[:20] = main[...]
    halo = jnp.concatenate(
        [jnp.where(low, above, below), jnp.where(low, pltpu.roll(above, 64, 2), pltpu.roll(below, 64, 2))], axis=0
    )
    lane = iota((8, 128), 1)
    free = jnp.logical_and(lane >= FREE, lane < FREE + 25)
    for guest in range(2):
        for piece, start in enumerate(PIECES):
            moved = pltpu.roll(halo[8 + guest], (FREE - start) % 128, 1)
            wide[20 + guest * 4 + piece] = jnp.where(free, moved, halo[guest * 4 + piece])
    wide[28:38] = halo[10:]
    wide[38:] = jnp.where(even, pltpu.roll(more, 64, 2), more)


def inverse_diagonal(scale, mass, blocks, factor):
    square = scale * scale
    parts = []
    for comp in range(3):
        diag = factor * blocks[13 * 9 + comp * 4] * square + mass
        parts.append(jnp.where(scale > 0.0, 1.0 / diag, 0.0)[:, None])
    return jnp.concatenate(parts, axis=1)


def line_lanes(shape, count, above, more_above, more_below, below, seam):
    index = lax.axis_index("gx")
    even = lax.rem(index, 2) == 0
    odd = jnp.logical_not(even)
    lane = iota(shape, 1)
    end_above = more_above + (more_above - above) - jnp.where(index + 1 == count - 1, 0, seam)
    start_below = more_below + jnp.where(index - 1 == 0, 0, seam)

    def within(first, last, condition):
        return jnp.logical_and(jnp.logical_and(lane >= first, lane < last), condition)

    found = lane < above
    for part in (
        within(above, more_above - jnp.where(even, 0, seam), index < count - 1),
        within(more_above, end_above, even),
        within(start_below, below, odd),
        within(below + jnp.where(even, seam, 0), shape[1], index > 0),
    ):
        found = jnp.logical_or(found, part)
    return found


def largest(ratio, *lanes):
    width = ratio.shape[1]
    flat = jnp.max(ratio.reshape(-1, 8, width), axis=0)
    flat = jnp.where(line_lanes(flat.shape, *lanes), flat, -jnp.inf)
    return functools.reduce(jnp.maximum, [flat[:, at : at + 128] for at in range(0, width, 128)])


def clear_pads(ref):
    planes = ref.shape[0] - 2 * PAD
    for at in (0, planes + PAD):
        ref[at : at + PAD] = jnp.zeros((PAD,) + ref.shape[1:], F32)


def paired_planes(values):
    pairs = values.reshape((-1, 2) + values.shape[1:])
    return pairs[:, 0] + pairs[:, 1]


def paired_rows(held, values):
    parts, count = held.shape[0], held.shape[1] // 2
    for part in range(parts):
        held[part] = values[:, part * 128 : part * 128 + 128]
    return jnp.concatenate(
        [held[part, pl.ds(0, count, stride=2)] + held[part, pl.ds(1, count, stride=2)] for part in range(parts)], axis=1
    )


def window_kernel(
    gxs, gys, ordered, blocks, *refs
):
    (*blocks_in, fine_bound, mid_bound, coarse_bound, coarse_diag, gather_rows, squeeze_line, source_w, scale_w, mass_w, inverse_w,
     spread_1w, weight_1w, inverse_1w, spread_2w, weight_2w, inverse_2w, bounds, scale_x, mass_x, held) = refs
    planes, rows = scale_w.shape[0] - 2 * PAD, scale_w.shape[1]
    gz, gy = lax.axis_index("gz"), lax.axis_index("gy")
    even = lax.rem(lax.axis_index("gx"), 2) == 0
    low = iota((4, 8, 128), 2) < 64
    lane = iota((8, 128), 1)
    for at in (0, planes + 1):
        scale_x[at] = jnp.zeros((rows, LINE), F32)
    for ref in (source_w, inverse_w, scale_w, mass_w):
        clear_pads(ref)
    number = 0
    for ref in blocks_in:
        for block in range(ref.shape[0]):
            if ordered:
                place_z, place_y = number // gys, number % gys
            else:
                place_z = lax.bitwise_xor(gz, number // 4 + 2 * (number % 2))
                place_y = lax.bitwise_xor(gy, number % 4 // 2)
            at_z = pl.ds(PAD + 4 * place_z, 4)
            at_y = pl.ds(pl.multiple_of(8 * place_y, 8), 8)
            here, more = ref.at[block], ref[block, 38:42]
            for comp in range(3):
                source_w[at_z, comp, at_y, :128] = here[comp * 4 : comp * 4 + 4]
            for comp in range(2):
                source_w[at_z, comp, at_y, 128:] = here[20 + comp * 4 : 24 + comp * 4]
            source_w[pl.ds(PAD + 4 * place_z + 2, 2), 2, at_y, 128:] = here[28:30]
            for guest in range(2):
                found = here[20 + guest * 4]
                for piece, start in enumerate(PIECES):
                    back = pltpu.roll(here[20 + guest * 4 + piece], (start - FREE) % 128, 1)
                    found = jnp.where(lane >= (0, 25, 64, 104)[piece], back, found)
                source_w[PAD + 4 * place_z + guest, 2, at_y, 128:] = found
            scale_w[at_z, at_y, :128], scale_w[at_z, at_y, 128:] = here[12:16], here[30:34]
            mass_w[at_z, at_y, :128], mass_w[at_z, at_y, 128:] = here[16:20], here[34:38]
            turned_more = pltpu.roll(more, 64, 2)
            for target, own, start, at_low, at_high in (
                (scale_x, 12, 1, more, turned_more),
                (mass_x, 16, 0, turned_more, more),
            ):
                at_x = pl.ds(start + 4 * place_z, 4)
                halo = here[own + 18 : own + 22]
                target[at_x, at_y, :128] = here[own : own + 4]
                target[at_x, at_y, 128:256] = jnp.where(low, halo, jnp.where(even, at_high, 0.0))
                target[at_x, at_y, 256:] = jnp.where(low, jnp.where(even, 0.0, at_low), halo)
            number += 1

    scale, mass = scale_x[1 : 1 + planes], mass_x[...]
    inverse = inverse_diagonal(scale, mass, blocks, 1.0)
    inverse_w[PAD : PAD + planes, :, :, :128] = inverse[..., :128]
    wide_low = iota(inverse.shape[:3] + (128,), 3) < 64
    inverse_w[PAD : PAD + planes, :, :, 128:] = jnp.where(wide_low, inverse[..., 128:256], inverse[..., 256:])
    slab = 3 * rows
    outs = []
    at = 0
    for size in groups(planes, group_of(slab))[::2]:
        beside = []
        for _ in range(2):
            near = scale_x[at : at + size + 2].reshape((size + 2) * rows, LINE)
            if size < group_of(slab):
                near = jnp.concatenate([near, jnp.zeros(((group_of(slab) - size) * rows, LINE), F32)], axis=0)
            beside.append(near)
            at += size
        depth = 3 * (group_of(slab) + 2) * rows
        product = banded_stacked(fine_bound[: size * 3 * slab, :depth], jnp.concatenate(beside, axis=1))
        outs += [shifted_sum(product[:, half * LINE : half * LINE + LINE], size, slab, LINE) for half in (0, 1)]
    total = jnp.concatenate(outs, axis=0).reshape(planes, 3, rows, LINE)
    ratio = (scale[:, None] * total + mass[:, None]) * inverse
    bounds[0] = largest(ratio.reshape(planes * slab, LINE), gxs, 128, 192, 256, 320, 1)

    rows, planes = rows // 2, planes // 2
    slab = 3 * rows
    count = planes * rows
    pairs = [
        paired_rows(held.at[at], paired_planes(values).reshape(2 * count, LINE))
        for at, values in enumerate((scale, mass))
    ]
    middle = lanes_apply(jnp.concatenate(pairs, axis=0), squeeze_line[...])
    scale_1 = (middle[:count] * 0.125).reshape(planes, rows, 256)
    mass_1 = middle[count:].reshape(planes, rows, 256)
    inverse_1 = inverse_diagonal(scale_1, mass_1, blocks, 2.0).reshape(planes * slab, 256)
    spread_1 = jnp.broadcast_to(scale_1[:, None], (planes, 3, rows, 256)).reshape(planes * slab, 256)
    weight_1 = jnp.broadcast_to(mass_1[:, None], (planes, 3, rows, 256)).reshape(planes * slab, 256)
    total = banded_planes(mid_bound, spread_1, planes, 1)
    bounds[1] = largest((2.0 * spread_1 * total + weight_1) * inverse_1, gxs, 64, 96, 192, 224, 1)

    def window(values):
        return jnp.where(iota((values.shape[0], 128), 1) < 96, values[:, :128], values[:, 128:])

    spread_1w[...], weight_1w[...], inverse_1w[...] = window(spread_1), window(weight_1), window(inverse_1)

    both = rows_apply(gather_rows[...], jnp.concatenate([spread_1, weight_1], axis=1))
    spread_2 = paired_lanes(both[:, :256]) * 0.125
    weight_2 = paired_lanes(both[:, 256:])
    diag = jnp.concatenate([coarse_diag[...]] * 2, axis=1)
    inverse_2 = jnp.where(spread_2 > 0.0, 1.0 / (4.0 * diag * spread_2 * spread_2 + weight_2), 0.0)
    total = banded_planes(coarse_bound, spread_2, planes // 2, 2)
    bounds[2] = largest((4.0 * spread_2 * total + weight_2) * inverse_2, gxs, 64, 96, 192, 224, 2)
    spread_2w[...], weight_2w[...], inverse_2w[...] = window(spread_2), window(weight_2), window(inverse_2)


def inner_power(scale_w, mass_w, inverse_w, matrix, values, finish):
    planes, rows = scale_w.shape[0] - 2 * PAD, scale_w.shape[1]
    fine_operator(
        matrix,
        lambda i: scale_w[PAD + i],
        lambda i: mass_w[PAD + i],
        lambda i: scale_w[PAD + i][None] * (inverse_w[PAD + i] * values[PAD + i]),
        lambda i: inverse_w[PAD + i] * values[PAD + i],
        planes,
        rows,
        finish,
    )


def powers_kernel(scale_w, mass_w, inverse_w, source_w, fine, squeeze, power_1, basis, power_2, held):
    planes, rows = scale_w.shape[0] - 2 * PAD, scale_w.shape[1]
    third = []
    for source, target in ((source_w, power_1), (power_1, power_2)):
        clear_pads(target)

        def finish(at, values, target=target):
            target[PAD + at] = values

        inner_power(scale_w, mass_w, inverse_w, fine, source, finish)
    inner_power(scale_w, mass_w, inverse_w, fine, power_2, lambda at, values: third.append(values))
    inner = slice(PAD, PAD + planes)
    size = planes // 2 * 3 * rows
    pairs = []
    for at, values in enumerate((source_w[inner], power_1[inner], power_2[inner], jnp.stack(third, axis=0))):
        pairs.append(paired_rows(held.at[at], paired_planes(values).reshape(size, LANES)))
    restricted = lanes_apply(jnp.concatenate(pairs, axis=0), squeeze[...])
    for at in range(4):
        basis[at] = restricted[at * size // 2 : (at + 1) * size // 2]


def chebyshev_constants(ratio, degree):
    sigma = (ratio + 1.0) / (ratio - 1.0)
    rho = 1.0 / sigma
    steps = []
    for _ in range(degree - 1):
        rho_next = 1.0 / (2.0 * sigma - rho)
        steps.append((rho_next * rho, 4.0 * rho_next / (1.0 - 1.0 / ratio)))
        rho = rho_next
    return 2.0 / (1.0 + 1.0 / ratio), steps


def chebyshev(residue, degree, inverse, ratio, operate, keep):
    first, steps = chebyshev_constants(ratio, degree)
    direction = first * (inverse * residue)
    total = direction
    for hold, push in steps:
        residue = residue - operate(direction)
        direction = hold * direction + push * (inverse * residue)
        total = total + direction
    if keep:
        residue = residue - operate(direction)
    return total, residue


def scaled(coeff, values):
    lanes = values.shape[-1]
    if lanes != 128:
        coeff = jnp.concatenate([coeff] * (lanes // 128), axis=1)
    flat = values.reshape(-1, 8, lanes)
    return (coeff[None] * flat).reshape(values.shape)


def final_kernel(
    bounds_a, bounds_b, source_w, scale_w, mass_w, inverse_w, power_1, basis,
    spread_1w, weight_1w, inverse_1w, spread_2w, weight_2w, inverse_2w,
    fine, fine_own, mid, coarse, gather_rows, spread_rows, stretch, result, lifted_w, doubled_w,
):
    rows = scale_w.shape[1] // 2
    planes = (scale_w.shape[0] - 2 * PAD) // 2
    slab = 3 * rows
    gz = lax.axis_index("gz")
    worst = jnp.maximum(bounds_a[...], bounds_b[...])
    inverse_bounds = [1.0 / jnp.full((8, 128), jnp.max(worst[level]), F32) for level in range(3)]
    over_0 = inverse_bounds[0]

    first, ((hold, push),) = chebyshev_constants(SMOOTH_RATIO, 2)
    beta = push * first
    gamma = first * (1.0 + hold) + push
    omega = 4.0 / 3.0
    source_1 = basis[0] - scaled(
        over_0,
        (gamma + omega) * basis[1]
        - scaled(over_0, (beta + omega * gamma) * basis[2] - scaled(over_0, (omega * beta) * basis[3])),
    )

    spread_1, weight_1 = spread_1w[...], weight_1w[...]
    spread_2, weight_2 = spread_2w[...], weight_2w[...]
    inverse_1 = scaled(inverse_bounds[1], inverse_1w[...])
    inverse_2 = scaled(inverse_bounds[2], inverse_2w[...])
    double_1, double_2 = 2.0 * spread_1, 4.0 * spread_2

    def operate_1(values):
        return double_1 * banded_planes(mid, spread_1 * values, planes, 1) + weight_1 * values

    def operate_2(values):
        return double_2 * banded_planes(coarse, spread_2 * values, planes // 2, 2) + weight_2 * values

    iterate, residue = chebyshev(source_1, 2, inverse_1, SMOOTH_RATIO, operate_1, True)
    smoothed = residue - omega * operate_1(inverse_1 * residue)
    source_2 = paired_lanes(rows_apply(gather_rows[...], smoothed))
    error_2, _ = chebyshev(source_2, COARSE_ITERS, inverse_2, COARSE_RATIO, operate_2, False)
    lifted = dot(spread_rows[...], jnp.concatenate(split(error_2), axis=0))
    iterate = iterate + lifted - omega * (inverse_1 * operate_1(lifted))
    residue = source_1 - operate_1(iterate)
    more, _ = chebyshev(residue, 2, inverse_1, SMOOTH_RATIO, operate_1, False)
    error_1 = iterate + more

    lifted_w[0:2] = jnp.zeros((2, slab, 128), F32)
    lifted_w[planes + 2 : planes + 4] = jnp.zeros((2, slab, 128), F32)
    lifted_w[2 : planes + 2] = error_1.reshape(planes, slab, 128)
    near = lifted_w[pl.ds(2 * gz, 6)].reshape(6 * slab, 128)
    wide = lanes_apply(near, stretch[...])
    for half in (0, 1):
        for odd in (0, 1):
            doubled_w[half, pl.ds(odd, 6 * slab, stride=2)] = wide[:, half * 128 : half * 128 + 128]
    slabs = jnp.concatenate([doubled_w[0], doubled_w[1]], axis=1).reshape(6, 3, 2 * rows, LANES)
    error = jnp.stack([slabs[(plane + 1) // 2] for plane in range(10)], axis=0)

    def near_own(ref, reach):
        return ref[pl.ds(4 * gz + PAD - reach, 4 + 2 * reach)]

    scale, mass = near_own(scale_w, 3), near_own(mass_w, 2)
    inverse = scaled(over_0, near_own(inverse_w, 2))
    source = near_own(source_w, 2)
    before = gamma * source - scaled(over_0, beta * near_own(power_1, 2))

    def apply(values, edge):
        outs = []
        fine_operator(
            fine,
            lambda i: scale[i + 4 - edge],
            lambda i: mass[i + 3 - edge],
            lambda i: scale[i + 4 - edge][None] * values[i + 1],
            lambda i: values[i + 1],
            2 + 2 * edge,
            2 * rows,
            lambda at, result: outs.append(result),
        )
        return jnp.stack(outs, axis=0)

    image = apply(error, 3)
    iterate = inverse * (before - omega * image) + error[1:9]
    residue = source[1:7] - apply(iterate, 2)
    direction = first * (inverse[1:7] * residue)

    def own(values):
        return own_rows(values, 2 * rows // 8)

    for plane in range(4):
        near = [split((scale[plane + 2 + i][None] * direction[plane + i]).reshape(6 * rows, LANES)) for i in range(3)]
        stacked = jnp.concatenate([part[0] for part in near] * 2 + [part[1] for part in near], axis=0)
        product = dot(fine_own[:, : 18 * slab], stacked)
        total = shifted_sum(product, 1, 24, LANES).reshape(3, 8, LANES)[..., :128]
        here = own(direction[plane + 1])[..., :128]
        image = own(scale[plane + 3])[None, :, :128] * total + own(mass[plane + 2])[None, :, :128] * here
        last = own(residue[plane + 1])[..., :128] - image
        answer = own(iterate[plane + 2])[..., :128] + (1.0 + hold) * here
        result[:, plane] = answer + push * (own(inverse[plane + 2])[..., :128] * last)


def swap_pairs(counts, target):
    def number(place):
        return (place[0] * counts[1] + place[1]) * counts[2] + place[2]

    places = [(x, y, z) for x in range(counts[0]) for y in range(counts[1]) for z in range(counts[2])]
    return [(number(place), number(target(*place))) for place in places]


def odd_partner(index):
    return index - 1 if index % 2 == 0 else index + 1


def on_device(right_side, stiff_scale, nodal_mass, stencil_blocks):
    counts = tuple(lax.axis_size(axis) for axis in AXES)
    gxs, gys, gzs = counts
    blocks = stencil_blocks.reshape(243)

    def send(values, target):
        return lax.ppermute(values, AXES, swap_pairs(counts, target))

    def x_second(x, y, z):
        return (x, y, z ^ 1) if x in (0, gxs - 1) else (odd_partner(x), y, z)

    rows, planes = 8 * gys, 4 * gzs
    grant = 20 if planes * rows <= 256 else 48
    slab = 3 * rows
    group = group_of(slab)
    size_1 = planes * slab // 4
    size = coarse_slab(rows // 4)
    size_2 = planes // 4 * size
    (
        fine, fine_own, fine_bound, mid, mid_bound, coarse, coarse_bound, coarse_diag, gather_rows, spread_rows, squeeze,
        squeeze_line, stretch,
    ) = call(
        functools.partial(matrices_kernel, rows, planes),
        [
            ((3 * slab, up128(9 * slab)), BF16),
            ((72, up128(9 * slab)), BF16),
            ((group * 3 * slab, up128(3 * (group + 2) * rows)), BF16),
            ((3 * slab // 2, up128(9 * slab // 2)), BF16),
            ((3 * slab // 2, up128(9 * slab // 2)), BF16),
            ((3 * size, up128(9 * size)), BF16),
            ((3 * size, up128(9 * size)), BF16),
            ((size_2, 128), F32),
            ((size_2, size_1), BF16),
            ((size_1, 2 * size_2), BF16),
            ((2 * LANES, 128), BF16),
            ((2 * LINE, 256), BF16),
            ((256, LANES), BF16),
        ],
        specs=[SM],
        flops=5000000000,
        size=8000000,
        grant=grant,
    )(blocks)

    half = ((14, 8, 128), F32)
    main = jnp.concatenate([right_side.reshape(12, 8, 128), stiff_scale, nodal_mass], axis=0)
    send_a, send_b = call(pack_kernel, [half, half], grant=8)(main)
    got_b = send(send_b, x_second)
    got_a = send(send_a, lambda x, y, z: (x ^ 1, y, z))
    (wide,) = call(functools.partial(widen_kernel, gxs), [((42, 8, 128), F32)], grant=8)(main, got_b, got_a)
    ordered = not (gys == 2 and gzs == 4)
    if ordered:
        gathered = [lax.all_gather(wide, ("gz", "gy"), tiled=False)]
    else:
        near = [
            wide,
            send(wide, lambda x, y, z: (x, y, z ^ 2)),
            send(wide, lambda x, y, z: (x, y ^ 1, z)),
            send(wide, lambda x, y, z: (x, y ^ 1, z ^ 2)),
        ]
        near[3], fine = lax.optimization_barrier((near[3], fine))
        gathered = [block[None] for block in near + [send(block, lambda x, y, z: (x, y, z ^ 1)) for block in near]]

    field = ((planes + 2 * PAD, 3, rows, LANES), F32)
    single = ((planes + 2 * PAD, rows, LANES), F32)
    source_w, scale_w, mass_w, inverse_w, *levels, bounds = call(
        functools.partial(window_kernel, gxs, gys, ordered),
        [field, single, single, field] + [((size_1, 128), F32)] * 3 + [((size_2, 128), F32)] * 3 + [((3, 8, 128), F32)],
        specs=[SM] + [VM] * (len(gathered) + 6),
        scratch=[
            pltpu.VMEM((planes + 2, rows, LINE), F32),
            pltpu.VMEM((planes, rows, LINE), F32),
            pltpu.VMEM((2, LINE // 128, planes * rows // 2, 128), F32),
        ],
        grant=grant,
    )(blocks, *gathered, fine_bound, mid_bound, coarse_bound, coarse_diag, gather_rows, squeeze_line)

    step, other = 2, bounds
    while step < gxs:
        bounds = jnp.maximum(bounds, other)
        other = send(bounds, lambda x, y, z: (x ^ step, y, z ^ 1))
        step *= 2
    power_1, basis = call(
        powers_kernel,
        [field, ((4, size_1, 128), F32)],
        scratch=[pltpu.VMEM(*field), pltpu.VMEM((4, 2, 2 * size_1, 128), F32)],
        flops=3000000000,
        size=12000000,
        grant=grant,
    )(scale_w, mass_w, inverse_w, source_w, fine, squeeze)
    (result,) = call(
        final_kernel,
        [(right_side.shape, F32)],
        scratch=[
            pltpu.VMEM((planes // 2 + 4, slab // 2, 128), F32),
            pltpu.VMEM((2, 6 * slab, 128), F32),
        ],
        grant=grant,
    )(
        bounds, other, source_w, scale_w, mass_w, inverse_w, power_1, basis, *levels,
        fine, fine_own, mid, coarse, gather_rows, spread_rows, stretch,
    )
    return result


def solution(mesh):
    placed = (P(None, "gz", "gy", "gx"), P("gz", "gy", "gx"), P("gz", "gy", "gx"), P())
    return jax.shard_map(
        on_device, mesh=mesh, in_specs=placed, out_specs=P(None, "gz", "gy", "gx"), check_vma=False
    )
```
